32 devices in a mesh: pass: 16 (over z, y, x), pb: 2 (over core).
Axes of the slice: x: 2, y: 2, z: 4, core: 2. Of those that a mesh axis runs over, the one named last changes fastest.
Arguments:
- hidden: bfloat16 [2, 16, 128, 768], P('pb', 'pass'), may hold values from -6 to 6
- encodings: bfloat16 [16, 2, 16, 128, 768], P('pass', 'pb'), may hold values from -6 to 6
- lengths: int32 [2, 16, 16], P('pb', 'pass'), may hold values from 32 to 128, as said below
- cotangent: bfloat16 [2, 16, 128, 768], P('pb', 'pass'), may hold values from -6 to 6
- self_query: bfloat16 [768, 768], replicated, may hold values from -0.0546875 to 0.0546875
- self_key: bfloat16 [768, 768], replicated, may hold values from -0.21875 to 0.21875
- self_value: bfloat16 [768, 768], replicated, may hold values from -0.21875 to 0.21875
- self_output: bfloat16 [768, 768], replicated, may hold values from -0.21875 to 0.21875
- cross_query: bfloat16 [768, 768], replicated, may hold values from -0.0546875 to 0.0546875
- cross_key: bfloat16 [768, 768], replicated, may hold values from -0.21875 to 0.21875
- cross_value: bfloat16 [768, 768], replicated, may hold values from -0.21875 to 0.21875
- cross_output: bfloat16 [768, 768], replicated, may hold values from -1.25 to 1.25
- feed_in: bfloat16 [768, 3072], replicated, may hold values from -0.21875 to 0.21875
- feed_out: bfloat16 [3072, 768], replicated, may hold values from -0.109375 to 0.109375
- gain_self: float32 [768], replicated, may hold values from 0.5 to 1.5
- gain_cross: float32 [768], replicated, may hold values from 0.5 to 1.5
- gain_feed: float32 [768], replicated, may hold values from 0.5 to 1.5
- bias_table: float32 [32, 12], replicated, may hold values from -4 to 4
Outputs:
- layer_out: float32 [2, 16, 128, 768], P('pb', 'pass')
- hidden_grad: float32 [2, 16, 128, 768], P('pb', 'pass')
- encodings_grad: bfloat16 [16, 2, 16, 128, 768], P('pass', 'pb')
- self_query_grad: float32 [768, 768], P('pass')
- self_key_grad: float32 [768, 768], P('pass')
- self_value_grad: float32 [768, 768], P('pass')
- self_output_grad: float32 [768, 768], P('pass')
- cross_query_grad: float32 [768, 768], P('pass')
- cross_key_grad: float32 [768, 768], P('pass')
- cross_value_grad: float32 [768, 768], P('pass')
- cross_output_grad: float32 [768, 768], P('pass')
- feed_in_grad: float32 [768, 3072], P('pass')
- feed_out_grad: float32 [3072, 768], P('pass')
- gain_self_grad: float32 [768], P('pass')
- gain_cross_grad: float32 [768], P('pass')
- gain_feed_grad: float32 [768], P('pass')
- bias_table_grad: float32 [32, 12], replicated
The draws below stay inside these ranges and needn't reach their ends.
Inputs may be any that keep to these rules, and one draw needn't show every extreme that they name: `lengths`: every question has a passage of the full 128 slots.
All inputs are finite; a program needn't handle non-finite values.
Results may differ from the reference program's by a relative error of at most 0.023.
The reference program's roundings to bfloat16 on the way count: a program that leaves them out, or rounds other values in their place, can miss the bound.
Values may be sent and summed in bfloat16 or wider, within the bound.
A program may use at most 384 MiB of HBM per device.

```python
import jax
import jax.numpy as jnp
from jax import lax

D = 768
H = 12
HD = 64
FF = 3072
NB = 32
DEC = 128
SLOT = 128
P_SIZE = 16
QG = 16
GROUPS = 2


def draw_lengths(key, part):
    key = jax.random.fold_in(key, 11)
    first, second = jax.random.split(key)
    shortest = max(SLOT // 4, 1)
    drawn = jax.random.randint(first, (GROUPS, QG, P_SIZE), shortest, SLOT + 1)
    picked = jax.random.randint(second, (GROUPS, QG, 1), 0, P_SIZE)
    spots = jnp.arange(P_SIZE, dtype=jnp.int32)[None, None, :]
    return jnp.where(spots == picked, SLOT, drawn).astype(jnp.int32)


def levels(own_key, extent, cuts, least, largest):
    level, own = 1.0, jax.random.fold_in(own_key, 6)
    for position, blocks in cuts:
        draws = jnp.exp(jax.random.uniform(jax.random.fold_in(own, position), (blocks,), jnp.float32, least / len(cuts), largest / len(cuts)))
        level = level * jnp.repeat(draws, extent[position] // blocks).reshape([-1 if axis == position else 1 for axis in range(len(extent))])
    return level


def normal_values(rng, shape, width, limit, cuts=(), held_as=jnp.bfloat16):
    entries = width * jax.random.normal(rng, shape, jnp.float32)
    if cuts:
        entries = entries * levels(rng, shape, cuts, -0.22, 0.18)
    return jnp.clip(entries, -limit, limit).astype(held_as)


def setup_inputs(seed: int = 0) -> dict:
    key_of = jax.random.split(jax.random.key(seed), 19)
    hidden = normal_values(key_of[0], (GROUPS, QG, DEC, D), 1.0, 6.0, ((0, 2), (1, 16)))
    encodings = normal_values(key_of[1], (P_SIZE, GROUPS, QG, SLOT, D), 1.0, 6.0, ((0, 16), (1, 2)))
    lengths = draw_lengths(jax.random.fold_in(key_of[18], 71), 0)
    cotangent = normal_values(key_of[3], (GROUPS, QG, DEC, D), 1.0, 6.0, ((0, 2), (1, 16)))
    self_query = normal_values(key_of[4], (D, D), (D * HD // 4) ** -0.5, 0.0546875)
    self_key = normal_values(key_of[5], (D, D), D ** -0.5, 0.21875)
    self_value = normal_values(key_of[6], (D, D), D ** -0.5, 0.21875)
    self_output = normal_values(key_of[7], (D, D), D ** -0.5, 0.21875)
    cross_query = normal_values(key_of[8], (D, D), (D * HD // 4) ** -0.5, 0.0546875)
    cross_key = normal_values(key_of[9], (D, D), D ** -0.5, 0.21875)
    cross_value = normal_values(key_of[10], (D, D), D ** -0.5, 0.21875)
    cross_output = normal_values(key_of[11], (D, D), (max(D // 32, 1)) ** -0.5, 1.25)
    feed_in = normal_values(key_of[12], (D, FF), D ** -0.5, 0.21875)
    feed_out = normal_values(key_of[13], (FF, D), FF ** -0.5, 0.109375)
    gain_self = jnp.clip(1.0 + 0.1 * jax.random.normal(key_of[14], (D,), jnp.float32), 0.5, 1.5)
    gain_cross = jnp.clip(1.0 + 0.1 * jax.random.normal(key_of[15], (D,), jnp.float32), 0.5, 1.5)
    gain_feed = jnp.clip(1.0 + 0.1 * jax.random.normal(key_of[16], (D,), jnp.float32), 0.5, 1.5)
    bias_table = normal_values(key_of[17], (NB, H), 1.0, 4.0, (), jnp.float32)
    return {"hidden": hidden, "encodings": encodings, "lengths": lengths, "cotangent": cotangent, "self_query": self_query, "self_key": self_key, "self_value": self_value, "self_output": self_output, "cross_query": cross_query, "cross_key": cross_key, "cross_value": cross_value, "cross_output": cross_output, "feed_in": feed_in, "feed_out": feed_out, "gain_self": gain_self, "gain_cross": gain_cross, "gain_feed": gain_feed, "bias_table": bias_table}


@jax.custom_vjp
def low(v):
    return lax.optimization_barrier(v.astype(jnp.bfloat16)).astype(jnp.float32)

@jax.custom_vjp
def low_back(v):
    return v

def low_keep(v):
    return (low(v), None)

def low_pass(kept, grad):
    return (grad,)

def back_keep(v):
    return (v, None)

def back_low(kept, grad):
    return (low(grad),)
low.defvjp(low_keep, low_pass)
low_back.defvjp(back_keep, back_low)
EPS = 1e-06
LIMITS = (19, 21, 24, 27, 31, 35, 40, 46, 52, 59, 67, 77, 87, 99, 113)

def matmul(left, right):
    return jnp.dot(left, right, precision=lax.Precision.HIGHEST, preferred_element_type=jnp.float32)

def rms_norm(value, gain):
    scale = lax.rsqrt(lax.optimization_barrier(jnp.mean(value * value, axis=-1, keepdims=True)) + EPS)
    return value * scale * gain

def smooth(value):
    return jax.nn.gelu(value, approximate=True)

def buckets(length):
    places = jnp.arange(length, dtype=jnp.int32)
    distance = jnp.maximum(places[:, None] - places[None, :], 0)
    beyond = jnp.zeros_like(distance)
    for edge in LIMITS:
        beyond = beyond + (distance >= edge).astype(jnp.int32)
    return jnp.where(distance < 16, distance, 16 + beyond)

def attend(query_rows, key_rows, value_rows, extra, allowed):
    heads = query_rows.shape[1] // HD

    def split(value):
        return value.reshape(value.shape[0], heads, HD).transpose(1, 0, 2)

    def one_head(parts):
        head_query, head_key, head_value, head_extra = parts
        scores = low_back(matmul(head_query, head_key.T)) + head_extra
        scores = jnp.where(allowed, scores, -1e+30)
        chances = low(jax.nn.softmax(scores, axis=-1))
        return matmul(chances, head_value)
    merged = lax.map(jax.checkpoint(one_head), (split(query_rows), split(key_rows), split(value_rows), extra))
    return merged.transpose(1, 0, 2).reshape(query_rows.shape[0], heads * HD)

def layer(hidden_rows, cross_rows, valid, causal, bucket, weights, gains, table):
    self_query, self_key, self_value, self_output, cross_query, cross_key, cross_value, cross_output, feed_in, feed_out = weights
    gain_self, gain_cross, gain_feed = gains
    normed_one = low(rms_norm(hidden_rows, gain_self))
    query_rows = low(low_back(matmul(normed_one, self_query)))
    key_rows = low(low_back(matmul(normed_one, self_key)))
    value_rows = low(low_back(matmul(normed_one, self_value)))
    extra = jnp.transpose(table[bucket], (2, 0, 1))
    mixed_one = low(low_back(attend(query_rows, key_rows, value_rows, extra, causal)))
    after_self = hidden_rows + low_back(matmul(mixed_one, self_output))
    normed_two = low(rms_norm(after_self, gain_cross))
    cross_queries = low(low_back(matmul(normed_two, cross_query)))
    cross_keys = low(low_back(matmul(cross_rows, cross_key)))
    cross_values = low(low_back(matmul(cross_rows, cross_value)))
    flat_extra = jnp.zeros((self_query.shape[1] // HD, 1, 1), jnp.float32)
    mixed_two = low(low_back(attend(cross_queries, cross_keys, cross_values, flat_extra, valid)))
    after_cross = after_self + low_back(matmul(mixed_two, cross_output))
    normed_three = low(rms_norm(after_cross, gain_feed))
    inner = low_back(matmul(normed_three, feed_in))
    active = low(smooth(inner))
    return after_cross + low_back(matmul(active, feed_out))

def reference(hidden, encodings, lengths, cotangent, self_query, self_key, self_value, self_output, cross_query, cross_key, cross_value, cross_output, feed_in, feed_out, gain_self, gain_cross, gain_feed, bias_table):
    weights = tuple((matrix.astype(jnp.float32) for matrix in (self_query, self_key, self_value, self_output, cross_query, cross_key, cross_value, cross_output, feed_in, feed_out)))
    gains = (gain_self, gain_cross, gain_feed)
    count = GROUPS * QG
    question_rows = hidden.reshape(count, DEC, D)
    cross_all = jnp.transpose(encodings, (1, 2, 0, 3, 4)).reshape(count, P_SIZE * SLOT, D)
    length_rows = lengths.reshape(count, P_SIZE)
    upstream_rows = cotangent.reshape(count, DEC, D)
    bucket = buckets(DEC)
    places = jnp.arange(DEC, dtype=jnp.int32)
    causal = places[:, None] >= places[None, :]
    slot_places = jnp.arange(SLOT, dtype=jnp.int32)

    def question(totals, item):
        rows_in, cross_in, length_in, upstream = item
        valid = (slot_places[None, :] < length_in[:, None]).reshape(1, P_SIZE * SLOT)

        def run(hidden_rows, cross_rows, weights_in, gains_in, table_in):
            return layer(hidden_rows, cross_rows, valid, causal, bucket, weights_in, gains_in, table_in)
        result, pull = jax.vjp(run, rows_in.astype(jnp.float32), cross_in.astype(jnp.float32), weights, gains, bias_table)
        grad_rows, grad_cross, grad_weights, grad_gains, grad_table = pull(upstream.astype(jnp.float32))
        totals = jax.tree.map(lambda left, right: left + right, totals, (grad_weights, grad_gains, grad_table))
        return (totals, (result, grad_rows, grad_cross.astype(jnp.bfloat16)))
    start = jax.tree.map(jnp.zeros_like, (weights, gains, bias_table))
    totals, (results, grad_rows, grad_cross) = lax.scan(question, start, (question_rows, cross_all, length_rows, upstream_rows))
    grad_weights, grad_gains, grad_table = totals
    layer_out = results.reshape(GROUPS, QG, DEC, D)
    hidden_grad = grad_rows.reshape(GROUPS, QG, DEC, D)
    encodings_grad = jnp.transpose(grad_cross.reshape(GROUPS, QG, P_SIZE, SLOT, D), (2, 0, 1, 3, 4))
    return (layer_out, hidden_grad, encodings_grad, grad_weights[0], grad_weights[1], grad_weights[2], grad_weights[3], grad_weights[4], grad_weights[5], grad_weights[6], grad_weights[7], grad_weights[8], grad_weights[9], grad_gains[0], grad_gains[1], grad_gains[2], grad_table)
```

```python
import functools

import jax
import jax.numpy as jnp
import numpy as np
from jax import lax
from jax.experimental import pallas as pl
from jax.experimental.pallas import tpu as pltpu
from jax.sharding import PartitionSpec as P

HD = 64
EPS = 1e-06
LIMITS = (19, 21, 24, 27, 31, 35, 40, 46, 52, 59, 67, 77, 87, 99, 113)
NEG = -1e30
BF = jnp.bfloat16
F32 = jnp.float32
MESH = pl.DeviceIdType.MESH
ROOT = 0.7978845608028654
VMEM_LIMIT = 56 << 20


def narrow(value):
    return value.astype(BF)


def dot_nn(left, right):
    return lax.dot_general(left, right, (((1,), (0,)), ((), ())), preferred_element_type=F32)


def dot_nt(left, right):
    return lax.dot_general(left, right, (((1,), (1,)), ((), ())), preferred_element_type=F32)


def dot_tn(left, right):
    return lax.dot_general(left, right, (((0,), (0,)), ((), ())), preferred_element_type=F32)


def rms(value, gain):
    scale = lax.rsqrt(jnp.mean(value * value, axis=-1, keepdims=True) + EPS)
    return value * scale * gain


def rms_back(value, gain, grad):
    scale = lax.rsqrt(jnp.mean(value * value, axis=-1, keepdims=True) + EPS)
    scaled = grad * gain
    inner = jnp.mean(scaled * value, axis=-1, keepdims=True)
    rows = scaled * scale - value * (scale * scale * scale * inner)
    gain_grad = jnp.sum(grad * (value * scale), axis=0, keepdims=True)
    return rows, gain_grad


def pair_mask(pair):
    lane = lax.broadcasted_iota(jnp.int32, pair.shape, 1)
    zero = jnp.zeros_like(pair)
    return jnp.concatenate(
        [jnp.where(lane < HD, pair, zero), jnp.where(lane >= HD, pair, zero)], axis=0
    )


def pair_diag(both, rows):
    return jnp.concatenate([both[:HD, :rows], both[HD:, rows:]], axis=0)


def bucket_onehot_rows(buckets, length):
    distance = lax.broadcasted_iota(jnp.int32, (buckets, length), 1)
    row = lax.broadcasted_iota(jnp.int32, (buckets, length), 0)
    beyond = jnp.zeros_like(distance)
    for edge in LIMITS:
        beyond = beyond + (distance >= edge).astype(jnp.int32)
    bucket = jnp.where(distance < 16, distance, 16 + beyond)
    return (bucket == row).astype(F32)


def head_bias(table, rows):
    onehot = bucket_onehot_rows(table.shape[0], rows)
    return lax.dot_general(
        table, onehot, (((0,), (0,)), ((), ())), precision=lax.Precision.HIGHEST,
        preferred_element_type=F32,
    )


def toeplitz(row, rows):
    return pltpu.roll(jnp.broadcast_to(row, (rows, rows)), 0, 1, stride=1, stride_axis=0)


def diagonal_sums(square):
    rows = square.shape[0]
    place = lax.broadcasted_iota(jnp.int32, square.shape, 0)
    for bit in range(3):
        moved = pltpu.roll(square, rows - (1 << bit), 1)
        square = jnp.where((place >> bit) & 1 == 1, moved, square)
    total = square[:8]
    for group in range(1, rows // 8):
        total = total + pltpu.roll(square[8 * group : 8 * group + 8], rows - 8 * group, 1)
    return jnp.sum(total, axis=0, keepdims=True)


def causal_mask(rows):
    key = lax.broadcasted_iota(jnp.int32, (rows, 2 * rows), 0)
    query = lax.broadcasted_iota(jnp.int32, (rows, 2 * rows), 1)
    query = jnp.where(query >= rows, query - rows, query)
    return key <= query


def self_forward_kernel(
    hidden, wq, wk, wv, wo, wcq, g1, g2, table,
    h1_out, q_out, k_out, v_out, mix_out, after_out, h2_out, cq_out,
):
    rows, width = hidden.shape
    pairs = width // (2 * HD)
    value = hidden[...].astype(F32)
    h1 = narrow(rms(value, g1[...]))
    h1_out[...] = h1
    q = narrow(dot_nn(h1, wq[...]))
    k = narrow(dot_nn(h1, wk[...]))
    v = narrow(dot_nn(h1, wv[...]))
    q_out[...] = q
    k_out[...] = k
    v_out[...] = v
    bias = head_bias(table[...], rows)
    allowed = causal_mask(rows)
    mixed = []
    for pair in range(pairs):
        at = slice(pair * 2 * HD, (pair + 1) * 2 * HD)
        scores = dot_nt(k[:, at], pair_mask(q[:, at]))
        both = jnp.concatenate(
            [toeplitz(bias[2 * pair : 2 * pair + 1], rows), toeplitz(bias[2 * pair + 1 : 2 * pair + 2], rows)],
            axis=1,
        )
        scores = jnp.where(allowed, scores + both, NEG)
        top = jnp.max(scores, axis=0, keepdims=True)
        raised = jnp.exp(scores - top)
        chances = raised / jnp.sum(raised, axis=0, keepdims=True)
        mixed.append(pair_diag(dot_tn(v[:, at], narrow(chances)), rows))
    mix = narrow(jnp.concatenate(mixed, axis=0).T)
    mix_out[...] = mix
    after = value + dot_nn(mix, wo[...])
    after_out[...] = after
    h2 = narrow(rms(after, g2[...]))
    h2_out[...] = h2
    cq_out[...] = narrow(dot_nn(h2, wcq[...]))


def cross_forward_kernel(slot, lengths, enc, wk, wv, cq, k_out, v_out, mix_out, lse_out, masked, top, total, acc):
    step = pl.program_id(0)
    rows, width = cq.shape
    block = enc.shape[0]
    pairs = width // (2 * HD)

    @pl.when(step == 0)
    def _():
        for pair in range(pairs):
            at = slice(pair * 2 * HD, (pair + 1) * 2 * HD)
            masked[pair] = pair_mask(cq[:, at])
        top[...] = jnp.full(top.shape, NEG, F32)
        total[...] = jnp.zeros(total.shape, F32)
        acc[...] = jnp.zeros(acc.shape, F32)

    source = enc[...]
    k_out[...] = narrow(dot_nn(source, wk[...]))
    v_out[...] = narrow(dot_nn(source, wv[...]))
    place = lax.broadcasted_iota(jnp.int32, (slot, 2 * rows), 0)
    passages = block // slot
    valid = jnp.concatenate([place < lengths[step * passages + i] for i in range(passages)], axis=0)
    for pair in range(pairs):
        at = slice(pair * 2 * HD, (pair + 1) * 2 * HD)
        scores = jnp.where(valid, dot_nt(k_out[:, at], masked[pair]), NEG)
        before = top[pair : pair + 1]
        now = jnp.maximum(before, jnp.max(scores, axis=0, keepdims=True))
        top[pair : pair + 1] = now
        fade = jnp.exp(before - now)
        raised = jnp.exp(scores - now)
        total[pair : pair + 1] = total[pair : pair + 1] * fade + jnp.sum(raised, axis=0, keepdims=True)
        part = pair_diag(dot_tn(v_out[:, at], narrow(raised)), rows)
        fades = jnp.concatenate(
            [jnp.broadcast_to(fade[:, :rows], (HD, rows)), jnp.broadcast_to(fade[:, rows:], (HD, rows))], axis=0
        )
        acc[at, :] = acc[at, :] * fades + part

    @pl.when(step == pl.num_programs(0) - 1)
    def _():
        for pair in range(pairs):
            at = slice(pair * 2 * HD, (pair + 1) * 2 * HD)
            sums = total[pair : pair + 1]
            lse_out[pair : pair + 1] = top[pair : pair + 1] + jnp.log(sums)
            inverse = 1.0 / sums
            spread = jnp.concatenate(
                [jnp.broadcast_to(inverse[:, :rows], (HD, rows)), jnp.broadcast_to(inverse[:, rows:], (HD, rows))],
                axis=0,
            )
            mix_out[at, :] = acc[at, :] * spread


def feed_kernel(
    mix_t, after_self, cot, wo, w_in, w_out, g3,
    result_out, grad_out, gmix_out, delta_out, dgain_out, d_in, d_out, d_o,
):
    rows, width = cot.shape
    hidden_units = w_in.shape[1]
    mix = narrow(mix_t[...].T)
    after = after_self[...] + dot_nn(mix, wo[...])
    h3 = narrow(rms(after, g3[...]))
    inner = dot_nn(h3, w_in[...])
    bent = jnp.tanh(ROOT * (inner + 0.044715 * (inner * inner * inner)))
    active = narrow(0.5 * inner * (1.0 + bent))
    result_out[...] = after + dot_nn(active, w_out[...])
    cb = cot[...]
    d_out[...] = narrow(dot_tn(active, cb))
    slope = 0.5 * (1.0 + bent) + (0.5 * ROOT) * inner * (1.0 - bent * bent) * (1.0 + (3 * 0.044715) * inner * inner)
    gi = narrow(dot_nt(cb, w_out[...]) * slope)
    pieces = hidden_units // width
    for piece in range(pieces):
        d_in[piece] = narrow(dot_tn(h3, gi[:, piece * width : (piece + 1) * width]))
    back, gain_grad = rms_back(after, g3[...], dot_nt(gi, w_in[...]))
    dgain_out[...] = gain_grad
    grad = cb.astype(F32) + back
    grad_out[...] = grad
    gb = narrow(grad)
    d_o[...] = narrow(dot_tn(mix, gb))
    gmix = narrow(dot_nt(gb, wo[...]))
    gmix_out[...] = gmix
    product = gmix.astype(F32).T * mix_t[...]
    for pair in range(width // (2 * HD)):
        first = jnp.sum(product[pair * 2 * HD : pair * 2 * HD + HD], axis=0, keepdims=True)
        second = jnp.sum(product[pair * 2 * HD + HD : (pair + 1) * 2 * HD], axis=0, keepdims=True)
        delta_out[pair : pair + 1] = jnp.concatenate([first, second], axis=1)


def cross_backward_kernel(
    slot, lengths, enc, k, v, wk, wv, cq, gmix, lse, delta,
    enc_out, dq_out, dk_out, dv_out, masked, gmasked, dq_t, dkv, acc,
):
    step = pl.program_id(0)
    rows, width = cq.shape
    block = enc.shape[0]
    pairs = width // (2 * HD)

    @pl.when(step == 0)
    def _():
        for pair in range(pairs):
            at = slice(pair * 2 * HD, (pair + 1) * 2 * HD)
            masked[pair] = pair_mask(cq[:, at])
            gmasked[pair] = pair_mask(gmix[:, at])
        dq_t[...] = jnp.zeros(dq_t.shape, F32)
        acc[...] = jnp.zeros(acc.shape, F32)

    place = lax.broadcasted_iota(jnp.int32, (slot, 2 * rows), 0)
    passages = block // slot
    valid = jnp.concatenate([place < lengths[step * passages + i] for i in range(passages)], axis=0)
    for pair in range(pairs):
        at = slice(pair * 2 * HD, (pair + 1) * 2 * HD)
        scores = jnp.where(valid, dot_nt(k[:, at], masked[pair]), NEG)
        chances = jnp.exp(scores - lse[pair : pair + 1])
        dkv[:, width + pair * 2 * HD : width + (pair + 1) * 2 * HD] = narrow(dot_nn(narrow(chances), gmasked[pair]))
        ds = narrow(chances * (dot_nt(v[:, at], gmasked[pair]) - delta[pair : pair + 1]))
        dkv[:, at] = narrow(dot_nn(ds, masked[pair]))
        dq_t[at, :] = dq_t[at, :] + pair_diag(dot_tn(k[:, at], ds), rows)
    enc_out[...] = narrow(dot_nt(dkv[:, :width], wk[...]) + dot_nt(dkv[:, width:], wv[...]))
    acc[...] = acc[...] + dot_tn(enc[...], dkv[...])

    @pl.when(step == pl.num_programs(0) - 1)
    def _():
        dq_out[...] = narrow(dq_t[...].T)
        dk_out[...] = narrow(acc[:, :width])
        dv_out[...] = narrow(acc[:, width:])


def self_backward_kernel(
    hidden, h1, q, k, v, mix, after_self, h2, dcq, grad_cross, wq, wk, wv, wo, wcq, g1, g2, table,
    hidden_out, d_cq, d_o, d_q, d_k, d_v, dg1_out, dg2_out, dtable_out,
):
    rows, width = hidden.shape
    pairs = width // (2 * HD)
    d_cq[...] = narrow(dot_tn(h2[...], dcq[...]))
    back, gain_grad = rms_back(after_self[...], g2[...], dot_nt(dcq[...], wcq[...]))
    dg2_out[...] = gain_grad
    grad = grad_cross[...] + back
    sb = narrow(grad)
    d_o[...] = narrow(dot_tn(mix[...], sb))
    gmix = narrow(dot_nt(sb, wo[...]))
    bias = head_bias(table[...], rows)
    allowed = causal_mask(rows)
    dq_parts, dk_parts, dv_parts, sums = [], [], [], []
    for pair in range(pairs):
        at = slice(pair * 2 * HD, (pair + 1) * 2 * HD)
        masked = pair_mask(q[:, at])
        gmasked = pair_mask(gmix[:, at])
        scores = dot_nt(k[:, at], masked)
        both = jnp.concatenate(
            [toeplitz(bias[2 * pair : 2 * pair + 1], rows), toeplitz(bias[2 * pair + 1 : 2 * pair + 2], rows)],
            axis=1,
        )
        scores = jnp.where(allowed, scores + both, NEG)
        top = jnp.max(scores, axis=0, keepdims=True)
        raised = jnp.exp(scores - top)
        chances = raised / jnp.sum(raised, axis=0, keepdims=True)
        dv_parts.append(narrow(dot_nn(narrow(chances), gmasked)))
        dp = dot_nt(v[:, at], gmasked)
        ds = chances * (dp - jnp.sum(chances * dp, axis=0, keepdims=True))
        sums.append(diagonal_sums(ds[:, :rows]))
        sums.append(diagonal_sums(ds[:, rows:]))
        dsb = narrow(ds)
        dk_parts.append(narrow(dot_nn(dsb, masked)))
        dq_parts.append(pair_diag(dot_tn(k[:, at], dsb), rows))
    dq = narrow(jnp.concatenate(dq_parts, axis=0).T)
    dk = jnp.concatenate(dk_parts, axis=1)
    dv = jnp.concatenate(dv_parts, axis=1)
    d_q[...] = narrow(dot_tn(h1[...], dq))
    d_k[...] = narrow(dot_tn(h1[...], dk))
    d_v[...] = narrow(dot_tn(h1[...], dv))
    into = dot_nt(dq, wq[...]) + dot_nt(dk, wk[...]) + dot_nt(dv, wv[...])
    back, gain_grad = rms_back(hidden[...].astype(F32), g1[...], into)
    dg1_out[...] = gain_grad
    hidden_out[...] = grad + back
    by_distance = jnp.concatenate(sums, axis=0)
    onehot = bucket_onehot_rows(table.shape[0], rows)
    dtable_out[...] = lax.dot_general(
        onehot, by_distance, (((1,), (1,)), ((), ())), precision=lax.Precision.HIGHEST, preferred_element_type=F32
    )


def add_rows(left, right, dest):
    count = dest.shape[0]

    def one(index, carry):
        dest[index] = narrow(left[index].astype(F32) + right[index].astype(F32))
        return carry

    lax.fori_loop(0, count, one, 0)


def reduce_kernel(n, singles, grouped, *refs):
    pieces = singles + grouped
    ins = list(refs[:singles]) + [refs[singles].at[:, i] for i in range(grouped)]
    small_in, out, small_out = refs[singles + 1 : singles + 4]
    bits = n.bit_length() - 1
    scratch = refs[singles + 4 :]
    mine, other, stages = scratch[0], scratch[1], scratch[2 : 2 + bits]
    local_sem, send_sem, recv_sem, small_buf, small_send, small_recv, last_sem = scratch[2 + bits : 9 + bits]
    half = pieces // 2
    me, core = lax.axis_index("pass"), lax.axis_index("pb")
    partner = (me, 1 - core)

    barrier = pltpu.get_barrier_semaphore()
    pl.semaphore_signal(barrier, inc=1, device_id=partner, device_id_type=MESH)
    for bit in range(bits):
        pl.semaphore_signal(barrier, inc=1, device_id=(me ^ (1 << bit), core), device_id_type=MESH)
    pl.semaphore_wait(barrier, bits + 1)

    def remote(src, dst, send, recv, device):
        return pltpu.make_async_remote_copy(
            src_ref=src, dst_ref=dst, send_sem=send, recv_sem=recv, device_id=device, device_id_type=MESH
        )

    def order(piece):
        first = list(range(bits))
        if piece % 2 and bits > 1:
            first[0], first[1] = first[1], first[0]
        return first

    def split(ref, piece, stage):
        done = order(piece)[:stage]
        bit = order(piece)[stage]
        low = 1 << len([b for b in range(bit) if b not in done])
        count = n >> stage
        view = ref.reshape(count // (2 * low), 2, low, ref.shape[-2], ref.shape[-1])
        return view, (me >> bit) & 1, low, count // (2 * low), bit

    def swap(i, c):
        return remote(ins[2 * i + 1 - c], other.at[i], send_sem.at[i, 0], recv_sem.at[i, 0], partner)

    def fetch(i, c):
        return pltpu.make_async_copy(ins[2 * i + c], mine.at[i], local_sem.at[i])

    for i in range(half):
        for c in range(2):

            @pl.when(core == c)
            def _(i=i, c=c):
                swap(i, c).start()
                fetch(i, c).start()

    def source(i, stage):
        return other.at[i] if stage == 0 else stages[stage - 1].at[i]

    def stage_copy(i, stage):
        view, value, low, high, bit = split(source(i, stage), i, stage)
        dst = stages[stage].at[i].reshape(high, low, *mine.shape[-2:])
        return remote(
            view.at[:, 1 - value], dst, send_sem.at[i, stage + 1], recv_sem.at[i, stage + 1], (me ^ (1 << bit), core)
        )

    def small_copy(stage):
        device = partner if stage == bits else (me ^ (1 << stage), core)
        return remote(small_buf.at[stage], small_buf.at[bits + 1 + stage], small_send.at[stage], small_recv.at[stage], device)

    small_buf[0] = small_in[...]
    small_copy(0).start()

    def last_copy(i):
        return remote(out_buf(i), out_buf2(i), last_sem.at[0, i], last_sem.at[1, i], partner)

    out_own, out_other = scratch[-2], scratch[-1]

    def out_buf(i):
        return out_own.at[i]

    def out_buf2(i):
        return out_other.at[i]

    for tick in range(half + bits + 1):
        for stage in reversed(range(bits + 1)):
            i = tick - stage
            if not 0 <= i < half:
                continue
            if stage == 0:
                for c in range(2):

                    @pl.when(core == c)
                    def _(i=i, c=c):
                        fetch(i, c).wait()

                swap(i, 0).wait_recv()
                add_rows(mine.at[i], other.at[i], other.at[i])
            else:
                copy = stage_copy(i, stage - 1)
                copy.wait_recv()
                view, value, low, high, bit = split(source(i, stage - 1), i, stage - 1)
                dst = stages[stage - 1].at[i]
                if stage < bits:
                    kept = view.at[:, value]

                    def one(index, carry, kept=kept, dst=dst, low=low):
                        dst[index] = narrow(kept[index // low, index % low].astype(F32) + dst[index].astype(F32))
                        return carry

                    lax.fori_loop(0, high * low, one, 0)
                else:
                    total = view[0, value, 0].astype(F32) + dst[0].astype(F32)
                    out_own[i] = narrow(total)
                    for c in range(2):

                        @pl.when(core == c)
                        def _(i=i, c=c, total=total):
                            out[2 * i + c] = total

            if stage < bits:
                stage_copy(i, stage).start()
            else:
                last_copy(i).start()
        if 1 <= tick <= bits + 1:
            stage = tick - 1
            small_copy(stage).wait_recv()
            total = small_buf[stage] + small_buf[bits + 1 + stage]
            if stage < bits:
                small_buf[stage + 1] = total
                small_copy(stage + 1).start()
            else:
                small_out[...] = total
    for i in range(half):
        last_copy(i).wait_recv()
        for c in range(2):

            @pl.when(core == c)
            def _(i=i, c=c):
                out[2 * i + 1 - c] = out_other[i].astype(F32)

    for i in range(half):
        swap(i, 0).wait_send()
        for stage in range(bits):
            stage_copy(i, stage).wait_send()
        last_copy(i).wait_send()
    for stage in range(bits + 1):
        small_copy(stage).wait_send()


def reduce_all(n, parts, group, small):
    pieces = len(parts) + group.shape[1]
    half = pieces // 2
    _, rows, width = parts[0].shape
    bits = n.bit_length() - 1
    stage_shapes = [pltpu.VMEM((half, n >> (s + 1), rows, width), BF) for s in range(bits)]
    return pl.pallas_call(
        functools.partial(reduce_kernel, n, len(parts), group.shape[1]),
        out_shape=(jax.ShapeDtypeStruct((pieces, rows, width), F32), jax.ShapeDtypeStruct(small.shape, F32)),
        in_specs=[pl.BlockSpec(memory_space=pl.ANY)] * (len(parts) + 1) + [pl.BlockSpec(memory_space=pltpu.VMEM)],
        out_specs=(pl.BlockSpec(memory_space=pltpu.VMEM), pl.BlockSpec(memory_space=pltpu.VMEM)),
        scratch_shapes=[pltpu.VMEM((half, n, rows, width), BF), pltpu.VMEM((half, n, rows, width), BF)]
        + stage_shapes
        + [
            pltpu.SemaphoreType.DMA((half,)),
            pltpu.SemaphoreType.DMA((half, bits + 1)),
            pltpu.SemaphoreType.DMA((half, bits + 1)),
            pltpu.VMEM((2 * (bits + 1),) + small.shape, F32),
            pltpu.SemaphoreType.DMA((bits + 1,)),
            pltpu.SemaphoreType.DMA((bits + 1,)),
            pltpu.SemaphoreType.DMA((2, half)),
            pltpu.VMEM((half, rows, width), BF),
            pltpu.VMEM((half, rows, width), BF),
        ],
        compiler_params=pltpu.CompilerParams(collective_id=0, has_side_effects=True, vmem_limit_bytes=VMEM_LIMIT),
    )(*parts, group, small)


def whole(shape=None):
    return pl.BlockSpec(memory_space=pltpu.VMEM)


def call(kernel, outs, *args):
    return pl.pallas_call(
        kernel,
        out_shape=tuple(jax.ShapeDtypeStruct(shape, kind) for shape, kind in outs),
        in_specs=[whole()] * len(args),
        out_specs=tuple(whole() for _ in outs),
        compiler_params=pltpu.CompilerParams(vmem_limit_bytes=VMEM_LIMIT),
    )(*args)


def per_device(
    n, hidden, encodings, lengths, cotangent, wq, wk, wv, wo, wcq, wck, wcv, wco, w_in, w_out,
    gain_self, gain_cross, gain_feed, table,
):
    rows, width = hidden.shape[2], hidden.shape[3]
    slot = encodings.shape[3]
    passages = lengths.shape[2]
    units = w_in.shape[1]
    pairs = width // (2 * HD)
    keys = passages * slot
    own = hidden.reshape(rows, width)
    cot = cotangent.reshape(rows, width)
    g1, g2, g3 = (gain.reshape(1, width) for gain in (gain_self, gain_cross, gain_feed))
    length_row = lengths.reshape(passages)
    source = lax.all_to_all(encodings, "pass", split_axis=2, concat_axis=0, tiled=True).reshape(keys, width)

    sixteen, wide = ((rows, width), BF), ((rows, width), F32)
    h1, q, k, v, mix1, after_self, h2, cq = call(
        self_forward_kernel,
        [sixteen] * 5 + [wide, sixteen, sixteen],
        own, wq, wk, wv, wo, wcq, g1, g2, table,
    )

    block = 4 * slot
    steps = keys // block
    stats = jax.ShapeDtypeStruct((pairs, 2 * rows), F32)
    smem = pl.BlockSpec(memory_space=pltpu.SMEM)
    tile = pl.BlockSpec((block, width), lambda i: (i, 0))
    square = pl.BlockSpec((width, width), lambda i: (0, 0))
    query = pl.BlockSpec((rows, width), lambda i: (0, 0))
    stat = pl.BlockSpec((pairs, 2 * rows), lambda i: (0, 0))
    ck, cv, mix_t, lse = pl.pallas_call(
        functools.partial(cross_forward_kernel, slot),
        grid=(steps,),
        out_shape=(
            jax.ShapeDtypeStruct((keys, width), BF),
            jax.ShapeDtypeStruct((keys, width), BF),
            jax.ShapeDtypeStruct((width, rows), F32),
            stats,
        ),
        in_specs=[smem, tile, square, square, query],
        out_specs=(tile, tile, pl.BlockSpec((width, rows), lambda i: (0, 0)), stat),
        scratch_shapes=[
            pltpu.VMEM((pairs, 2 * rows, 2 * HD), BF),
            pltpu.VMEM((pairs, 2 * rows), F32),
            pltpu.VMEM((pairs, 2 * rows), F32),
            pltpu.VMEM((width, rows), F32),
        ],
        compiler_params=pltpu.CompilerParams(vmem_limit_bytes=VMEM_LIMIT),
    )(length_row, source, wck, wcv, cq)

    pieces = units // width
    result, grad_cross, gmix, delta, dg3, d_in, d_out, d_co = call(
        feed_kernel,
        [wide, wide, sixteen, ((pairs, 2 * rows), F32), ((1, width), F32), ((pieces, width, width), BF),
         ((units, width), BF), ((width, width), BF)],
        mix_t, after_self, cot, wco, w_in, w_out, g3,
    )

    enc_grad, dcq, d_ck, d_cv = pl.pallas_call(
        functools.partial(cross_backward_kernel, slot),
        grid=(steps,),
        out_shape=(
            jax.ShapeDtypeStruct((keys, width), BF),
            jax.ShapeDtypeStruct((rows, width), BF),
            jax.ShapeDtypeStruct((width, width), BF),
            jax.ShapeDtypeStruct((width, width), BF),
        ),
        in_specs=[smem, tile, tile, tile, square, square, query, query, stat, stat],
        out_specs=(tile, query, square, square),
        scratch_shapes=[
            pltpu.VMEM((pairs, 2 * rows, 2 * HD), BF),
            pltpu.VMEM((pairs, 2 * rows, 2 * HD), BF),
            pltpu.VMEM((width, rows), F32),
            pltpu.VMEM((block, 2 * width), BF),
            pltpu.VMEM((width, 2 * width), F32),
        ],
        compiler_params=pltpu.CompilerParams(vmem_limit_bytes=VMEM_LIMIT),
    )(length_row, source, ck, cv, wck, wcv, cq, gmix, lse, delta)
    returned = lax.all_to_all(
        enc_grad.reshape(passages, 1, 1, slot, width), "pass", split_axis=0, concat_axis=2, tiled=True
    )

    gain_kind = ((1, width), F32)
    squared = ((width, width), BF)
    hidden_grad, d_cq, d_so, d_q, d_k, d_v, dg1, dg2, dtable = call(
        self_backward_kernel,
        [wide] + [squared] * 5 + [gain_kind, gain_kind, (table.shape, F32)],
        own, h1, q, k, v, mix1, after_self, h2, dcq, grad_cross, wq, wk, wv, wo, wcq, g1, g2, table,
    )

    share = width // n
    if n & (n - 1) == 0 and share % 16 == 0:
        squares = [d_q, d_k, d_v, d_so, d_cq, d_ck, d_cv, d_co]
        parts = [d.reshape(n, share, width) for d in squares]
        parts += [d_in[i].reshape(n, share, width) for i in range(pieces)]
        big = d_out.reshape(n, pieces, share, width)
        flat = jnp.concatenate([dg1, dg2, dg3, jnp.pad(dtable.reshape(1, -1), ((0, 0), (0, width - dtable.size))),
                                jnp.zeros((4, width), F32)], axis=0)
        sums, small = reduce_all(n, parts, big, flat)
        totals = [sums[i] for i in range(8)]
        count = len(squares)
        in_total = jnp.concatenate([sums[count + i] for i in range(pieces)], axis=1)
        out_total = sums[count + pieces :].reshape(pieces * share, width)
        me = lax.axis_index("pass")
        gains = [lax.dynamic_slice(small[i], (me * share,), (share,)) for i in range(3)]
        table_sum = small[3, : dtable.size].reshape(table.shape)
    else:
        both = [d_q, d_k, d_v, d_so, d_cq, d_ck, d_cv, d_co, d_in.transpose(1, 0, 2).reshape(width, units), d_out]

        def total(part):
            shared = lax.psum_scatter(part, "pass", scatter_dimension=0, tiled=True)
            return lax.psum(shared.astype(BF), "pb").astype(F32)

        sums = [total(part.astype(F32)) for part in both]
        totals, in_total, out_total = sums[:8], sums[8], sums[9]
        gains = [total(part.reshape(width)) for part in (dg1, dg2, dg3)]
        table_sum = lax.psum(dtable, ("pass", "pb"))
    return (
        (result.reshape(hidden.shape), hidden_grad.reshape(hidden.shape), returned)
        + tuple(totals)
        + (in_total, out_total)
        + tuple(gains)
        + (table_sum,)
    )


def solution(mesh):
    rows = P("pb", "pass", None, None)
    passage = P("pass", "pb", None, None, None)
    in_specs = (rows, passage, P("pb", "pass", None), rows) + (P(),) * 14
    out_specs = (rows, rows, passage) + (P("pass", None),) * 10 + (P("pass"),) * 3 + (P(),)
    return jax.shard_map(
        functools.partial(per_device, mesh.shape["pass"]),
        mesh=mesh,
        in_specs=in_specs,
        out_specs=out_specs,
        check_vma=False,
    )
```

```python
import functools

import jax
import jax.numpy as jnp
import numpy as np
from jax import lax
from jax.experimental import pallas as pl
from jax.experimental.pallas import tpu as pltpu
from jax.sharding import PartitionSpec as P

HD = 64
EPS = 1e-06
LIMITS = (19, 21, 24, 27, 31, 35, 40, 46, 52, 59, 67, 77, 87, 99, 113)
NEG = -1e30
BF = jnp.bfloat16
F32 = jnp.float32
MESH = pl.DeviceIdType.MESH
ROOT = 0.7978845608028654
VMEM_LIMIT = 56 << 20
LAYER_LIMIT = 63 << 20


def narrow(value):
    return value.astype(BF)


def dot_nn(left, right):
    return lax.dot_general(left, right, (((1,), (0,)), ((), ())), preferred_element_type=F32)


def dot_nt(left, right):
    return lax.dot_general(left, right, (((1,), (1,)), ((), ())), preferred_element_type=F32)


def dot_tn(left, right):
    return lax.dot_general(left, right, (((0,), (0,)), ((), ())), preferred_element_type=F32)


def rms(value, gain):
    scale = lax.rsqrt(jnp.mean(value * value, axis=-1, keepdims=True) + EPS)
    return value * scale * gain


def rms_back(value, gain, grad):
    scale = lax.rsqrt(jnp.mean(value * value, axis=-1, keepdims=True) + EPS)
    scaled = grad * gain
    inner = jnp.mean(scaled * value, axis=-1, keepdims=True)
    rows = scaled * scale - value * (scale * scale * scale * inner)
    gain_grad = jnp.sum(grad * (value * scale), axis=0, keepdims=True)
    return rows, gain_grad


def pair_mask(pair):
    lane = lax.broadcasted_iota(jnp.int32, pair.shape, 1)
    zero = jnp.zeros_like(pair)
    return jnp.concatenate(
        [jnp.where(lane < HD, pair, zero), jnp.where(lane >= HD, pair, zero)], axis=0
    )


def pair_diag(both, rows):
    return jnp.concatenate([both[:HD, :rows], both[HD:, rows:]], axis=0)


def bucket_onehot_rows(buckets, length):
    distance = lax.broadcasted_iota(jnp.int32, (buckets, length), 1)
    row = lax.broadcasted_iota(jnp.int32, (buckets, length), 0)
    beyond = jnp.zeros_like(distance)
    for edge in LIMITS:
        beyond = beyond + (distance >= edge).astype(jnp.int32)
    bucket = jnp.where(distance < 16, distance, 16 + beyond)
    return (bucket == row).astype(F32)


def head_bias(table, rows):
    onehot = bucket_onehot_rows(table.shape[1], rows)
    return lax.dot_general(
        table, onehot, (((1,), (0,)), ((), ())), precision=lax.Precision.HIGHEST,
        preferred_element_type=F32,
    )


def toeplitz(row, rows):
    return pltpu.roll(jnp.broadcast_to(row, (rows, rows)), 0, 1, stride=1, stride_axis=0)


def diagonal_sums(square):
    rows = square.shape[0]
    place = lax.broadcasted_iota(jnp.int32, square.shape, 0)
    for bit in range(3):
        moved = pltpu.roll(square, rows - (1 << bit), 1)
        square = jnp.where((place >> bit) & 1 == 1, moved, square)
    total = square[:8]
    for group in range(1, rows // 8):
        total = total + pltpu.roll(square[8 * group : 8 * group + 8], rows - 8 * group, 1)
    return jnp.sum(total, axis=0, keepdims=True)


def causal_mask(rows):
    key = lax.broadcasted_iota(jnp.int32, (rows, 2 * rows), 0)
    query = lax.broadcasted_iota(jnp.int32, (rows, 2 * rows), 1)
    query = jnp.where(query >= rows, query - rows, query)
    return key <= query


def self_forward_kernel(
    hidden, wq, wk, wv, wo, wcq, g1, g2, table,
    h1_out, q_out, k_out, v_out, mix_out, after_out, h2_out, cq_out,
):
    rows, width = hidden.shape
    pairs = width // (2 * HD)
    value = hidden[...].astype(F32)
    h1 = narrow(rms(value, g1[...]))
    h1_out[...] = h1
    q = narrow(dot_nn(h1, wq[...]))
    k = narrow(dot_nn(h1, wk[...]))
    v = narrow(dot_nn(h1, wv[...]))
    q_out[...] = q
    k_out[...] = k
    v_out[...] = v
    bias = head_bias(table[...].T, rows)
    allowed = causal_mask(rows)
    mixed = []
    for pair in range(pairs):
        at = slice(pair * 2 * HD, (pair + 1) * 2 * HD)
        scores = dot_nt(k[:, at], pair_mask(q[:, at]))
        both = jnp.concatenate(
            [toeplitz(bias[2 * pair : 2 * pair + 1], rows), toeplitz(bias[2 * pair + 1 : 2 * pair + 2], rows)],
            axis=1,
        )
        scores = jnp.where(allowed, scores + both, NEG)
        top = jnp.max(scores, axis=0, keepdims=True)
        raised = jnp.exp(scores - top)
        chances = raised / jnp.sum(raised, axis=0, keepdims=True)
        mixed.append(pair_diag(dot_tn(v[:, at], narrow(chances)), rows))
    mix = narrow(jnp.concatenate(mixed, axis=0).T)
    mix_out[...] = mix
    after = value + dot_nn(mix, wo[...])
    after_out[...] = after
    h2 = narrow(rms(after, g2[...]))
    h2_out[...] = h2
    cq_out[...] = narrow(dot_nn(h2, wcq[...]))


def cross_forward_kernel(slot, lengths, enc, wk, wv, cq, k_out, v_out, mix_out, lse_out, masked, top, total, acc):
    step = pl.program_id(0)
    rows, width = cq.shape
    block = enc.shape[0]
    pairs = width // (2 * HD)

    @pl.when(step == 0)
    def _():
        for pair in range(pairs):
            at = slice(pair * 2 * HD, (pair + 1) * 2 * HD)
            masked[pair] = pair_mask(cq[:, at])
        top[...] = jnp.full(top.shape, NEG, F32)
        total[...] = jnp.zeros(total.shape, F32)
        acc[...] = jnp.zeros(acc.shape, F32)

    source = enc[...]
    k_out[...] = narrow(dot_nn(source, wk[...]))
    v_out[...] = narrow(dot_nn(source, wv[...]))
    place = lax.broadcasted_iota(jnp.int32, (slot, 2 * rows), 0)
    passages = block // slot
    valid = jnp.concatenate([place < lengths[step * passages + i] for i in range(passages)], axis=0)
    for pair in range(pairs):
        at = slice(pair * 2 * HD, (pair + 1) * 2 * HD)
        scores = jnp.where(valid, dot_nt(k_out[:, at], masked[pair]), NEG)
        before = top[pair : pair + 1]
        now = jnp.maximum(before, jnp.max(scores, axis=0, keepdims=True))
        top[pair : pair + 1] = now
        fade = jnp.exp(before - now)
        raised = jnp.exp(scores - now)
        total[pair : pair + 1] = total[pair : pair + 1] * fade + jnp.sum(raised, axis=0, keepdims=True)
        part = pair_diag(dot_tn(v_out[:, at], narrow(raised)), rows)
        fades = jnp.concatenate(
            [jnp.broadcast_to(fade[:, :rows], (HD, rows)), jnp.broadcast_to(fade[:, rows:], (HD, rows))], axis=0
        )
        acc[at, :] = acc[at, :] * fades + part

    @pl.when(step == pl.num_programs(0) - 1)
    def _():
        for pair in range(pairs):
            at = slice(pair * 2 * HD, (pair + 1) * 2 * HD)
            sums = total[pair : pair + 1]
            lse_out[pair : pair + 1] = top[pair : pair + 1] + jnp.log(sums)
            inverse = 1.0 / sums
            spread = jnp.concatenate(
                [jnp.broadcast_to(inverse[:, :rows], (HD, rows)), jnp.broadcast_to(inverse[:, rows:], (HD, rows))],
                axis=0,
            )
            mix_out[at, :] = acc[at, :] * spread


def feed_kernel(
    mix_t, after_self, cot, wo, w_in, w_out, g3,
    result_out, grad_out, gmix_out, delta_out, dgain_out, d_in, d_out, d_o,
):
    rows, width = cot.shape
    hidden_units = w_in.shape[1]
    mix = narrow(mix_t[...].T)
    after = after_self[...] + dot_nn(mix, wo[...])
    h3 = narrow(rms(after, g3[...]))
    inner = dot_nn(h3, w_in[...])
    bent = jnp.tanh(ROOT * (inner + 0.044715 * (inner * inner * inner)))
    active = narrow(0.5 * inner * (1.0 + bent))
    result_out[...] = after + dot_nn(active, w_out[...])
    cb = cot[...]
    d_out[...] = narrow(dot_tn(active, cb))
    slope = 0.5 * (1.0 + bent) + (0.5 * ROOT) * inner * (1.0 - bent * bent) * (1.0 + (3 * 0.044715) * inner * inner)
    gi = narrow(dot_nt(cb, w_out[...]) * slope)
    pieces = hidden_units // width
    for piece in range(pieces):
        d_in[piece] = narrow(dot_tn(h3, gi[:, piece * width : (piece + 1) * width]))
    back, gain_grad = rms_back(after, g3[...], dot_nt(gi, w_in[...]))
    dgain_out[...] = gain_grad
    grad = cb.astype(F32) + back
    grad_out[...] = grad
    gb = narrow(grad)
    d_o[...] = narrow(dot_tn(mix, gb))
    gmix = narrow(dot_nt(gb, wo[...]))
    gmix_out[...] = gmix
    product = gmix.astype(F32).T * mix_t[...]
    for pair in range(width // (2 * HD)):
        first = jnp.sum(product[pair * 2 * HD : pair * 2 * HD + HD], axis=0, keepdims=True)
        second = jnp.sum(product[pair * 2 * HD + HD : (pair + 1) * 2 * HD], axis=0, keepdims=True)
        delta_out[pair : pair + 1] = jnp.concatenate([first, second], axis=1)


def cross_backward_kernel(
    slot, lengths, enc, k, v, wk, wv, cq, gmix, lse, delta,
    enc_out, dq_out, dk_out, dv_out, masked, gmasked, dq_t, dkv, acc,
):
    step = pl.program_id(0)
    rows, width = cq.shape
    block = enc.shape[0]
    pairs = width // (2 * HD)

    @pl.when(step == 0)
    def _():
        for pair in range(pairs):
            at = slice(pair * 2 * HD, (pair + 1) * 2 * HD)
            masked[pair] = pair_mask(cq[:, at])
            gmasked[pair] = pair_mask(gmix[:, at])
        dq_t[...] = jnp.zeros(dq_t.shape, F32)
        acc[...] = jnp.zeros(acc.shape, F32)

    place = lax.broadcasted_iota(jnp.int32, (slot, 2 * rows), 0)
    passages = block // slot
    valid = jnp.concatenate([place < lengths[step * passages + i] for i in range(passages)], axis=0)
    for pair in range(pairs):
        at = slice(pair * 2 * HD, (pair + 1) * 2 * HD)
        scores = jnp.where(valid, dot_nt(k[:, at], masked[pair]), NEG)
        chances = jnp.exp(scores - lse[pair : pair + 1])
        dkv[:, width + pair * 2 * HD : width + (pair + 1) * 2 * HD] = narrow(dot_nn(narrow(chances), gmasked[pair]))
        ds = narrow(chances * (dot_nt(v[:, at], gmasked[pair]) - delta[pair : pair + 1]))
        dkv[:, at] = narrow(dot_nn(ds, masked[pair]))
        dq_t[at, :] = dq_t[at, :] + pair_diag(dot_tn(k[:, at], ds), rows)
    enc_out[...] = narrow(dot_nt(dkv[:, :width], wk[...]) + dot_nt(dkv[:, width:], wv[...]))
    acc[...] = acc[...] + dot_tn(enc[...], dkv[...])

    @pl.when(step == pl.num_programs(0) - 1)
    def _():
        dq_out[...] = narrow(dq_t[...].T)
        dk_out[...] = narrow(acc[:, :width])
        dv_out[...] = narrow(acc[:, width:])


def self_backward_kernel(
    hidden, h1, q, k, v, mix, after_self, h2, dcq, grad_cross, wq, wk, wv, wo, wcq, g1, g2, table,
    hidden_out, d_cq, d_o, d_q, d_k, d_v, dg1_out, dg2_out, dtable_out,
):
    rows, width = hidden.shape
    pairs = width // (2 * HD)
    d_cq[...] = narrow(dot_tn(h2[...], dcq[...]))
    back, gain_grad = rms_back(after_self[...], g2[...], dot_nt(dcq[...], wcq[...]))
    dg2_out[...] = gain_grad
    grad = grad_cross[...] + back
    sb = narrow(grad)
    d_o[...] = narrow(dot_tn(mix[...], sb))
    gmix = narrow(dot_nt(sb, wo[...]))
    bias = head_bias(table[...].T, rows)
    allowed = causal_mask(rows)
    dq_parts, dk_parts, dv_parts, sums = [], [], [], []
    for pair in range(pairs):
        at = slice(pair * 2 * HD, (pair + 1) * 2 * HD)
        masked = pair_mask(q[:, at])
        gmasked = pair_mask(gmix[:, at])
        scores = dot_nt(k[:, at], masked)
        both = jnp.concatenate(
            [toeplitz(bias[2 * pair : 2 * pair + 1], rows), toeplitz(bias[2 * pair + 1 : 2 * pair + 2], rows)],
            axis=1,
        )
        scores = jnp.where(allowed, scores + both, NEG)
        top = jnp.max(scores, axis=0, keepdims=True)
        raised = jnp.exp(scores - top)
        chances = raised / jnp.sum(raised, axis=0, keepdims=True)
        dv_parts.append(narrow(dot_nn(narrow(chances), gmasked)))
        dp = dot_nt(v[:, at], gmasked)
        ds = chances * (dp - jnp.sum(chances * dp, axis=0, keepdims=True))
        sums.append(diagonal_sums(ds[:, :rows]))
        sums.append(diagonal_sums(ds[:, rows:]))
        dsb = narrow(ds)
        dk_parts.append(narrow(dot_nn(dsb, masked)))
        dq_parts.append(pair_diag(dot_tn(k[:, at], dsb), rows))
    dq = narrow(jnp.concatenate(dq_parts, axis=0).T)
    dk = jnp.concatenate(dk_parts, axis=1)
    dv = jnp.concatenate(dv_parts, axis=1)
    d_q[...] = narrow(dot_tn(h1[...], dq))
    d_k[...] = narrow(dot_tn(h1[...], dk))
    d_v[...] = narrow(dot_tn(h1[...], dv))
    into = dot_nt(dq, wq[...]) + dot_nt(dk, wk[...]) + dot_nt(dv, wv[...])
    back, gain_grad = rms_back(hidden[...].astype(F32), g1[...], into)
    dg1_out[...] = gain_grad
    hidden_out[...] = grad + back
    by_distance = jnp.concatenate(sums, axis=0)
    onehot = bucket_onehot_rows(table.shape[0], rows)
    dtable_out[...] = lax.dot_general(
        onehot, by_distance, (((1,), (1,)), ((), ())), precision=lax.Precision.HIGHEST, preferred_element_type=F32
    )


def add_rows(left, right, dest):
    count = dest.shape[0]

    def one(index, carry):
        dest[index] = narrow(left[index].astype(F32) + right[index].astype(F32))
        return carry

    lax.fori_loop(0, count, one, 0)


def reduce_kernel(n, singles, grouped, *refs):
    pieces = singles + grouped
    ins = list(refs[:singles]) + [refs[singles].at[:, i] for i in range(grouped)]
    small_in, out, small_out = refs[singles + 1 : singles + 4]
    bits = n.bit_length() - 1
    scratch = refs[singles + 4 :]
    mine, other, stages = scratch[0], scratch[1], scratch[2 : 2 + bits]
    local_sem, send_sem, recv_sem, small_buf, small_send, small_recv, last_sem = scratch[2 + bits : 9 + bits]
    half = pieces // 2
    me, core = lax.axis_index("pass"), lax.axis_index("pb")
    partner = (me, 1 - core)

    barrier = pltpu.get_barrier_semaphore()
    pl.semaphore_signal(barrier, inc=1, device_id=partner, device_id_type=MESH)
    for bit in range(bits):
        pl.semaphore_signal(barrier, inc=1, device_id=(me ^ (1 << bit), core), device_id_type=MESH)
    pl.semaphore_wait(barrier, bits + 1)

    def remote(src, dst, send, recv, device):
        return pltpu.make_async_remote_copy(
            src_ref=src, dst_ref=dst, send_sem=send, recv_sem=recv, device_id=device, device_id_type=MESH
        )

    def order(piece):
        first = list(range(bits))
        if piece % 2 and bits > 1:
            first[0], first[1] = first[1], first[0]
        return first

    def split(ref, piece, stage):
        done = order(piece)[:stage]
        bit = order(piece)[stage]
        low = 1 << len([b for b in range(bit) if b not in done])
        count = n >> stage
        view = ref.reshape(count // (2 * low), 2, low, ref.shape[-2], ref.shape[-1])
        return view, (me >> bit) & 1, low, count // (2 * low), bit

    def swap(i, c):
        return remote(ins[2 * i + 1 - c], other.at[i], send_sem.at[i, 0], recv_sem.at[i, 0], partner)

    def fetch(i, c):
        return pltpu.make_async_copy(ins[2 * i + c], mine.at[i], local_sem.at[i])

    for i in range(half):
        for c in range(2):

            @pl.when(core == c)
            def _(i=i, c=c):
                swap(i, c).start()
                fetch(i, c).start()

    def source(i, stage):
        return other.at[i] if stage == 0 else stages[stage - 1].at[i]

    def stage_copy(i, stage):
        view, value, low, high, bit = split(source(i, stage), i, stage)
        dst = stages[stage].at[i].reshape(high, low, *mine.shape[-2:])
        return remote(
            view.at[:, 1 - value], dst, send_sem.at[i, stage + 1], recv_sem.at[i, stage + 1], (me ^ (1 << bit), core)
        )

    def small_copy(stage):
        device = partner if stage == bits else (me ^ (1 << stage), core)
        return remote(small_buf.at[stage], small_buf.at[bits + 1 + stage], small_send.at[stage], small_recv.at[stage], device)

    small_buf[0] = small_in[...]
    small_copy(0).start()

    def last_copy(i):
        return remote(out_buf(i), out_buf2(i), last_sem.at[0, i], last_sem.at[1, i], partner)

    out_own, out_other = scratch[-2], scratch[-1]

    def out_buf(i):
        return out_own.at[i]

    def out_buf2(i):
        return out_other.at[i]

    for tick in range(half + bits + 1):
        for stage in reversed(range(bits + 1)):
            i = tick - stage
            if not 0 <= i < half:
                continue
            if stage == 0:
                for c in range(2):

                    @pl.when(core == c)
                    def _(i=i, c=c):
                        fetch(i, c).wait()

                swap(i, 0).wait_recv()
                add_rows(mine.at[i], other.at[i], other.at[i])
            else:
                copy = stage_copy(i, stage - 1)
                copy.wait_recv()
                view, value, low, high, bit = split(source(i, stage - 1), i, stage - 1)
                dst = stages[stage - 1].at[i]
                if stage < bits:
                    kept = view.at[:, value]

                    def one(index, carry, kept=kept, dst=dst, low=low):
                        dst[index] = narrow(kept[index // low, index % low].astype(F32) + dst[index].astype(F32))
                        return carry

                    lax.fori_loop(0, high * low, one, 0)
                else:
                    total = view[0, value, 0].astype(F32) + dst[0].astype(F32)
                    out_own[i] = narrow(total)
                    for c in range(2):

                        @pl.when(core == c)
                        def _(i=i, c=c, total=total):
                            out[2 * i + c] = total

            if stage < bits:
                stage_copy(i, stage).start()
            else:
                last_copy(i).start()
        if 1 <= tick <= bits + 1:
            stage = tick - 1
            small_copy(stage).wait_recv()
            total = small_buf[stage] + small_buf[bits + 1 + stage]
            if stage < bits:
                small_buf[stage + 1] = total
                small_copy(stage + 1).start()
            else:
                small_out[...] = total
    for i in range(half):
        last_copy(i).wait_recv()
        for c in range(2):

            @pl.when(core == c)
            def _(i=i, c=c):
                out[2 * i + 1 - c] = out_other[i].astype(F32)

    for i in range(half):
        swap(i, 0).wait_send()
        for stage in range(bits):
            stage_copy(i, stage).wait_send()
        last_copy(i).wait_send()
    for stage in range(bits + 1):
        small_copy(stage).wait_send()


def reduce_all(n, parts, group, small):
    pieces = len(parts) + group.shape[1]
    half = pieces // 2
    _, rows, width = parts[0].shape
    bits = n.bit_length() - 1
    stage_shapes = [pltpu.VMEM((half, n >> (s + 1), rows, width), BF) for s in range(bits)]
    return pl.pallas_call(
        functools.partial(reduce_kernel, n, len(parts), group.shape[1]),
        out_shape=(jax.ShapeDtypeStruct((pieces, rows, width), F32), jax.ShapeDtypeStruct(small.shape, F32)),
        in_specs=[pl.BlockSpec(memory_space=pl.ANY)] * (len(parts) + 1) + [pl.BlockSpec(memory_space=pltpu.VMEM)],
        out_specs=(pl.BlockSpec(memory_space=pltpu.VMEM), pl.BlockSpec(memory_space=pltpu.VMEM)),
        scratch_shapes=[pltpu.VMEM((half, n, rows, width), BF), pltpu.VMEM((half, n, rows, width), BF)]
        + stage_shapes
        + [
            pltpu.SemaphoreType.DMA((half,)),
            pltpu.SemaphoreType.DMA((half, bits + 1)),
            pltpu.SemaphoreType.DMA((half, bits + 1)),
            pltpu.VMEM((2 * (bits + 1),) + small.shape, F32),
            pltpu.SemaphoreType.DMA((bits + 1,)),
            pltpu.SemaphoreType.DMA((bits + 1,)),
            pltpu.SemaphoreType.DMA((2, half)),
            pltpu.VMEM((half, rows, width), BF),
            pltpu.VMEM((half, rows, width), BF),
        ],
        compiler_params=pltpu.CompilerParams(collective_id=0, has_side_effects=True, vmem_limit_bytes=VMEM_LIMIT),
    )(*parts, group, small)


def halving_order(bits, piece):
    first = list(range(bits))
    if piece % 2 and bits > 1:
        first[0], first[1] = first[1], first[0]
    return first


def drain_order(bits, early, pieces):
    free, waiting, steps, now = {0: 5.0, 1: 5.0, 2: 13.0}, [], [], 0.0

    def send(piece, stage, time):
        bit = halving_order(bits, piece)[stage]
        link = min(bit, 2)
        free[link] = max(time, free.get(link, 0.0)) + 1.0 / (1 << stage) + (0.1 if bit > 2 else 0.0)
        waiting.append((free[link] + 0.3, piece, stage))

    for piece in range(early):
        send(piece, 0, 0.0)
    first = early
    while waiting:
        waiting.sort()
        time, piece, stage = waiting.pop(0)
        now = max(now, time)
        steps.append(("arrive", piece, stage))
        if stage + 1 < bits:
            send(piece, stage + 1, now)
        first -= stage == 0
        if first == 0:
            first = pieces
            for piece in range(early, pieces):
                steps.append(("begin", piece, 0))
                send(piece, 0, now)
    for turn in range(bits):
        steps.insert((turn + 1) * len(steps) // (bits + 1), ("small", 0, 0))
    return steps


INPUTS = (
    "lengths", "encodings", "wq", "wk", "wv", "wo", "wcq", "wck", "wcv", "wco", "w_in", "w_out",
    "hidden", "cot", "g1", "g2", "g3", "table",
)
OUTPUTS = (
    "result_out", "hidden_out", "enc_out", "sq", "sk", "sv", "so", "cqo", "cko", "cvo", "coo", "fin", "fout",
    "gs", "gc", "gf", "table_out",
)
SCRATCH = (
    "L1", "L2", "R", "give", "own_late", "send_late", "encb", "kb", "vb", "eg", "wb", "masked", "gmasked", "dq_t",
    "q", "k", "v", "after_self", "grad_cross", "top", "lse", "delta", "swap_send", "swap_recv", "mine",
)
AFTER = (
    "last_own", "last_other", "small_g", "small_t", "load_sem", "pair_send", "pair_recv", "rs_send", "rs_recv",
    "in_send", "in_recv", "a2a_send", "a2a_recv", "a2a_own", "small_send", "small_recv", "last_send", "last_recv",
)
SQUARES = ("wq", "wk", "wv", "wo", "wcq", "wck", "wcv", "wco")


def layer_kernel(n, slot, count_in, count_out, *refs):
    bits = n.bit_length() - 1
    names = INPUTS + OUTPUTS + SCRATCH + tuple("s%d" % b for b in range(bits)) + AFTER
    r = dict(zip(names, refs, strict=True))
    lengths, table, hidden = r["lengths"], r["table"], r["hidden"]
    stages = [r["s%d" % b] for b in range(bits)]
    mine, wb, L1, L2 = r["mine"], r["wb"], r["L1"], r["L2"]
    pieces, _, share, half = mine.shape
    rows, width = hidden.shape
    units = count_out * width
    span = count_in * half
    pairs = width // (2 * HD)
    two = 2 * HD
    me, core = lax.axis_index("pass"), lax.axis_index("pb")
    partner = (me, 1 - core)
    gains = {name: r[name][...].reshape(1, width) for name in ("g1", "g2", "g3")}
    W = {name: wb.at[i] for i, name in enumerate(SQUARES)}

    def remote(src, dst, send, recv, device):
        return pltpu.make_async_remote_copy(
            src_ref=src, dst_ref=dst, send_sem=send, recv_sem=recv, device_id=device, device_id_type=MESH
        )

    parts = units // half
    loads = [(r[w], wb.at[i]) for i, w in enumerate(SQUARES)]
    tiles = [mine.at[i].reshape(width, half) for i in range(2 * parts)]
    for j in range(parts):
        loads.append((r["w_in"].at[:, j * half : (j + 1) * half], tiles[j]))
        for c in range(2):
            loads.append((
                r["w_out"].at[j * half : (j + 1) * half, c * half : (c + 1) * half],
                tiles[parts + j].at[c * half : (c + 1) * half],
            ))

    def load(i):
        return pltpu.make_async_copy(loads[i][0], loads[i][1], r["load_sem"].at[i])

    for i in range(len(SQUARES)):
        load(i).start()

    barrier = pltpu.get_barrier_semaphore()
    pl.semaphore_signal(barrier, inc=1, device_id=partner, device_id_type=MESH)

    def greet(d, carry):
        pl.semaphore_signal(barrier, inc=1, device_id=(me ^ d, core), device_id_type=MESH)
        return carry

    lax.fori_loop(1, n, greet, 0)
    pl.semaphore_wait(barrier, n)

    def passage_at(p):
        return pl.ds(pl.multiple_of(p * slot, slot), slot)

    def bring(q):
        return remote(r["encodings"].at[q], r["encb"].at[passage_at(me)], r["in_send"].at[q], r["in_recv"].at[me], (q, core))

    def arrived(p):
        return remote(r["encodings"].at[p], r["encb"].at[passage_at(p)], r["in_send"].at[p], r["in_recv"].at[p], (p, core))

    def bring_one(i, carry):
        bring(me ^ (n // 2 + i)).start()
        return carry

    lax.fori_loop(0, n // 2, bring_one, 0)
    quarter = n // 4

    def bring_near(i, carry):
        bring(me ^ (quarter + i)).start()
        return carry

    lax.fori_loop(0, quarter, bring_near, 0)

    def bring_rest(i, carry):
        bring(me ^ i).start()
        return carry

    lax.fori_loop(1, quarter, bring_rest, 0)
    own_passage = pltpu.make_async_copy(r["encodings"].at[me], r["encb"].at[passage_at(me)], r["a2a_own"].at[0])
    own_passage.start()
    for i in range(len(SQUARES), len(loads)):
        load(i).start()

    value = hidden[...].astype(F32)
    h1 = narrow(rms(value, gains["g1"]))
    L1[0, :, :width] = h1
    for i, name in enumerate(("q", "k", "v")):
        load(i).wait()
        r[name][...] = narrow(dot_nn(h1, wb[i]))
    bias = head_bias(table[...], rows)
    allowed = causal_mask(rows)

    def self_chances(pair):
        at = slice(pair * two, (pair + 1) * two)
        masked = pair_mask(r["q"][:, at])
        scores = dot_nt(r["k"][:, at], masked)
        both = jnp.concatenate([toeplitz(bias[2 * pair + i : 2 * pair + i + 1], rows) for i in range(2)], axis=1)
        scores = jnp.where(allowed, scores + both, NEG)
        raised = jnp.exp(scores - jnp.max(scores, axis=0, keepdims=True))
        return at, masked, raised / jnp.sum(raised, axis=0, keepdims=True)

    for pair in range(pairs):
        at, _, chances = self_chances(pair)
        r["dq_t"][at, :] = pair_diag(dot_tn(r["v"][:, at], narrow(chances)), rows)
    mix1 = narrow(r["dq_t"][...].T)
    L1[0, :, 2 * width :] = mix1
    load(3).wait()
    after_self = value + dot_nn(mix1, W["wo"][...])
    r["after_self"][...] = after_self
    h2 = narrow(rms(after_self, gains["g2"]))
    L1[0, :, width : 2 * width] = h2
    load(4).wait()
    cq = narrow(dot_nn(h2, W["wcq"][...]))
    for pair in range(pairs):
        r["masked"][pair] = pair_mask(cq[:, pair * two : (pair + 1) * two])
    r["top"][...] = jnp.full(r["top"].shape, NEG, F32)
    r["lse"][...] = jnp.zeros(r["lse"].shape, F32)
    r["dq_t"][...] = jnp.zeros(r["dq_t"].shape, F32)

    def pair_copy(i):
        src = (L1.at[0], L2.at[0], r["give"])[i]
        dst = (L1, L2, r["R"])[i].at[1]
        return remote(src, dst, r["pair_send"].at[i], r["pair_recv"].at[i], partner)

    pair_copy(0).start()

    place = lax.broadcasted_iota(jnp.int32, (slot, 2 * rows), 0)

    def spread(row):
        return jnp.concatenate(
            [jnp.broadcast_to(row[:, :rows], (HD, rows)), jnp.broadcast_to(row[:, rows:], (HD, rows))], axis=0
        )

    load(5).wait()
    load(6).wait()
    own_passage.wait()
    few = 2

    def forward_block(turn, carry):
        first = (turn ^ (me // few)) * few
        for i in range(few):

            @pl.when(first + i != me)
            def _(i=i):
                arrived(first + i).wait_recv()

        at = pl.ds(pl.multiple_of(first * slot, few * slot), few * slot)
        source = r["encb"][at]
        r["kb"][at] = narrow(dot_nn(source, W["wck"][...]))
        r["vb"][at] = narrow(dot_nn(source, W["wcv"][...]))
        valid = jnp.concatenate([place < lengths[first + i] for i in range(few)], axis=0)
        for pair in range(pairs):
            cols = slice(pair * two, (pair + 1) * two)
            scores = jnp.where(valid, dot_nt(r["kb"][at, cols], r["masked"][pair]), NEG)
            before = r["top"][pair : pair + 1]
            now = jnp.maximum(before, jnp.max(scores, axis=0, keepdims=True))
            r["top"][pair : pair + 1] = now
            fade = jnp.exp(before - now)
            raised = jnp.exp(scores - now)
            r["lse"][pair : pair + 1] = r["lse"][pair : pair + 1] * fade + jnp.sum(raised, axis=0, keepdims=True)
            part = pair_diag(dot_tn(r["vb"][at, cols], narrow(raised)), rows)
            r["dq_t"][cols, :] = r["dq_t"][cols, :] * spread(fade) + part
        return carry

    lax.fori_loop(0, n // few, forward_block, 0)
    for pair in range(pairs):
        cols = slice(pair * two, (pair + 1) * two)
        sums = r["lse"][pair : pair + 1]
        r["lse"][pair : pair + 1] = r["top"][pair : pair + 1] + jnp.log(sums)
        r["dq_t"][cols, :] = r["dq_t"][cols, :] * spread(1.0 / sums)

    mix2 = narrow(r["dq_t"][...].T)
    L2[0, :, units + width :] = mix2
    load(7).wait()
    after_cross = r["after_self"][...] + dot_nn(mix2, W["wco"][...])
    h3 = narrow(rms(after_cross, gains["g3"]))
    L2[0, :, units : units + width] = h3
    cb = r["cot"][...]
    outs = [after_cross[:, c * half : (c + 1) * half] for c in range(2)]
    into = jnp.zeros((rows, width), F32)
    for j in range(parts):
        for i in range(3):
            load(len(SQUARES) + 3 * j + i).wait()
        inner = dot_nn(h3, tiles[j][...])
        bent = jnp.tanh(ROOT * (inner + 0.044715 * (inner * inner * inner)))
        active = narrow(0.5 * inner * (1.0 + bent))
        L2[0, :, j * half : (j + 1) * half] = active
        slope = 0.5 * (1.0 + bent) + (0.5 * ROOT) * inner * (1.0 - bent * bent) * (1.0 + (3 * 0.044715) * inner * inner)
        back = jnp.zeros((rows, half), F32)
        for c in range(2):
            tile = tiles[parts + j][c * half : (c + 1) * half]
            outs[c] = outs[c] + dot_nn(active, tile)
            back = back + dot_nt(cb[:, c * half : (c + 1) * half], tile)
        gi = narrow(back * slope)
        to = j % count_in
        c = j // count_in

        @pl.when(core == c)
        def _(gi=gi, to=to):
            r["R"][0, :, to * half : (to + 1) * half] = gi

        @pl.when(core != c)
        def _(gi=gi, to=to):
            r["give"][:, to * half : (to + 1) * half] = gi

        into = into + dot_nt(gi, tiles[j][...])
    pair_copy(1).start()
    for c in range(2):
        r["result_out"][:, c * half : (c + 1) * half] = outs[c]
    back, dg3 = rms_back(after_cross, gains["g3"], into)
    grad = cb.astype(F32) + back
    r["grad_cross"][...] = grad
    gb = narrow(grad)
    for c in range(2):
        for j, value in enumerate((cb, gb)):
            part = value[:, c * half : (c + 1) * half]

            @pl.when(core == c)
            def _(part=part, j=j):
                r["R"][0, :, span + j * half : span + (j + 1) * half] = part

            @pl.when(core != c)
            def _(part=part, j=j):
                r["give"][:, span + j * half : span + (j + 1) * half] = part

    pair_copy(2).start()
    gmix = narrow(dot_nt(gb, W["wco"][...]))
    product = gmix.astype(F32).T * r["dq_t"][...]
    for pair in range(pairs):
        at = slice(pair * two, (pair + 1) * two)
        r["gmasked"][pair] = pair_mask(gmix[:, at])
        part = product[at]
        r["delta"][pair : pair + 1] = jnp.concatenate(
            [jnp.sum(part[:HD], axis=0, keepdims=True), jnp.sum(part[HD:], axis=0, keepdims=True)], axis=1
        )
    r["dq_t"][...] = jnp.zeros(r["dq_t"].shape, F32)
    group = 4
    blocks = n // group
    block = group * slot

    def send_back(passage, wait):
        at = passage_at(passage)
        away = remote(r["eg"].at[at], r["enc_out"].at[me], r["a2a_send"].at[passage], r["a2a_recv"].at[me], (passage, core))
        stay = pltpu.make_async_copy(r["eg"].at[at], r["enc_out"].at[me], r["a2a_own"].at[0])

        @pl.when(passage != me)
        def _():
            away.wait_send() if wait else away.start()

        @pl.when(passage == me)
        def _():
            stay.wait() if wait else stay.start()

    def cross_block(turn, carry):
        first = (blocks - 1 - turn) ^ (me // group)
        at = pl.ds(pl.multiple_of(first * block, block), block)
        valid = jnp.concatenate([place < lengths[first * group + i] for i in range(group)], axis=0)
        for pair in range(pairs):
            cols = slice(pair * two, (pair + 1) * two)
            key, value = r["kb"][at, cols], r["vb"][at, cols]
            scores = jnp.where(valid, dot_nt(key, r["masked"][pair]), NEG)
            chances = jnp.exp(scores - r["lse"][pair : pair + 1])
            ds = narrow(chances * (dot_nt(value, r["gmasked"][pair]) - r["delta"][pair : pair + 1]))
            r["vb"][at, cols] = narrow(dot_nn(narrow(chances), r["gmasked"][pair]))
            r["dq_t"][cols, :] = r["dq_t"][cols, :] + pair_diag(dot_tn(key, ds), rows)
            r["kb"][at, cols] = narrow(dot_nn(ds, r["masked"][pair]))
        r["eg"][at] = narrow(dot_nt(r["kb"][at], W["wck"][...]) + dot_nt(r["vb"][at], W["wcv"][...]))
        for i in range(group):
            send_back(first * group + i, False)
        return carry

    def split(ref, piece, stage):
        done = halving_order(bits, piece)[:stage]
        bit = halving_order(bits, piece)[stage]
        low = 1 << len([b for b in range(bit) if b not in done])
        high = (n >> stage) // (2 * low)
        return ref.reshape(high, 2, low, share, half), (me >> bit) & 1, low, high, bit

    def source(piece, stage):
        return mine.at[piece] if stage == 0 else stages[stage - 1].at[piece]

    def stage_copy(piece, stage):
        view, value, low, high, bit = split(source(piece, stage), piece, stage)
        dst = stages[stage].at[piece].reshape(high, low, share, half)
        sems = r["rs_send"].at[piece, stage], r["rs_recv"].at[piece, stage]
        return remote(view.at[:, 1 - value], dst, *sems, (me ^ (1 << bit), core))

    squares = ("sq", "sk", "sv", "so", "cqo", "cko", "cvo", "coo")
    order = ["in"] * count_in + ["out"] * count_out + ["coo", "cko", "cvo", "cqo", "so", "sq", "sk", "sv"]
    index = {name: order.index(name) for name in squares}

    def put(piece, c, total):
        name = order[piece]
        if name == "in":
            r["fin"][:, c * count_in * half + piece * half : c * count_in * half + (piece + 1) * half] = total
        elif name == "out":
            k = piece - count_in
            r["fout"][k * share : (k + 1) * share, c * half : (c + 1) * half] = total
        else:
            r[name][:, c * half : (c + 1) * half] = total

    def last_copy(piece):
        sems = r["last_send"].at[piece], r["last_recv"].at[piece]
        return remote(r["last_own"].at[piece], r["last_other"].at[piece], *sems, partner)

    def arrive(piece, stage):
        stage_copy(piece, stage).wait_recv()
        view, value, low, high, bit = split(source(piece, stage), piece, stage)
        kept = view.at[:, value]
        dst = stages[stage].at[piece]
        if stage + 1 < bits:

            def one(i, carry):
                dst[i] = narrow(kept[i // low, i % low].astype(F32) + dst[i].astype(F32))
                return carry

            lax.fori_loop(0, high * low, one, 0)
            stage_copy(piece, stage + 1).start()
        else:
            total = kept[0, 0].astype(F32) + dst[0].astype(F32)
            r["last_own"][piece] = narrow(total)
            last_copy(piece).start()
            for c in range(2):

                @pl.when(core == c)
                def _(c=c):
                    put(piece, c, total)

    def begin(piece):
        stage_copy(piece, 0).start()

    lax.fori_loop(0, blocks, cross_block, 0)

    for i in range(3):
        pair_copy(i).wait_recv()
    F1, F2, FR = (r[x].reshape(2 * rows, r[x].shape[2]) for x in ("L1", "L2", "R"))

    def owners(value):
        return narrow(value).reshape(n, share, half)

    for piece in range(count_in):
        mine[piece] = owners(dot_tn(F2[:, units : units + width], FR[:, piece * half : (piece + 1) * half]))
        begin(piece)
    per = width // (count_out * share)
    for part in range(count_out):
        value = narrow(dot_tn(F2[:, part * width : (part + 1) * width], FR[:, span : span + half]))
        value = value.reshape(per, count_out, share, half)
        for k in range(count_out):
            mine[count_in + k, part * per : (part + 1) * per] = value[:, k]
    for k in range(count_out):
        begin(count_in + k)
    mine[index["coo"]] = owners(dot_tn(F2[:, units + width :], FR[:, span + half :]))
    begin(index["coo"])

    late_names = ("cqo", "so", "sq", "sk", "sv")
    lefts = {"cqo": width, "so": 2 * width, "sq": 0, "sk": 0, "sv": 0}

    def late_copy(i):
        return remote(
            r["send_late"].at[i], r["own_late"].at[i, 1], r["pair_send"].at[3 + i], r["pair_recv"].at[3 + i], partner
        )

    def late_give(name, value):
        i = late_names.index(name)
        for c in range(2):

            @pl.when(core == c)
            def _(c=c):
                r["own_late"][i, 0] = value[:, c * half : (c + 1) * half]
                r["send_late"][i] = value[:, (1 - c) * half : (2 - c) * half]

        late_copy(i).start()

    def late_take(name):
        i = late_names.index(name)
        late_copy(i).wait_recv()
        left = F1[:, lefts[name] : lefts[name] + width]
        mine[index[name]] = owners(dot_tn(left, r["own_late"].at[i].reshape(2 * rows, half)[...]))

    dcq = narrow(r["dq_t"][...].T)
    late_give("cqo", dcq)


    def swap_copy(i):
        return remote(
            r["swap_send"].at[i], r["swap_recv"].at[i], r["pair_send"].at[8 + i], r["pair_recv"].at[8 + i], partner
        )

    for i, (name, ref) in enumerate((("cko", r["kb"]), ("cvo", r["vb"]))):
        for c in range(2):
            part = owners(dot_tn(r["encb"][...], ref[:, c * half : (c + 1) * half]))

            @pl.when(core == c)
            def _(part=part):
                mine[index[name]] = part

            @pl.when(core != c)
            def _(part=part):
                r["swap_send"][i] = part

        swap_copy(i).start()

    back, dg2 = rms_back(r["after_self"][...], gains["g2"], dot_nt(dcq, W["wcq"][...]))
    grad = r["grad_cross"][...] + back
    sb = narrow(grad)
    late_give("so", sb)
    late_take("cqo")
    for i, name in enumerate(("cko", "cvo")):
        swap_copy(i).wait_recv()

        def one(o, carry, i=i, name=name):
            to = mine.at[index[name]]
            to[o] = narrow(to[o].astype(F32) + r["swap_recv"][i, o].astype(F32))
            return carry

        lax.fori_loop(0, n, one, 0)

    gself = narrow(dot_nt(sb, W["wo"][...]))
    dq_parts, dk_parts, dv_parts, sums = [], [], [], []
    for pair in range(pairs):
        at, masked, chances = self_chances(pair)
        gmasked = pair_mask(gself[:, at])
        dv_parts.append(narrow(dot_nn(narrow(chances), gmasked)))
        dp = dot_nt(r["v"][:, at], gmasked)
        ds = chances * (dp - jnp.sum(chances * dp, axis=0, keepdims=True))
        sums.append(diagonal_sums(ds[:, :rows]))
        sums.append(diagonal_sums(ds[:, rows:]))
        dsb = narrow(ds)
        dk_parts.append(narrow(dot_nn(dsb, masked)))
        dq_parts.append(pair_diag(dot_tn(r["k"][:, at], dsb), rows))
    dq = narrow(jnp.concatenate(dq_parts, axis=0).T)
    dk = jnp.concatenate(dk_parts, axis=1)
    dv = jnp.concatenate(dv_parts, axis=1)
    late_give("sq", dq)
    late_give("sk", dk)
    late_give("sv", dv)
    late_take("so")
    into = dot_nt(dq, W["wq"][...]) + dot_nt(dk, W["wk"][...]) + dot_nt(dv, W["wv"][...])
    late_take("sq")
    late_take("sk")
    late_take("sv")
    back, dg1 = rms_back(hidden[...].astype(F32), gains["g1"], into)
    r["hidden_out"][...] = grad + back
    onehot = bucket_onehot_rows(table.shape[1], rows)
    dtable = lax.dot_general(
        jnp.concatenate(sums, axis=0), onehot, (((1,), (1,)), ((), ())), precision=lax.Precision.HIGHEST,
        preferred_element_type=F32,
    )

    small_g, small_t = r["small_g"], r["small_t"]

    def small_copies(step):
        device = partner if step == bits else (me ^ (1 << step), core)
        return [
            remote(ref.at[step], ref.at[bits + 1 + step], r["small_send"].at[j, step], r["small_recv"].at[j, step], device)
            for j, ref in enumerate((small_g, small_t))
        ]

    small_g[0] = jnp.concatenate([dg1, dg2, dg3, jnp.zeros((5, width), F32)], axis=0)
    small_t[0] = jnp.zeros(small_t.shape[1:], F32)
    small_t[0, : table.shape[0], : table.shape[1]] = dtable
    for copy in small_copies(0):
        copy.start()

    def small_step(step):
        for copy in small_copies(step):
            copy.wait_recv()
        for ref in (small_g, small_t):
            total = ref[step] + ref[bits + 1 + step]
            if step < bits:
                ref[step + 1] = total
            elif ref is small_t:
                r["table_out"][...] = total[: table.shape[0], : table.shape[1]]
            else:
                for j, name in enumerate(("gs", "gc", "gf")):
                    own = jnp.zeros((1, share), F32)
                    for o in range(n):
                        own = jnp.where(me == o, total[j : j + 1, o * share : (o + 1) * share], own)
                    r[name][...] = own
        if step < bits:
            for copy in small_copies(step + 1):
                copy.start()

    early = count_in + count_out + 1
    step = 0
    for kind, piece, stage in drain_order(bits, early, pieces):
        if kind == "begin":
            begin(piece)
        elif kind == "arrive":
            arrive(piece, stage)
        elif step <= bits:
            small_step(step)
            step += 1
    for left in range(step, bits + 1):
        small_step(left)
    for piece in range(pieces):
        last_copy(piece).wait_recv()
        total = r["last_other"][piece].astype(F32)
        for c in range(2):

            @pl.when(core != c)
            def _(c=c, total=total, piece=piece):
                put(piece, c, total)

    def others(d, carry):
        q = me ^ d
        remote(r["eg"].at[pl.ds(0, slot)], r["enc_out"].at[q], r["a2a_send"].at[q], r["a2a_recv"].at[q], (q, core)).wait_recv()
        return carry

    lax.fori_loop(1, n, others, 0)

    def sent(p, carry):
        send_back(p, True)
        return carry

    lax.fori_loop(0, n, sent, 0)

    def brought(d, carry):
        bring(me ^ d).wait_send()
        return carry

    lax.fori_loop(1, n, brought, 0)
    for i in range(3):
        pair_copy(i).wait_send()
    for i in range(5):
        late_copy(i).wait_send()
    for i in range(2):
        swap_copy(i).wait_send()
    for piece in range(pieces):
        for stage in range(bits):
            stage_copy(piece, stage).wait_send()
        last_copy(piece).wait_send()
    for step in range(bits + 1):
        for copy in small_copies(step):
            copy.wait_send()


def layer(n, slot, args):
    rows, width = args["hidden"].shape
    units = args["w_in"].shape[1]
    share, half = width // n, width // 2
    bits = n.bit_length() - 1
    pairs = width // (2 * HD)
    keys = n * slot
    count_in = count_out = units // width
    pieces = 8 + count_in + count_out
    table = args["table"].shape
    in_hbm = ("encodings", "w_in", "w_out") + SQUARES
    vmem = pl.BlockSpec(memory_space=pltpu.VMEM)
    anyw = pl.BlockSpec(memory_space=pl.ANY)
    in_specs = [pl.BlockSpec(memory_space=pltpu.SMEM)] + [anyw if name in in_hbm else vmem for name in INPUTS[1:]]
    wide = jax.ShapeDtypeStruct((rows, width), F32)
    square = jax.ShapeDtypeStruct((share, width), F32)
    gain = jax.ShapeDtypeStruct((1, share), F32)
    outs = [wide, wide, jax.ShapeDtypeStruct((n, slot, width), BF)] + [square] * 8
    outs += [jax.ShapeDtypeStruct((share, units), F32), jax.ShapeDtypeStruct((count_out * share, width), F32)]
    outs += [gain] * 3 + [jax.ShapeDtypeStruct(table, F32)]
    out_specs = [vmem, vmem, anyw] + [vmem] * 14
    dma = pltpu.SemaphoreType.DMA
    sixteen, full = pltpu.VMEM((rows, width), BF), pltpu.VMEM((rows, width), F32)
    stat, masks = pltpu.VMEM((pairs, 2 * rows), F32), pltpu.VMEM((pairs, 2 * rows, 2 * HD), BF)
    scratch = [
        pltpu.VMEM((2, rows, 3 * width), BF),
        pltpu.VMEM((2, rows, units + 2 * width), BF),
        pltpu.VMEM((2, rows, units // 2 + width), BF),
        pltpu.VMEM((rows, units // 2 + width), BF),
        pltpu.VMEM((5, 2, rows, half), BF),
        pltpu.VMEM((5, rows, half), BF),
    ]
    scratch += [pltpu.VMEM((keys, width), BF)] * 4
    scratch += [pltpu.VMEM((8, width, width), BF), masks, masks, pltpu.VMEM((width, rows), F32)]
    scratch += [sixteen] * 3 + [full] * 2 + [stat] * 3
    scratch += [
        pltpu.VMEM((2, n, share, half), BF),
        pltpu.VMEM((2, n, share, half), BF),
        pltpu.VMEM((pieces, n, share, half), BF),
    ]
    scratch += [pltpu.VMEM((pieces, n >> (b + 1), share, half), BF) for b in range(bits)]
    scratch += [
        pltpu.VMEM((pieces, share, half), BF),
        pltpu.VMEM((pieces, share, half), BF),
        pltpu.VMEM((2 * (bits + 1), 8, width), F32),
        pltpu.VMEM((2 * (bits + 1), -(-table[0] // 8) * 8, 128), F32),
        dma((8 + 3 * (units // half),)),
        dma((10,)),
        dma((10,)),
        dma((pieces, bits)),
        dma((pieces, bits)),
        dma((n,)),
        dma((n,)),
        dma((n,)),
        dma((n,)),
        dma((1,)),
        dma((2, bits + 1)),
        dma((2, bits + 1)),
        dma((pieces,)),
        dma((pieces,)),
    ]
    return pl.pallas_call(
        functools.partial(layer_kernel, n, slot, count_in, count_out),
        out_shape=tuple(outs),
        in_specs=in_specs,
        out_specs=tuple(out_specs),
        scratch_shapes=scratch,
        compiler_params=pltpu.CompilerParams(collective_id=1, has_side_effects=True, vmem_limit_bytes=LAYER_LIMIT),
    )(*[args[name] for name in INPUTS])


def finish_kernel(count, *refs):
    ins, outs, held, sems = refs[:count], refs[count : 2 * count], refs[2 * count : 3 * count], refs[-1]
    into = [pltpu.make_async_copy(ins[i], held[i], sems.at[0, i]) for i in range(count)]
    back = [pltpu.make_async_copy(held[i], outs[i], sems.at[1, i]) for i in range(count)]
    for copy in into:
        copy.start()
    for i in range(count):
        into[i].wait()
        back[i].start()
    for copy in back:
        copy.wait()


def finish(arrays):
    count = len(arrays)
    spec = pl.BlockSpec(memory_space=pl.ANY)
    return pl.pallas_call(
        functools.partial(finish_kernel, count),
        out_shape=tuple(jax.ShapeDtypeStruct(a.shape, a.dtype) for a in arrays),
        in_specs=[spec] * count,
        out_specs=(spec,) * count,
        scratch_shapes=[pltpu.VMEM(a.shape, a.dtype) for a in arrays] + [pltpu.SemaphoreType.DMA((2, count))],
        compiler_params=pltpu.CompilerParams(vmem_limit_bytes=VMEM_LIMIT),
    )(*arrays)


def whole(shape=None):
    return pl.BlockSpec(memory_space=pltpu.VMEM)


def call(kernel, outs, *args):
    return pl.pallas_call(
        kernel,
        out_shape=tuple(jax.ShapeDtypeStruct(shape, kind) for shape, kind in outs),
        in_specs=[whole()] * len(args),
        out_specs=tuple(whole() for _ in outs),
        compiler_params=pltpu.CompilerParams(vmem_limit_bytes=VMEM_LIMIT),
    )(*args)


def per_device(
    n, hidden, encodings, lengths, cotangent, wq, wk, wv, wo, wcq, wck, wcv, wco, w_in, w_out,
    gain_self, gain_cross, gain_feed, table,
):
    rows, width = hidden.shape[2], hidden.shape[3]
    slot = encodings.shape[3]
    passages = lengths.shape[2]
    units = w_in.shape[1]
    pairs = width // (2 * HD)
    keys = passages * slot
    own = hidden.reshape(rows, width)
    cot = cotangent.reshape(rows, width)
    g1, g2, g3 = (gain.reshape(1, width) for gain in (gain_self, gain_cross, gain_feed))
    length_row = lengths.reshape(passages)
    share = width // n
    fits = passages == n and keys * width * 8 <= 16 << 20 and units == 4 * width
    if n & (n - 1) == 0 and n >= 4 and share % 16 == 0 and fits:
        out = layer(n, slot, dict(
            lengths=length_row, encodings=encodings.reshape(n, slot, width), wq=wq, wk=wk, wv=wv, wo=wo, wcq=wcq, wck=wck,
            wcv=wcv, wco=wco, w_in=w_in, w_out=w_out, hidden=own, cot=cot, g1=gain_self, g2=gain_cross,
            g3=gain_feed, table=table.T,
        ))
        out = finish(out)
        rows_out = tuple(o.reshape(hidden.shape) for o in out[:2])
        gains = tuple(gain.reshape(share) for gain in out[13:16])
        return rows_out + (out[2].reshape(encodings.shape),) + tuple(out[3:13]) + gains + (out[16].T,)

    source = lax.all_to_all(encodings, "pass", split_axis=2, concat_axis=0, tiled=True).reshape(keys, width)

    sixteen, wide = ((rows, width), BF), ((rows, width), F32)
    h1, q, k, v, mix1, after_self, h2, cq = call(
        self_forward_kernel,
        [sixteen] * 5 + [wide, sixteen, sixteen],
        own, wq, wk, wv, wo, wcq, g1, g2, table,
    )

    block = 4 * slot
    steps = keys // block
    stats = jax.ShapeDtypeStruct((pairs, 2 * rows), F32)
    smem = pl.BlockSpec(memory_space=pltpu.SMEM)
    tile = pl.BlockSpec((block, width), lambda i: (i, 0))
    square = pl.BlockSpec((width, width), lambda i: (0, 0))
    query = pl.BlockSpec((rows, width), lambda i: (0, 0))
    stat = pl.BlockSpec((pairs, 2 * rows), lambda i: (0, 0))
    ck, cv, mix_t, lse = pl.pallas_call(
        functools.partial(cross_forward_kernel, slot),
        grid=(steps,),
        out_shape=(
            jax.ShapeDtypeStruct((keys, width), BF),
            jax.ShapeDtypeStruct((keys, width), BF),
            jax.ShapeDtypeStruct((width, rows), F32),
            stats,
        ),
        in_specs=[smem, tile, square, square, query],
        out_specs=(tile, tile, pl.BlockSpec((width, rows), lambda i: (0, 0)), stat),
        scratch_shapes=[
            pltpu.VMEM((pairs, 2 * rows, 2 * HD), BF),
            pltpu.VMEM((pairs, 2 * rows), F32),
            pltpu.VMEM((pairs, 2 * rows), F32),
            pltpu.VMEM((width, rows), F32),
        ],
        compiler_params=pltpu.CompilerParams(vmem_limit_bytes=VMEM_LIMIT),
    )(length_row, source, wck, wcv, cq)

    pieces = units // width
    result, grad_cross, gmix, delta, dg3, d_in, d_out, d_co = call(
        feed_kernel,
        [wide, wide, sixteen, ((pairs, 2 * rows), F32), ((1, width), F32), ((pieces, width, width), BF),
         ((units, width), BF), ((width, width), BF)],
        mix_t, after_self, cot, wco, w_in, w_out, g3,
    )

    enc_grad, dcq, d_ck, d_cv = pl.pallas_call(
        functools.partial(cross_backward_kernel, slot),
        grid=(steps,),
        out_shape=(
            jax.ShapeDtypeStruct((keys, width), BF),
            jax.ShapeDtypeStruct((rows, width), BF),
            jax.ShapeDtypeStruct((width, width), BF),
            jax.ShapeDtypeStruct((width, width), BF),
        ),
        in_specs=[smem, tile, tile, tile, square, square, query, query, stat, stat],
        out_specs=(tile, query, square, square),
        scratch_shapes=[
            pltpu.VMEM((pairs, 2 * rows, 2 * HD), BF),
            pltpu.VMEM((pairs, 2 * rows, 2 * HD), BF),
            pltpu.VMEM((width, rows), F32),
            pltpu.VMEM((block, 2 * width), BF),
            pltpu.VMEM((width, 2 * width), F32),
        ],
        compiler_params=pltpu.CompilerParams(vmem_limit_bytes=VMEM_LIMIT),
    )(length_row, source, ck, cv, wck, wcv, cq, gmix, lse, delta)
    returned = lax.all_to_all(
        enc_grad.reshape(passages, 1, 1, slot, width), "pass", split_axis=0, concat_axis=2, tiled=True
    )

    gain_kind = ((1, width), F32)
    squared = ((width, width), BF)
    hidden_grad, d_cq, d_so, d_q, d_k, d_v, dg1, dg2, dtable = call(
        self_backward_kernel,
        [wide] + [squared] * 5 + [gain_kind, gain_kind, (table.shape, F32)],
        own, h1, q, k, v, mix1, after_self, h2, dcq, grad_cross, wq, wk, wv, wo, wcq, g1, g2, table,
    )

    if n & (n - 1) == 0 and share % 16 == 0:
        squares = [d_q, d_k, d_v, d_so, d_cq, d_ck, d_cv, d_co]
        parts = [d.reshape(n, share, width) for d in squares]
        parts += [d_in[i].reshape(n, share, width) for i in range(pieces)]
        big = d_out.reshape(n, pieces, share, width)
        flat = jnp.concatenate([dg1, dg2, dg3, jnp.pad(dtable.reshape(1, -1), ((0, 0), (0, width - dtable.size))),
                                jnp.zeros((4, width), F32)], axis=0)
        sums, small = reduce_all(n, parts, big, flat)
        totals = [sums[i] for i in range(8)]
        count = len(squares)
        in_total = jnp.concatenate([sums[count + i] for i in range(pieces)], axis=1)
        out_total = sums[count + pieces :].reshape(pieces * share, width)
        me = lax.axis_index("pass")
        gains = [lax.dynamic_slice(small[i], (me * share,), (share,)) for i in range(3)]
        table_sum = small[3, : dtable.size].reshape(table.shape)
    else:
        both = [d_q, d_k, d_v, d_so, d_cq, d_ck, d_cv, d_co, d_in.transpose(1, 0, 2).reshape(width, units), d_out]

        def total(part):
            shared = lax.psum_scatter(part, "pass", scatter_dimension=0, tiled=True)
            return lax.psum(shared.astype(BF), "pb").astype(F32)

        sums = [total(part.astype(F32)) for part in both]
        totals, in_total, out_total = sums[:8], sums[8], sums[9]
        gains = [total(part.reshape(width)) for part in (dg1, dg2, dg3)]
        table_sum = lax.psum(dtable, ("pass", "pb"))
    return (
        (result.reshape(hidden.shape), hidden_grad.reshape(hidden.shape), returned)
        + tuple(totals)
        + (in_total, out_total)
        + tuple(gains)
        + (table_sum,)
    )


def solution(mesh):
    rows = P("pb", "pass", None, None)
    passage = P("pass", "pb", None, None, None)
    in_specs = (rows, passage, P("pb", "pass", None), rows) + (P(),) * 14
    out_specs = (rows, rows, passage) + (P("pass", None),) * 10 + (P("pass"),) * 3 + (P(),)
    return jax.shard_map(
        functools.partial(per_device, mesh.shape["pass"]),
        mesh=mesh,
        in_specs=in_specs,
        out_specs=out_specs,
        check_vma=False,
    )
```

```python
import functools
from typing import Any, NamedTuple

import jax
import jax.numpy as jnp
from jax import lax
from jax.experimental import pallas as pl
from jax.experimental.pallas import tpu as pltpu
from jax.sharding import PartitionSpec as P

HD = 64
EPS = 1e-06
LIMITS = (19, 21, 24, 27, 31, 35, 40, 46, 52, 59, 67, 77, 87, 99, 113)
NEG = -1e30
BF = jnp.bfloat16
F32 = jnp.float32
MESH = pl.DeviceIdType.MESH
PASS, CORE = "pass", "pb"
PLANES_FIRST = (2, 3, 6, 7, 11)
ROOT = 0.7978845608028654
VMEM_LIMIT = 56 << 20
LAYER_LIMIT = 64 << 20


def narrow(value):
    return value.astype(BF)


def dot_nn(left, right):
    return lax.dot_general(left, right, (((1,), (0,)), ((), ())), preferred_element_type=F32)


def dot_nt(left, right):
    return lax.dot_general(left, right, (((1,), (1,)), ((), ())), preferred_element_type=F32)


def dot_tn(left, right):
    return lax.dot_general(left, right, (((0,), (0,)), ((), ())), preferred_element_type=F32)


def rms(value, gain):
    scale = lax.rsqrt(jnp.mean(value * value, axis=-1, keepdims=True) + EPS)
    return value * scale * gain


def rms_back(value, gain, grad):
    scale = lax.rsqrt(jnp.mean(value * value, axis=-1, keepdims=True) + EPS)
    scaled = grad * gain
    inner = jnp.mean(scaled * value, axis=-1, keepdims=True)
    rows = scaled * scale - value * (scale * scale * scale * inner)
    gain_grad = jnp.sum(grad * (value * scale), axis=0, keepdims=True)
    return rows, gain_grad


def pair_mask(pair):
    lane = lax.broadcasted_iota(jnp.int32, pair.shape, 1)
    zero = jnp.zeros_like(pair)
    return jnp.concatenate(
        [jnp.where(lane < HD, pair, zero), jnp.where(lane >= HD, pair, zero)], axis=0
    )


def pair_diag(both, rows):
    return jnp.concatenate([both[:HD, :rows], both[HD:, rows:]], axis=0)


def bucket_onehot_rows(buckets, length):
    distance = lax.broadcasted_iota(jnp.int32, (buckets, length), 1)
    row = lax.broadcasted_iota(jnp.int32, (buckets, length), 0)
    beyond = jnp.zeros_like(distance)
    for edge in LIMITS:
        beyond = beyond + (distance >= edge).astype(jnp.int32)
    bucket = jnp.where(distance < 16, distance, 16 + beyond)
    return (bucket == row).astype(F32)


def head_bias(table, rows):
    onehot = bucket_onehot_rows(table.shape[1], rows)
    return lax.dot_general(
        table, onehot, (((1,), (0,)), ((), ())), precision=lax.Precision.HIGHEST,
        preferred_element_type=F32,
    )


def toeplitz(row, rows):
    return pltpu.roll(jnp.broadcast_to(row, (rows, rows)), 0, 1, stride=1, stride_axis=0)


def diagonal_sums(square):
    rows = square.shape[0]
    place = lax.broadcasted_iota(jnp.int32, square.shape, 0)
    for bit in range(3):
        moved = pltpu.roll(square, rows - (1 << bit), 1)
        square = jnp.where((place >> bit) & 1 == 1, moved, square)
    total = square[:8]
    for group in range(1, rows // 8):
        total = total + pltpu.roll(square[8 * group : 8 * group + 8], rows - 8 * group, 1)
    return jnp.sum(total, axis=0, keepdims=True)


def causal_mask(rows):
    key = lax.broadcasted_iota(jnp.int32, (rows, 2 * rows), 0)
    query = lax.broadcasted_iota(jnp.int32, (rows, 2 * rows), 1)
    query = jnp.where(query >= rows, query - rows, query)
    return key <= query


def self_forward_kernel(
    hidden, wq, wk, wv, wo, wcq, g1, g2, table,
    h1_out, q_out, k_out, v_out, mix_out, after_out, h2_out, cq_out,
):
    rows, width = hidden.shape
    pairs = width // (2 * HD)
    value = hidden[...].astype(F32)
    h1 = narrow(rms(value, g1[...]))
    h1_out[...] = h1
    q = narrow(dot_nn(h1, wq[...]))
    k = narrow(dot_nn(h1, wk[...]))
    v = narrow(dot_nn(h1, wv[...]))
    q_out[...] = q
    k_out[...] = k
    v_out[...] = v
    bias = head_bias(table[...].T, rows)
    allowed = causal_mask(rows)
    mixed = []
    for pair in range(pairs):
        at = slice(pair * 2 * HD, (pair + 1) * 2 * HD)
        scores = dot_nt(k[:, at], pair_mask(q[:, at]))
        both = jnp.concatenate(
            [toeplitz(bias[2 * pair : 2 * pair + 1], rows), toeplitz(bias[2 * pair + 1 : 2 * pair + 2], rows)],
            axis=1,
        )
        scores = jnp.where(allowed, scores + both, NEG)
        top = jnp.max(scores, axis=0, keepdims=True)
        raised = jnp.exp(scores - top)
        chances = raised / jnp.sum(raised, axis=0, keepdims=True)
        mixed.append(pair_diag(dot_tn(v[:, at], narrow(chances)), rows))
    mix = narrow(jnp.concatenate(mixed, axis=0).T)
    mix_out[...] = mix
    after = value + dot_nn(mix, wo[...])
    after_out[...] = after
    h2 = narrow(rms(after, g2[...]))
    h2_out[...] = h2
    cq_out[...] = narrow(dot_nn(h2, wcq[...]))


def cross_forward_kernel(slot, lengths, enc, wk, wv, cq, k_out, v_out, mix_out, lse_out, masked, top, total, acc):
    step = pl.program_id(0)
    rows, width = cq.shape
    block = enc.shape[0]
    pairs = width // (2 * HD)

    @pl.when(step == 0)
    def _():
        for pair in range(pairs):
            at = slice(pair * 2 * HD, (pair + 1) * 2 * HD)
            masked[pair] = pair_mask(cq[:, at])
        top[...] = jnp.full(top.shape, NEG, F32)
        total[...] = jnp.zeros(total.shape, F32)
        acc[...] = jnp.zeros(acc.shape, F32)

    source = enc[...]
    k_out[...] = narrow(dot_nn(source, wk[...]))
    v_out[...] = narrow(dot_nn(source, wv[...]))
    place = lax.broadcasted_iota(jnp.int32, (slot, 2 * rows), 0)
    passages = block // slot
    valid = jnp.concatenate([place < lengths[step * passages + i] for i in range(passages)], axis=0)
    for pair in range(pairs):
        at = slice(pair * 2 * HD, (pair + 1) * 2 * HD)
        scores = jnp.where(valid, dot_nt(k_out[:, at], masked[pair]), NEG)
        before = top[pair : pair + 1]
        now = jnp.maximum(before, jnp.max(scores, axis=0, keepdims=True))
        top[pair : pair + 1] = now
        fade = jnp.exp(before - now)
        raised = jnp.exp(scores - now)
        total[pair : pair + 1] = total[pair : pair + 1] * fade + jnp.sum(raised, axis=0, keepdims=True)
        part = pair_diag(dot_tn(v_out[:, at], narrow(raised)), rows)
        fades = jnp.concatenate(
            [jnp.broadcast_to(fade[:, :rows], (HD, rows)), jnp.broadcast_to(fade[:, rows:], (HD, rows))], axis=0
        )
        acc[at, :] = acc[at, :] * fades + part

    @pl.when(step == pl.num_programs(0) - 1)
    def _():
        for pair in range(pairs):
            at = slice(pair * 2 * HD, (pair + 1) * 2 * HD)
            sums = total[pair : pair + 1]
            lse_out[pair : pair + 1] = top[pair : pair + 1] + jnp.log(sums)
            inverse = 1.0 / sums
            spread = jnp.concatenate(
                [jnp.broadcast_to(inverse[:, :rows], (HD, rows)), jnp.broadcast_to(inverse[:, rows:], (HD, rows))],
                axis=0,
            )
            mix_out[at, :] = acc[at, :] * spread


def feed_kernel(
    mix_t, after_self, cot, wo, w_in, w_out, g3,
    result_out, grad_out, gmix_out, delta_out, dgain_out, d_in, d_out, d_o,
):
    rows, width = cot.shape
    hidden_units = w_in.shape[1]
    mix = narrow(mix_t[...].T)
    after = after_self[...] + dot_nn(mix, wo[...])
    h3 = narrow(rms(after, g3[...]))
    inner = dot_nn(h3, w_in[...])
    bent = jnp.tanh(ROOT * (inner + 0.044715 * (inner * inner * inner)))
    active = narrow(0.5 * inner * (1.0 + bent))
    result_out[...] = after + dot_nn(active, w_out[...])
    cb = cot[...]
    d_out[...] = narrow(dot_tn(active, cb))
    slope = 0.5 * (1.0 + bent) + (0.5 * ROOT) * inner * (1.0 - bent * bent) * (1.0 + (3 * 0.044715) * inner * inner)
    gi = narrow(dot_nt(cb, w_out[...]) * slope)
    pieces = hidden_units // width
    for piece in range(pieces):
        d_in[piece] = narrow(dot_tn(h3, gi[:, piece * width : (piece + 1) * width]))
    back, gain_grad = rms_back(after, g3[...], dot_nt(gi, w_in[...]))
    dgain_out[...] = gain_grad
    grad = cb.astype(F32) + back
    grad_out[...] = grad
    gb = narrow(grad)
    d_o[...] = narrow(dot_tn(mix, gb))
    gmix = narrow(dot_nt(gb, wo[...]))
    gmix_out[...] = gmix
    product = gmix.astype(F32).T * mix_t[...]
    for pair in range(width // (2 * HD)):
        first = jnp.sum(product[pair * 2 * HD : pair * 2 * HD + HD], axis=0, keepdims=True)
        second = jnp.sum(product[pair * 2 * HD + HD : (pair + 1) * 2 * HD], axis=0, keepdims=True)
        delta_out[pair : pair + 1] = jnp.concatenate([first, second], axis=1)


def cross_backward_kernel(
    slot, lengths, enc, k, v, wk, wv, cq, gmix, lse, delta,
    enc_out, dq_out, dk_out, dv_out, masked, gmasked, dq_t, dkv, acc,
):
    step = pl.program_id(0)
    rows, width = cq.shape
    block = enc.shape[0]
    pairs = width // (2 * HD)

    @pl.when(step == 0)
    def _():
        for pair in range(pairs):
            at = slice(pair * 2 * HD, (pair + 1) * 2 * HD)
            masked[pair] = pair_mask(cq[:, at])
            gmasked[pair] = pair_mask(gmix[:, at])
        dq_t[...] = jnp.zeros(dq_t.shape, F32)
        acc[...] = jnp.zeros(acc.shape, F32)

    place = lax.broadcasted_iota(jnp.int32, (slot, 2 * rows), 0)
    passages = block // slot
    valid = jnp.concatenate([place < lengths[step * passages + i] for i in range(passages)], axis=0)
    for pair in range(pairs):
        at = slice(pair * 2 * HD, (pair + 1) * 2 * HD)
        scores = jnp.where(valid, dot_nt(k[:, at], masked[pair]), NEG)
        chances = jnp.exp(scores - lse[pair : pair + 1])
        dkv[:, width + pair * 2 * HD : width + (pair + 1) * 2 * HD] = narrow(dot_nn(narrow(chances), gmasked[pair]))
        ds = narrow(chances * (dot_nt(v[:, at], gmasked[pair]) - delta[pair : pair + 1]))
        dkv[:, at] = narrow(dot_nn(ds, masked[pair]))
        dq_t[at, :] = dq_t[at, :] + pair_diag(dot_tn(k[:, at], ds), rows)
    enc_out[...] = narrow(dot_nt(dkv[:, :width], wk[...]) + dot_nt(dkv[:, width:], wv[...]))
    acc[...] = acc[...] + dot_tn(enc[...], dkv[...])

    @pl.when(step == pl.num_programs(0) - 1)
    def _():
        dq_out[...] = narrow(dq_t[...].T)
        dk_out[...] = narrow(acc[:, :width])
        dv_out[...] = narrow(acc[:, width:])


def self_backward_kernel(
    hidden, h1, q, k, v, mix, after_self, h2, dcq, grad_cross, wq, wk, wv, wo, wcq, g1, g2, table,
    hidden_out, d_cq, d_o, d_q, d_k, d_v, dg1_out, dg2_out, dtable_out,
):
    rows, width = hidden.shape
    pairs = width // (2 * HD)
    d_cq[...] = narrow(dot_tn(h2[...], dcq[...]))
    back, gain_grad = rms_back(after_self[...], g2[...], dot_nt(dcq[...], wcq[...]))
    dg2_out[...] = gain_grad
    grad = grad_cross[...] + back
    sb = narrow(grad)
    d_o[...] = narrow(dot_tn(mix[...], sb))
    gmix = narrow(dot_nt(sb, wo[...]))
    bias = head_bias(table[...].T, rows)
    allowed = causal_mask(rows)
    dq_parts, dk_parts, dv_parts, sums = [], [], [], []
    for pair in range(pairs):
        at = slice(pair * 2 * HD, (pair + 1) * 2 * HD)
        masked = pair_mask(q[:, at])
        gmasked = pair_mask(gmix[:, at])
        scores = dot_nt(k[:, at], masked)
        both = jnp.concatenate(
            [toeplitz(bias[2 * pair : 2 * pair + 1], rows), toeplitz(bias[2 * pair + 1 : 2 * pair + 2], rows)],
            axis=1,
        )
        scores = jnp.where(allowed, scores + both, NEG)
        top = jnp.max(scores, axis=0, keepdims=True)
        raised = jnp.exp(scores - top)
        chances = raised / jnp.sum(raised, axis=0, keepdims=True)
        dv_parts.append(narrow(dot_nn(narrow(chances), gmasked)))
        dp = dot_nt(v[:, at], gmasked)
        ds = chances * (dp - jnp.sum(chances * dp, axis=0, keepdims=True))
        sums.append(diagonal_sums(ds[:, :rows]))
        sums.append(diagonal_sums(ds[:, rows:]))
        dsb = narrow(ds)
        dk_parts.append(narrow(dot_nn(dsb, masked)))
        dq_parts.append(pair_diag(dot_tn(k[:, at], dsb), rows))
    dq = narrow(jnp.concatenate(dq_parts, axis=0).T)
    dk = jnp.concatenate(dk_parts, axis=1)
    dv = jnp.concatenate(dv_parts, axis=1)
    d_q[...] = narrow(dot_tn(h1[...], dq))
    d_k[...] = narrow(dot_tn(h1[...], dk))
    d_v[...] = narrow(dot_tn(h1[...], dv))
    into = dot_nt(dq, wq[...]) + dot_nt(dk, wk[...]) + dot_nt(dv, wv[...])
    back, gain_grad = rms_back(hidden[...].astype(F32), g1[...], into)
    dg1_out[...] = gain_grad
    hidden_out[...] = grad + back
    by_distance = jnp.concatenate(sums, axis=0)
    onehot = bucket_onehot_rows(table.shape[0], rows)
    dtable_out[...] = lax.dot_general(
        onehot, by_distance, (((1,), (1,)), ((), ())), precision=lax.Precision.HIGHEST, preferred_element_type=F32
    )


def halving_order(bits, piece):
    first = list(range(bits))
    if sum(other in PLANES_FIRST for other in range(piece + 1)) % 2 != piece % 2:
        first[0], first[1] = first[1], first[0]
    return first[2:] + first[:2] if piece in PLANES_FIRST else first


class Inputs(NamedTuple):
    lengths: Any
    encodings: Any
    wq: Any
    wk: Any
    wv: Any
    wo: Any
    wcq: Any
    wck: Any
    wcv: Any
    wco: Any
    w_in: Any
    w_out: Any
    hidden: Any
    cot: Any
    g1: Any
    g2: Any
    g3: Any
    table: Any


class Outputs(NamedTuple):
    result: Any
    hidden: Any
    enc: Any
    sq: Any
    sk: Any
    sv: Any
    so: Any
    cq: Any
    ck: Any
    cv: Any
    co: Any
    fin: Any
    fout: Any
    gs: Any
    gc: Any
    gf: Any
    table: Any


class Scratch(NamedTuple):
    left_self: Any
    left_feed: Any
    right: Any
    give: Any
    late: Any
    late_give: Any
    enc: Any
    keys: Any
    values: Any
    queries: Any
    grads: Any
    stats: Any
    weights: Any
    masked: Any
    gmasked: Any
    acc: Any
    q: Any
    k: Any
    v: Any
    after_self: Any
    grad_cross: Any
    top: Any
    lse: Any
    delta: Any
    swap_give: Any
    swap_take: Any
    mine: Any
    last_own: Any
    last_other: Any
    small_gains: Any
    small_table: Any
    load: Any
    pair_send: Any
    pair_recv: Any
    sum_send: Any
    sum_recv: Any
    in_send: Any
    in_recv: Any
    all_send: Any
    all_recv: Any
    own: Any
    out: Any
    small_send: Any
    small_recv: Any
    last_send: Any
    last_recv: Any


CO, CQ, SO, SQ, SK, SV, CK, CV = range(8)


def layer_kernel(n, slot, count_in, count_out, *refs):
    bits = n.bit_length() - 1
    ins = Inputs(*refs[: len(Inputs._fields)])
    outs = Outputs(*refs[len(ins) : len(ins) + len(Outputs._fields)])
    scratch = refs[len(ins) + len(outs) :]
    r, stages = Scratch(*scratch[: len(Scratch._fields)]), scratch[len(Scratch._fields) :]
    mine, weights = r.mine, r.weights
    share, half = mine.shape[2], mine.shape[3] // 2
    pieces = 2 * mine.shape[0]
    rows, width = ins.hidden.shape
    units = count_out * width
    span = count_in * half
    pairs = width // (2 * HD)
    two = 2 * HD
    line = n // 4
    me, core = lax.axis_index(PASS), lax.axis_index(CORE)
    low = me % 4
    partner = (me, 1 - core)
    wq, wk, wv, wo, wcq, wck, wcv, wco = (weights.at[i] for i in range(8))
    g1, g2, g3 = (g[...].reshape(1, width) for g in (ins.g1, ins.g2, ins.g3))

    def remote(src, dst, send, recv, device):
        return pltpu.make_async_remote_copy(
            src_ref=src, dst_ref=dst, send_sem=send, recv_sem=recv, device_id=device, device_id_type=MESH
        )

    def by_core(body):
        for c in range(2):
            pl.when(core == c)(functools.partial(body, c))

    def columns(pair):
        return slice(pair * two, (pair + 1) * two)

    parts = units // width
    loads = [(w, weights.at[i]) for i, w in enumerate(ins[2:10])]
    tiles = mine.reshape(2 * parts, width, width)
    for j in range(parts):
        at = slice(j * width, (j + 1) * width)
        loads += [(ins.w_in.at[:, at], tiles.at[j]), (ins.w_out.at[at], tiles.at[parts + j])]

    def load(i):
        return pltpu.make_async_copy(loads[i][0], loads[i][1], r.load.at[i])

    for i in range(8):
        load(i).start()

    barrier = pltpu.get_barrier_semaphore()
    pl.semaphore_signal(barrier, inc=1, device_id=partner, device_id_type=MESH)

    def greet(d, carry):
        pl.semaphore_signal(barrier, inc=1, device_id=(me ^ d, core), device_id_type=MESH)
        return carry

    lax.fori_loop(1, n, greet, 0)
    pl.semaphore_wait(barrier, n)

    def passage_at(p):
        return pl.ds(pl.multiple_of(p * slot, slot), slot)

    def bring(q):
        return remote(ins.encodings.at[q], r.enc.at[passage_at(me)], r.in_send.at[q], r.in_recv.at[me], (q, core))

    def arrived(p):
        return remote(ins.encodings.at[p], r.enc.at[passage_at(p)], r.in_send.at[p], r.in_recv.at[p], (p, core))

    def bring_range(first, last):
        def one(d, carry):
            bring(me ^ d).start()
            return carry

        lax.fori_loop(first, last, one, 0)

    bring_range(1, 4)
    own_passage = pltpu.make_async_copy(ins.encodings.at[me], r.enc.at[passage_at(me)], r.own.at[0])
    own_passage.start()
    for i in range(8, len(loads)):
        load(i).start()

    x_peer, y_peer = (me ^ 1, core), (me ^ 2, core)

    steps_of_line = [[k for k in range(1, line) if k.bit_count() == hops] for hops in range(1, bits - 1)]
    line_bits = len(steps_of_line)

    def line_copy(kind, k):
        last = k & -k
        origin = me ^ (4 * (k ^ last))
        ref = r.stats.at[origin] if kind == 2 else (r.queries, r.grads)[kind].at[:, origin]
        return remote(ref, ref, r.all_send.at[kind, k - 1], r.all_recv.at[kind, k - 1], (me ^ (4 * last), core))

    def spread_line(kind, number):
        if number:
            for k in steps_of_line[number - 1]:
                line_copy(kind, k).wait_recv()
        for k in reversed(steps_of_line[number]) if number < line_bits else ():
            line_copy(kind, k).start()

    def plane_copy(kind, number, k):
        part = number % 2
        first, second = (x_peer, y_peer) if part == 0 else (y_peer, x_peer)
        origin = me ^ (4 * k) if number < 4 else me ^ (4 * k) ^ (1 << part)
        at = (r.queries, r.grads)[kind].at[part, origin]
        sem = line - 1 + number * line + k
        return remote(at, at, r.all_send.at[kind, sem], r.all_recv.at[kind, sem], first if number < 2 else second)

    def stat_plane(d):
        view = r.stats.reshape(line, 4, *r.stats.shape[1:]).at[:, low]
        sem = line - 2 + d
        return remote(view, view, r.all_send.at[2, sem], r.all_recv.at[2, sem], (me ^ d, core))

    def spread_plane(kind, blocks):
        for number in range(4):
            for k in blocks:
                plane_copy(kind, number, k).start()

    def spread_rest(kind, blocks):
        for k in blocks:
            for number in range(2):
                plane_copy(kind, number, k).wait_recv()
        for k in blocks:
            for number in range(4, 6):
                plane_copy(kind, number, k).start()

    def spread_taken(kind):
        for number in range(2, 6):
            for k in range(line):
                plane_copy(kind, number, k).wait_recv()

    def spread_sent(kind):
        for k in range(1, line):
            line_copy(kind, k).wait_send()
        for number in range(6):
            for k in range(line):
                plane_copy(kind, number, k).wait_send()

    value = ins.hidden[...].astype(F32)
    h1 = narrow(rms(value, g1))
    r.left_self[0, :, :width] = h1
    for i, ref in enumerate((r.q, r.k, r.v)):
        load(i).wait()
        ref[...] = narrow(dot_nn(h1, weights[i]))
    bias = head_bias(ins.table[...], rows)
    allowed = causal_mask(rows)

    def self_chances(pair):
        at = columns(pair)
        masked = pair_mask(r.q[:, at])
        scores = dot_nt(r.k[:, at], masked)
        both = jnp.concatenate([toeplitz(bias[2 * pair + i : 2 * pair + i + 1], rows) for i in range(2)], axis=1)
        scores = jnp.where(allowed, scores + both, NEG)
        raised = jnp.exp(scores - jnp.max(scores, axis=0, keepdims=True))
        return at, masked, raised / jnp.sum(raised, axis=0, keepdims=True)

    for pair in range(pairs):
        at, _, chances = self_chances(pair)
        r.acc[at, :] = pair_diag(dot_tn(r.v[:, at], narrow(chances)), rows)
    mix1 = narrow(r.acc[...].T)
    r.left_self[0, :, 2 * width :] = mix1
    load(3).wait()
    after_self = value + dot_nn(mix1, wo[...])
    r.after_self[...] = after_self
    h2 = narrow(rms(after_self, g2))
    r.left_self[0, :, width : 2 * width] = h2
    load(4).wait()
    cq = narrow(dot_nn(h2, wcq[...]))
    for c in range(2):
        r.queries[c, me] = cq[:, c * half : (c + 1) * half]
    spread_line(0, 0)
    bring_range(n // 2, 3 * n // 4)
    for pair in range(pairs):
        r.masked[pair] = pair_mask(cq[:, columns(pair)])
    r.top[...] = jnp.full(r.top.shape, NEG, F32)
    r.lse[...] = jnp.zeros(r.lse.shape, F32)
    r.acc[...] = jnp.zeros(r.acc.shape, F32)

    def pair_copy(i):
        src = (r.left_self.at[0], r.left_feed.at[0], r.give)[i]
        dst = (r.left_self, r.left_feed, r.right)[i].at[1]
        return remote(src, dst, r.pair_send.at[i], r.pair_recv.at[i], partner)

    pair_copy(0).start()

    place = lax.broadcasted_iota(jnp.int32, (slot, 2 * rows), 0)

    def spread(row):
        return jnp.concatenate(
            [jnp.broadcast_to(row[:, :rows], (HD, rows)), jnp.broadcast_to(row[:, rows:], (HD, rows))], axis=0
        )

    load(5).wait()
    load(6).wait()
    own_passage.wait()
    few = 2
    turns = n // few

    def forward_block(turn, carry):
        @pl.when(turn == 1)
        def _():
            for number in range(1, line_bits):
                spread_line(0, number)
            bring_range(3 * n // 4, n)
            bring_range(4, n // 2)

        @pl.when(turn == 3)
        def _():
            spread_line(0, line_bits)
            spread_plane(0, range(line))

        pl.when(turn == turns - 2)(functools.partial(spread_rest, 0, range(line)))
        part = turn // (turns // 4)
        moved = turn % (turns // 4) + (part % 2 * 2 + part // 2) * (turns // 4)
        first = (moved ^ (me // few)) * few
        for i in range(few):

            @pl.when(first + i != me)
            def _(i=i):
                arrived(first + i).wait_recv()

        at = pl.ds(pl.multiple_of(first * slot, few * slot), few * slot)
        source = r.enc[at]
        r.keys[at] = narrow(dot_nn(source, wck[...]))
        r.values[at] = narrow(dot_nn(source, wcv[...]))
        valid = jnp.concatenate([place < ins.lengths[first + i] for i in range(few)], axis=0)
        for pair in range(pairs):
            cols = columns(pair)
            scores = jnp.where(valid, dot_nt(r.keys[at, cols], r.masked[pair]), NEG)
            before = r.top[pair : pair + 1]
            now = jnp.maximum(before, jnp.max(scores, axis=0, keepdims=True))
            r.top[pair : pair + 1] = now
            fade = jnp.exp(before - now)
            raised = jnp.exp(scores - now)
            r.lse[pair : pair + 1] = r.lse[pair : pair + 1] * fade + jnp.sum(raised, axis=0, keepdims=True)
            part = pair_diag(dot_tn(r.values[at, cols], narrow(raised)), rows)
            r.acc[cols, :] = r.acc[cols, :] * spread(fade) + part
        return carry

    lax.fori_loop(0, turns, forward_block, 0)
    for pair in range(pairs):
        cols = columns(pair)
        sums = r.lse[pair : pair + 1]
        r.lse[pair : pair + 1] = r.top[pair : pair + 1] + jnp.log(sums)
        r.acc[cols, :] = r.acc[cols, :] * spread(1.0 / sums)

    own_load = pltpu.make_async_copy(ins.encodings, r.enc.reshape(n, slot, width), r.own.at[0])
    own_load.start()
    mix2 = narrow(r.acc[...].T)
    r.left_feed[0, :, units + width :] = mix2
    load(7).wait()
    after_cross = r.after_self[...] + dot_nn(mix2, wco[...])
    h3 = narrow(rms(after_cross, g3))
    r.left_feed[0, :, units : units + width] = h3
    cb = ins.cot[...]
    result = after_cross
    into = jnp.zeros((rows, width), F32)
    for j in range(parts):
        load(8 + 2 * j).wait()
        inner = dot_nn(h3, tiles[j])
        bent = jnp.tanh(ROOT * (inner + 0.044715 * (inner * inner * inner)))
        active = narrow(0.5 * inner * (1.0 + bent))
        r.left_feed[0, :, j * width : (j + 1) * width] = active
        slope = 0.5 * (1.0 + bent) + (0.5 * ROOT) * inner * (1.0 - bent * bent) * (1.0 + (3 * 0.044715) * inner * inner)
        load(9 + 2 * j).wait()
        result = result + dot_nn(active, tiles[parts + j])
        gi = narrow(dot_nt(cb, tiles[parts + j]) * slope)
        to = slice((j % (parts // 2)) * width, (j % (parts // 2) + 1) * width)

        def keep(c, gi=gi, to=to, owner=j // (parts // 2)):
            if c == owner:
                r.right[0, :, to] = gi
            else:
                r.give[:, to] = gi

        by_core(keep)
        into = into + dot_nt(gi, tiles[j])
    outs.result[...] = result
    pair_copy(1).start()
    back, dg3 = rms_back(after_cross, g3, into)
    grad = cb.astype(F32) + back
    r.grad_cross[...] = grad
    gb = narrow(grad)

    def keep_columns(c):
        for j, value in enumerate((cb, gb)):
            to = slice(span + j * half, span + (j + 1) * half)
            r.right[0, :, to] = value[:, c * half : (c + 1) * half]
            r.give[:, to] = value[:, (1 - c) * half : (2 - c) * half]

    by_core(keep_columns)
    pair_copy(2).start()
    gmix = narrow(dot_nt(gb, wco[...]))
    for c in range(2):
        r.grads[c, me] = gmix[:, c * half : (c + 1) * half]
    spread_line(1, 0)
    spread_plane(1, [0])
    product = gmix.astype(F32).T * r.acc[...]
    for pair in range(pairs):
        at = columns(pair)
        r.gmasked[pair] = pair_mask(gmix[:, at])
        part = product[at]
        r.delta[pair : pair + 1] = jnp.concatenate(
            [jnp.sum(part[:HD], axis=0, keepdims=True), jnp.sum(part[HD:], axis=0, keepdims=True)], axis=1
        )
    lane = lax.broadcasted_iota(jnp.int32, (1, 2 * rows), 1)
    extent = jnp.zeros((1, 2 * rows), F32)
    for p in range(n):
        extent = jnp.where(lane == p, ins.lengths[p].astype(F32), extent)
    r.stats[me, :pairs] = r.lse[...]
    r.stats[me, pairs : 2 * pairs] = r.delta[...]
    r.stats[me, 2 * pairs : 2 * pairs + 1] = extent
    spread_line(2, 0)
    r.acc[...] = jnp.zeros(r.acc.shape, F32)

    def lanes(piece):
        return slice((piece % 2) * half, (piece % 2 + 1) * half)

    def split(piece, stage):
        done = halving_order(bits, piece)[:stage]
        bit = halving_order(bits, piece)[stage]
        inner = 1 << len([b for b in range(bit) if b not in done])
        outer = (n >> stage) // (2 * inner)

        def half_of(value):
            if stage:
                return stages[stage - 1].reshape(pieces, outer, 2, inner, share, half).at[piece, :, value]
            return mine.reshape(pieces // 2, outer, 2, inner, share, 2 * half).at[piece // 2, :, value, :, :, lanes(piece)]

        return half_of, (me >> bit) & 1, inner, outer, bit

    def stage_copy(piece, stage):
        half_of, value, inner, outer, bit = split(piece, stage)
        dst = stages[stage].at[piece].reshape(outer, inner, share, half)
        sems = r.sum_send.at[piece, stage], r.sum_recv.at[piece, stage]
        return remote(half_of(1 - value), dst, *sems, (me ^ (1 << bit), core))

    first_square = count_in + count_out
    square_outs = (outs.co, outs.cq, outs.so, outs.sq, outs.sk, outs.sv, outs.ck, outs.cv)

    def put(piece, c, total):
        if piece < count_in:
            outs.fin[:, (c * count_in + piece) * half : (c * count_in + piece + 1) * half] = total
        elif piece < first_square:
            k = piece - count_in
            outs.fout[k * share : (k + 1) * share, c * half : (c + 1) * half] = total
        else:
            square_outs[piece - first_square][:, c * half : (c + 1) * half] = total

    def last_copy(piece):
        return remote(r.last_own.at[piece], r.last_other.at[piece], r.last_send.at[piece], r.last_recv.at[piece], partner)

    def begin(piece):
        stage_copy(piece, 0).start()

    def arrive(piece, stage):
        stage_copy(piece, stage).wait_recv()
        half_of, value, inner, outer, _ = split(piece, stage)
        kept = half_of(value)
        dst = stages[stage].at[piece]
        if stage + 1 < bits:

            def one(i, carry):
                dst[i] = narrow(kept[i // inner, i % inner].astype(F32) + dst[i].astype(F32))
                return carry

            lax.fori_loop(0, outer * inner, one, 0)
            stage_copy(piece, stage + 1).start()
        else:
            total = kept[0, 0].astype(F32) + dst[0].astype(F32)
            r.last_own[piece] = narrow(total)
            last_copy(piece).start()
            by_core(lambda c: put(piece, c, total))

    def owners(value):
        return narrow(value).reshape(n, share, half)

    def keep_piece(piece, value):
        mine[piece // 2, :, :, lanes(piece)] = value

    for i in range(3):
        pair_copy(i).wait_recv()
    left_self, left_feed, right = (x.reshape(2 * rows, x.shape[2]) for x in (r.left_self, r.left_feed, r.right))
    early = [piece for piece in range(first_square) if piece not in PLANES_FIRST]
    for piece in range(count_in):
        keep_piece(piece, owners(dot_tn(left_feed[:, units : units + width], right[:, piece * half : (piece + 1) * half])))
        if piece in early[:2]:
            begin(piece)
    per = width // (count_out * share)
    for part in range(count_out):
        value = narrow(dot_tn(left_feed[:, part * width : (part + 1) * width], right[:, span : span + half]))
        value = value.reshape(per, count_out, share, half)
        for k in range(count_out):
            piece = count_in + k
            mine[piece // 2, part * per : (part + 1) * per, :, lanes(piece)] = value[:, k]
    keep_piece(first_square + CO, owners(dot_tn(left_feed[:, units + width :], right[:, span + half :])))
    for piece in early[2:]:
        begin(piece)

    many = 4

    def question_block(turn, carry):
        at = pl.ds(pl.multiple_of(turn * many * slot, many * slot), many * slot)
        valid = jnp.concatenate([place < ins.lengths[turn * many + i] for i in range(many)], axis=0)
        for pair in range(pairs):
            cols = columns(pair)
            key = r.keys[at, cols]
            scores = jnp.where(valid, dot_nt(key, r.masked[pair]), NEG)
            chances = jnp.exp(scores - r.lse[pair : pair + 1])
            ds = narrow(chances * (dot_nt(r.values[at, cols], r.gmasked[pair]) - r.delta[pair : pair + 1]))
            r.acc[cols, :] = r.acc[cols, :] + pair_diag(dot_tn(key, ds), rows)
        return carry

    lax.fori_loop(0, n // (2 * many), question_block, 0)

    for number in range(1, line_bits):
        spread_line(1, number)
        spread_line(2, number)
        spread_plane(1, steps_of_line[number - 1])
    for piece in PLANES_FIRST:
        if piece < first_square:
            begin(piece)
    lax.fori_loop(n // (2 * many), n // many, question_block, 0)

    late = (CQ, SO, SQ, SK, SV)
    lefts = (width, 2 * width, 0, 0, 0)

    def late_copy(i):
        return remote(r.late_give.at[i], r.late.at[i, 1], r.pair_send.at[3 + i], r.pair_recv.at[3 + i], partner)

    def late_give(name, value):
        i = late.index(name)

        def part(c):
            r.late[i, 0] = value[:, c * half : (c + 1) * half]
            r.late_give[i] = value[:, (1 - c) * half : (2 - c) * half]

        by_core(part)
        late_copy(i).start()

    def late_take(name, now=True):
        i = late.index(name)
        late_copy(i).wait_recv()
        left = left_self[:, lefts[i] : lefts[i] + width]
        keep_piece(first_square + name, owners(dot_tn(left, r.late.at[i].reshape(2 * rows, half)[...])))
        if now:
            begin(first_square + name)

    dcq = narrow(r.acc[...].T)
    late_give(CQ, dcq)
    back, dg2 = rms_back(r.after_self[...], g2, dot_nt(dcq, wcq[...]))
    grad = r.grad_cross[...] + back
    sb = narrow(grad)
    late_give(SO, sb)

    own_load.wait()

    def project(turn, carry):
        at = pl.ds(pl.multiple_of(turn * many * slot, many * slot), many * slot)
        source = r.enc[at]
        r.keys[at] = narrow(dot_nn(source, wck[...]))
        r.values[at] = narrow(dot_nn(source, wcv[...]))
        return carry

    lax.fori_loop(0, n // (2 * many), project, 0)
    spread_rest(1, [0])
    spread_line(1, line_bits)
    spread_plane(1, steps_of_line[-1])
    spread_line(2, line_bits)
    for d in range(1, 4):
        stat_plane(d).start()
    for ks in steps_of_line[:-1]:
        spread_rest(1, ks)
    lax.fori_loop(n // (2 * many), n // many, project, 0)
    late_take(CQ, False)

    gself = narrow(dot_nt(sb, wo[...]))
    dq_parts, dk_parts, dv_parts, sums = [], [], [], []
    for pair in range(pairs):
        at, masked, chances = self_chances(pair)
        gmasked = pair_mask(gself[:, at])
        dv_parts.append(narrow(dot_nn(narrow(chances), gmasked)))
        dp = dot_nt(r.v[:, at], gmasked)
        ds = chances * (dp - jnp.sum(chances * dp, axis=0, keepdims=True))
        sums.append(diagonal_sums(ds[:, :rows]))
        sums.append(diagonal_sums(ds[:, rows:]))
        dsb = narrow(ds)
        dk_parts.append(narrow(dot_nn(dsb, masked)))
        dq_parts.append(pair_diag(dot_tn(r.k[:, at], dsb), rows))
    dq = narrow(jnp.concatenate(dq_parts, axis=0).T)
    dk = jnp.concatenate(dk_parts, axis=1)
    dv = jnp.concatenate(dv_parts, axis=1)
    late_give(SQ, dq)
    late_give(SK, dk)
    late_give(SV, dv)
    late_take(SO, False)
    into = dot_nt(dq, wq[...]) + dot_nt(dk, wk[...]) + dot_nt(dv, wv[...])
    late_take(SQ, False)
    late_take(SK, False)
    late_take(SV, False)
    back, dg1 = rms_back(ins.hidden[...].astype(F32), g1, into)
    outs.hidden[...] = grad + back
    onehot = bucket_onehot_rows(ins.table.shape[1], rows)
    dtable = lax.dot_general(
        jnp.concatenate(sums, axis=0), onehot, (((1,), (1,)), ((), ())), precision=lax.Precision.HIGHEST,
        preferred_element_type=F32,
    )

    small = (r.small_gains, r.small_table)

    def small_copies(step):
        device = partner if step == bits else (me ^ (1 << step), core)
        return [
            remote(ref.at[step], ref.at[bits + 1 + step], r.small_send.at[j, step], r.small_recv.at[j, step], device)
            for j, ref in enumerate(small)
        ]

    r.small_gains[0] = jnp.concatenate([dg1, dg2, dg3, jnp.zeros((5, width), F32)], axis=0)
    r.small_table[0] = jnp.zeros(r.small_table.shape[1:], F32)
    r.small_table[0, : dtable.shape[0], : dtable.shape[1]] = dtable
    for copy in small_copies(0):
        copy.start()

    def small_step(step):
        for copy in small_copies(step):
            copy.wait_recv()
        gains, table = (ref[step] + ref[bits + 1 + step] for ref in small)
        if step < bits:
            r.small_gains[step + 1] = gains
            r.small_table[step + 1] = table
            for copy in small_copies(step + 1):
                copy.start()
        else:
            outs.table[...] = table[: dtable.shape[0], : dtable.shape[1]]
            for j, out in enumerate((outs.gs, outs.gc, outs.gf)):
                own = jnp.zeros((1, share), F32)
                for o in range(n):
                    own = jnp.where(me == o, gains[j : j + 1, o * share : (o + 1) * share], own)
                out[...] = own

    place_f = place.astype(F32)

    def owner_block(turn, carry):
        q = (turn % line) * 4 + (low ^ (turn // line))
        at = passage_at(q)
        stats = r.stats[q]
        extent = jnp.sum(jnp.where(lane == me, stats[2 * pairs : 2 * pairs + 1], 0.0), axis=1, keepdims=True)
        valid = place_f < extent
        for pair in range(pairs):
            cols = columns(pair)
            c, within = pair // (pairs // 2), columns(pair % (pairs // 2))
            masked, gmasked = pair_mask(r.queries[c, q, :, within]), pair_mask(r.grads[c, q, :, within])
            scores = jnp.where(valid, dot_nt(r.keys[at, cols], masked), NEG)
            chances = jnp.exp(scores - stats[pair : pair + 1])
            ds = narrow(chances * (dot_nt(r.values[at, cols], gmasked) - stats[pairs + pair : pairs + pair + 1]))
            r.values[at, cols] = narrow(dot_nn(narrow(chances), gmasked))
            r.keys[at, cols] = narrow(dot_nn(ds, masked))
        return carry

    spread_rest(1, steps_of_line[-1])

    middle, last = range(first_square, first_square + CK), range(first_square + CK, pieces)

    def taken_up(event):
        piece, stage = event
        if piece in early:
            keys = (0.0, 1.1, 3.0, 4.3)
        elif piece in last:
            keys = (3.5, 3.8, 4.2, 4.9)
        elif piece not in middle:
            keys = (0.5 if piece < count_in else 1.0, 3.3, 3.9, 4.4)
        elif piece in PLANES_FIRST:
            keys = (3.25, 3.75, 4.1, 4.7)
        elif piece == first_square + SV:
            keys = (3.05, 3.85, 4.25, 4.75)
        elif piece == first_square + SK:
            keys = (2.1, 3.35, 3.65, 4.65)
        else:
            keys = (2.0, 3.1, 3.6, 4.6)
        return keys[min(stage, 2)] if stage + 1 < bits else keys[3]

    events = sorted(((piece, stage) for piece in range(pieces) for stage in range(bits)), key=taken_up)
    visits = [[event for event in events if min(int(taken_up(event)), 3) == visit] for visit in range(4)]
    for piece, stage in visits[0]:
        arrive(piece, stage)
    for piece in middle:
        begin(piece)

    lax.fori_loop(0, line, owner_block, 0)

    spread_taken(0)
    spread_taken(1)
    for d in range(1, 4):
        stat_plane(d).wait_recv()
    lax.fori_loop(line, 2 * line, owner_block, 0)
    small_step(0)
    for piece, stage in visits[1]:
        arrive(piece, stage)
    lax.fori_loop(2 * line, n, owner_block, 0)
    for piece, stage in visits[2]:
        arrive(piece, stage)

    def encoding_block(turn):
        at = slice(turn * many * slot, (turn + 1) * many * slot)
        value = narrow(dot_nt(r.keys[at], wck[...]) + dot_nt(r.values[at], wcv[...]))
        for c in range(2):
            to = slice(turn * many, (turn + 1) * many)
            r.grads[c, to] = value[:, c * half : (c + 1) * half].reshape(many, slot, half)

    def out_copy(c):
        return pltpu.make_async_copy(r.grads.at[c], outs.enc.at[:, :, c * half : (c + 1) * half], r.out.at[c])

    spread_sent(0)
    spread_sent(1)

    def swap_copy(i):
        return remote(r.swap_give.at[i], r.swap_take.at[i], r.pair_send.at[8 + i], r.pair_recv.at[8 + i], partner)

    def columns_of(ref, c):
        return owners(dot_tn(r.enc[...], ref[:, pl.ds(pl.multiple_of(c * half, 128), half)]))

    for i, ref in enumerate((r.keys, r.values)):
        r.swap_give[i] = columns_of(ref, 1 - core)
        swap_copy(i).start()
    for i, (name, ref) in enumerate(((CK, r.keys), (CV, r.values))):
        piece = first_square + name
        keep_piece(piece, columns_of(ref, core))
        swap_copy(i).wait_recv()

        def one(o, carry, i=i, to=mine.at[piece // 2, :, :, lanes(piece)]):
            to[o] = narrow(to[o].astype(F32) + r.swap_take[i, o].astype(F32))
            return carry

        lax.fori_loop(0, n, one, 0)
        begin(piece)

    rest = visits[3]
    for number, (piece, stage) in enumerate(rest):
        if (piece, stage) == (last[0], 0):
            for turn in range(n // many):
                encoding_block(turn)
            for c in range(2):
                out_copy(c).start()
        arrive(piece, stage)
        for step in range(1, bits + 1):
            if (piece, stage) == (last[1], step - 1):
                small_step(step)

    for piece in range(pieces):
        last_copy(piece).wait_recv()
        total = r.last_other[piece].astype(F32)
        by_core(lambda c: put(piece, 1 - c, total))

    for c in range(2):
        out_copy(c).wait()

    def brought(d, carry):
        bring(me ^ d).wait_send()
        return carry

    lax.fori_loop(1, n, brought, 0)
    for k in range(1, line):
        line_copy(2, k).wait_send()
    for d in range(1, 4):
        stat_plane(d).wait_send()
    for i in range(3):
        pair_copy(i).wait_send()
    for i in range(5):
        late_copy(i).wait_send()
    for i in range(2):
        swap_copy(i).wait_send()
    for piece in range(pieces):
        for stage in range(bits):
            stage_copy(piece, stage).wait_send()
        last_copy(piece).wait_send()
    for step in range(bits + 1):
        for copy in small_copies(step):
            copy.wait_send()


def layer(n, slot, args):
    rows, width = args.hidden.shape
    units = args.w_in.shape[1]
    share, half = width // n, width // 2
    bits = n.bit_length() - 1
    pairs = width // (2 * HD)
    keys = n * slot
    count_in = count_out = units // width
    pieces = 8 + count_in + count_out
    table = args.table.shape
    vmem, hbm = pl.BlockSpec(memory_space=pltpu.VMEM), pl.BlockSpec(memory_space=pl.ANY)
    in_specs = [pl.BlockSpec(memory_space=pltpu.SMEM)] + [hbm] * 11 + [vmem] * 6
    wide = jax.ShapeDtypeStruct((rows, width), F32)
    square = jax.ShapeDtypeStruct((share, width), F32)
    gain = jax.ShapeDtypeStruct((1, share), F32)
    results = [wide, wide, jax.ShapeDtypeStruct((n, slot, width), BF)] + [square] * 8
    results += [jax.ShapeDtypeStruct((share, units), F32), jax.ShapeDtypeStruct((count_out * share, width), F32)]
    results += [gain] * 3 + [jax.ShapeDtypeStruct(table, F32)]
    dma = pltpu.SemaphoreType.DMA
    sixteen, full = pltpu.VMEM((rows, width), BF), pltpu.VMEM((rows, width), F32)
    stat, masks = pltpu.VMEM((pairs, 2 * rows), F32), pltpu.VMEM((pairs, 2 * rows, 2 * HD), BF)
    blocks, shared = pltpu.VMEM((keys, width), BF), pltpu.VMEM((2, n, rows, half), BF)
    swap = pltpu.VMEM((2, n, share, half), BF)
    last = pltpu.VMEM((pieces, share, half), BF)
    up = lambda count: -(-count // 8) * 8
    scratch = Scratch(
        left_self=pltpu.VMEM((2, rows, 3 * width), BF),
        left_feed=pltpu.VMEM((2, rows, units + 2 * width), BF),
        right=pltpu.VMEM((2, rows, units // 2 + width), BF),
        give=pltpu.VMEM((rows, units // 2 + width), BF),
        late=pltpu.VMEM((5, 2, rows, half), BF),
        late_give=pltpu.VMEM((5, rows, half), BF),
        enc=blocks, keys=blocks, values=blocks, queries=shared, grads=shared,
        stats=pltpu.VMEM((n, up(2 * pairs + 1), 2 * rows), F32),
        weights=pltpu.VMEM((8, width, width), BF),
        masked=masks, gmasked=masks,
        acc=pltpu.VMEM((width, rows), F32),
        q=sixteen, k=sixteen, v=sixteen, after_self=full, grad_cross=full,
        top=stat, lse=stat, delta=stat, swap_give=swap, swap_take=swap,
        mine=pltpu.VMEM((pieces // 2, n, share, width), BF),
        last_own=last, last_other=last,
        small_gains=pltpu.VMEM((2 * (bits + 1), 8, width), F32),
        small_table=pltpu.VMEM((2 * (bits + 1), up(table[0]), 128), F32),
        load=dma((8 + 2 * (units // width),)),
        pair_send=dma((10,)), pair_recv=dma((10,)),
        sum_send=dma((pieces, bits)), sum_recv=dma((pieces, bits)),
        in_send=dma((n,)), in_recv=dma((n,)),
        all_send=dma((3, 7 * (n // 4))), all_recv=dma((3, 7 * (n // 4))),
        own=dma((1,)), out=dma((2,)),
        small_send=dma((2, bits + 1)), small_recv=dma((2, bits + 1)),
        last_send=dma((pieces,)), last_recv=dma((pieces,)),
    )
    stages = [pltpu.VMEM((pieces, n >> (b + 1), share, half), BF) for b in range(bits)]
    return pl.pallas_call(
        functools.partial(layer_kernel, n, slot, count_in, count_out),
        out_shape=tuple(results),
        in_specs=in_specs,
        out_specs=tuple([vmem, vmem, hbm] + [vmem] * 14),
        scratch_shapes=list(scratch) + stages,
        compiler_params=pltpu.CompilerParams(collective_id=1, has_side_effects=True, vmem_limit_bytes=LAYER_LIMIT),
    )(*args)


def finish_kernel(count, *refs):
    ins, outs, held, sems = refs[:count], refs[count : 2 * count], refs[2 * count : 3 * count], refs[-1]
    into = [pltpu.make_async_copy(ins[i], held[i], sems.at[0, i]) for i in range(count)]
    back = [pltpu.make_async_copy(held[i], outs[i], sems.at[1, i]) for i in range(count)]
    for copy in into:
        copy.start()
    for i in range(count):
        into[i].wait()
        back[i].start()
    for copy in back:
        copy.wait()


def finish(arrays):
    count = len(arrays)
    spec = pl.BlockSpec(memory_space=pl.ANY)
    return pl.pallas_call(
        functools.partial(finish_kernel, count),
        out_shape=tuple(jax.ShapeDtypeStruct(a.shape, a.dtype) for a in arrays),
        in_specs=[spec] * count,
        out_specs=(spec,) * count,
        scratch_shapes=[pltpu.VMEM(a.shape, a.dtype) for a in arrays] + [pltpu.SemaphoreType.DMA((2, count))],
        compiler_params=pltpu.CompilerParams(vmem_limit_bytes=VMEM_LIMIT),
    )(*arrays)


def whole(shape=None):
    return pl.BlockSpec(memory_space=pltpu.VMEM)


def call(kernel, outs, *args):
    return pl.pallas_call(
        kernel,
        out_shape=tuple(jax.ShapeDtypeStruct(shape, kind) for shape, kind in outs),
        in_specs=[whole()] * len(args),
        out_specs=tuple(whole() for _ in outs),
        compiler_params=pltpu.CompilerParams(vmem_limit_bytes=VMEM_LIMIT),
    )(*args)


def per_device(
    n, hidden, encodings, lengths, cotangent, wq, wk, wv, wo, wcq, wck, wcv, wco, w_in, w_out,
    gain_self, gain_cross, gain_feed, table,
):
    rows, width = hidden.shape[2], hidden.shape[3]
    slot = encodings.shape[3]
    passages = lengths.shape[2]
    units = w_in.shape[1]
    pairs = width // (2 * HD)
    keys = passages * slot
    own = hidden.reshape(rows, width)
    cot = cotangent.reshape(rows, width)
    g1, g2, g3 = (gain.reshape(1, width) for gain in (gain_self, gain_cross, gain_feed))
    length_row = lengths.reshape(passages)
    share = width // n
    fits = passages == n and keys * width * 8 <= 16 << 20 and units == 4 * width
    if n & (n - 1) == 0 and n >= 8 and share % 16 == 0 and fits:
        out = layer(n, slot, Inputs(
            length_row, encodings.reshape(n, slot, width), wq, wk, wv, wo, wcq, wck, wcv, wco, w_in, w_out, own, cot,
            gain_self, gain_cross, gain_feed, table.T,
        ))
        out = finish(out)
        rows_out = tuple(o.reshape(hidden.shape) for o in out[:2])
        gains = tuple(gain.reshape(share) for gain in out[13:16])
        return rows_out + (out[2].reshape(encodings.shape),) + tuple(out[3:13]) + gains + (out[16].T,)

    source = lax.all_to_all(encodings, PASS, split_axis=2, concat_axis=0, tiled=True).reshape(keys, width)

    sixteen, wide = ((rows, width), BF), ((rows, width), F32)
    h1, q, k, v, mix1, after_self, h2, cq = call(
        self_forward_kernel,
        [sixteen] * 5 + [wide, sixteen, sixteen],
        own, wq, wk, wv, wo, wcq, g1, g2, table,
    )

    block = 4 * slot
    steps = keys // block
    stats = jax.ShapeDtypeStruct((pairs, 2 * rows), F32)
    smem = pl.BlockSpec(memory_space=pltpu.SMEM)
    tile = pl.BlockSpec((block, width), lambda i: (i, 0))
    square = pl.BlockSpec((width, width), lambda i: (0, 0))
    query = pl.BlockSpec((rows, width), lambda i: (0, 0))
    stat = pl.BlockSpec((pairs, 2 * rows), lambda i: (0, 0))
    ck, cv, mix_t, lse = pl.pallas_call(
        functools.partial(cross_forward_kernel, slot),
        grid=(steps,),
        out_shape=(
            jax.ShapeDtypeStruct((keys, width), BF),
            jax.ShapeDtypeStruct((keys, width), BF),
            jax.ShapeDtypeStruct((width, rows), F32),
            stats,
        ),
        in_specs=[smem, tile, square, square, query],
        out_specs=(tile, tile, pl.BlockSpec((width, rows), lambda i: (0, 0)), stat),
        scratch_shapes=[
            pltpu.VMEM((pairs, 2 * rows, 2 * HD), BF),
            pltpu.VMEM((pairs, 2 * rows), F32),
            pltpu.VMEM((pairs, 2 * rows), F32),
            pltpu.VMEM((width, rows), F32),
        ],
        compiler_params=pltpu.CompilerParams(vmem_limit_bytes=VMEM_LIMIT),
    )(length_row, source, wck, wcv, cq)

    pieces = units // width
    result, grad_cross, gmix, delta, dg3, d_in, d_out, d_co = call(
        feed_kernel,
        [wide, wide, sixteen, ((pairs, 2 * rows), F32), ((1, width), F32), ((pieces, width, width), BF),
         ((units, width), BF), ((width, width), BF)],
        mix_t, after_self, cot, wco, w_in, w_out, g3,
    )

    enc_grad, dcq, d_ck, d_cv = pl.pallas_call(
        functools.partial(cross_backward_kernel, slot),
        grid=(steps,),
        out_shape=(
            jax.ShapeDtypeStruct((keys, width), BF),
            jax.ShapeDtypeStruct((rows, width), BF),
            jax.ShapeDtypeStruct((width, width), BF),
            jax.ShapeDtypeStruct((width, width), BF),
        ),
        in_specs=[smem, tile, tile, tile, square, square, query, query, stat, stat],
        out_specs=(tile, query, square, square),
        scratch_shapes=[
            pltpu.VMEM((pairs, 2 * rows, 2 * HD), BF),
            pltpu.VMEM((pairs, 2 * rows, 2 * HD), BF),
            pltpu.VMEM((width, rows), F32),
            pltpu.VMEM((block, 2 * width), BF),
            pltpu.VMEM((width, 2 * width), F32),
        ],
        compiler_params=pltpu.CompilerParams(vmem_limit_bytes=VMEM_LIMIT),
    )(length_row, source, ck, cv, wck, wcv, cq, gmix, lse, delta)
    returned = lax.all_to_all(
        enc_grad.reshape(passages, 1, 1, slot, width), PASS, split_axis=0, concat_axis=2, tiled=True
    )

    gain_kind = ((1, width), F32)
    squared = ((width, width), BF)
    hidden_grad, d_cq, d_so, d_q, d_k, d_v, dg1, dg2, dtable = call(
        self_backward_kernel,
        [wide] + [squared] * 5 + [gain_kind, gain_kind, (table.shape, F32)],
        own, h1, q, k, v, mix1, after_self, h2, dcq, grad_cross, wq, wk, wv, wo, wcq, g1, g2, table,
    )

    both = [d_q, d_k, d_v, d_so, d_cq, d_ck, d_cv, d_co, d_in.transpose(1, 0, 2).reshape(width, units), d_out]

    def total(part):
        shared = lax.psum_scatter(part, PASS, scatter_dimension=0, tiled=True)
        return lax.psum(shared.astype(BF), CORE).astype(F32)

    sums = [total(part.astype(F32)) for part in both]
    totals, in_total, out_total = sums[:8], sums[8], sums[9]
    gains = [total(part.reshape(width)) for part in (dg1, dg2, dg3)]
    table_sum = lax.psum(dtable, (PASS, CORE))
    return (
        (result.reshape(hidden.shape), hidden_grad.reshape(hidden.shape), returned)
        + tuple(totals)
        + (in_total, out_total)
        + tuple(gains)
        + (table_sum,)
    )


def solution(mesh):
    rows = P(CORE, PASS, None, None)
    passage = P(PASS, CORE, None, None, None)
    in_specs = (rows, passage, P(CORE, PASS, None), rows) + (P(),) * 14
    out_specs = (rows, rows, passage) + (P(PASS, None),) * 10 + (P(PASS),) * 3 + (P(),)
    return jax.shard_map(
        functools.partial(per_device, mesh.shape[PASS]),
        mesh=mesh,
        in_specs=in_specs,
        out_specs=out_specs,
        check_vma=False,
    )
```

```python
import functools
from typing import Any, NamedTuple

import jax
import jax.numpy as jnp
from jax import lax
from jax.experimental import pallas as pl
from jax.experimental.pallas import tpu as pltpu
from jax.sharding import PartitionSpec as P

HD = 64
EPS = 1e-06
LIMITS = (19, 21, 24, 27, 31, 35, 40, 46, 52, 59, 67, 77, 87, 99, 113)
NEG = -1e30
BF = jnp.bfloat16
F32 = jnp.float32
MESH = pl.DeviceIdType.MESH
PASS, CORE = "pass", "pb"
PLANES_FIRST = (2, 3, 6, 7, 13)
ROOT = 0.7978845608028654
VMEM_LIMIT = 56 << 20
LAYER_LIMIT = 64 << 20


def narrow(value):
    return value.astype(BF)


def dot_nn(left, right):
    return lax.dot_general(left, right, (((1,), (0,)), ((), ())), preferred_element_type=F32)


def dot_nt(left, right):
    return lax.dot_general(left, right, (((1,), (1,)), ((), ())), preferred_element_type=F32)


def dot_tn(left, right):
    return lax.dot_general(left, right, (((0,), (0,)), ((), ())), preferred_element_type=F32)


def rms(value, gain):
    scale = lax.rsqrt(jnp.mean(value * value, axis=-1, keepdims=True) + EPS)
    return value * scale * gain


def rms_back(value, gain, grad):
    scale = lax.rsqrt(jnp.mean(value * value, axis=-1, keepdims=True) + EPS)
    scaled = grad * gain
    inner = jnp.mean(scaled * value, axis=-1, keepdims=True)
    rows = scaled * scale - value * (scale * scale * scale * inner)
    gain_grad = jnp.sum(grad * (value * scale), axis=0, keepdims=True)
    return rows, gain_grad


def pair_mask(pair):
    lane = lax.broadcasted_iota(jnp.int32, pair.shape, 1)
    zero = jnp.zeros_like(pair)
    return jnp.concatenate(
        [jnp.where(lane < HD, pair, zero), jnp.where(lane >= HD, pair, zero)], axis=0
    )


def pair_diag(both, rows):
    return jnp.concatenate([both[:HD, :rows], both[HD:, rows:]], axis=0)


def bucket_onehot_rows(buckets, length):
    distance = lax.broadcasted_iota(jnp.int32, (buckets, length), 1)
    row = lax.broadcasted_iota(jnp.int32, (buckets, length), 0)
    beyond = jnp.zeros_like(distance)
    for edge in LIMITS:
        beyond = beyond + (distance >= edge).astype(jnp.int32)
    bucket = jnp.where(distance < 16, distance, 16 + beyond)
    return (bucket == row).astype(F32)


def head_bias(table, rows):
    onehot = bucket_onehot_rows(table.shape[1], rows)
    return lax.dot_general(
        table, onehot, (((1,), (0,)), ((), ())), precision=lax.Precision.HIGHEST,
        preferred_element_type=F32,
    )


def toeplitz(row, rows):
    return pltpu.roll(jnp.broadcast_to(row, (rows, rows)), 0, 1, stride=1, stride_axis=0)


def diagonal_sums(square):
    rows = square.shape[0]
    place = lax.broadcasted_iota(jnp.int32, square.shape, 0)
    for bit in range(3):
        moved = pltpu.roll(square, rows - (1 << bit), 1)
        square = jnp.where((place >> bit) & 1 == 1, moved, square)
    total = square[:8]
    for group in range(1, rows // 8):
        total = total + pltpu.roll(square[8 * group : 8 * group + 8], rows - 8 * group, 1)
    return jnp.sum(total, axis=0, keepdims=True)


def causal_mask(rows):
    key = lax.broadcasted_iota(jnp.int32, (rows, 2 * rows), 0)
    query = lax.broadcasted_iota(jnp.int32, (rows, 2 * rows), 1)
    query = jnp.where(query >= rows, query - rows, query)
    return key <= query


def self_forward_kernel(
    hidden, wq, wk, wv, wo, wcq, g1, g2, table,
    h1_out, q_out, k_out, v_out, mix_out, after_out, h2_out, cq_out,
):
    rows, width = hidden.shape
    pairs = width // (2 * HD)
    value = hidden[...].astype(F32)
    h1 = narrow(rms(value, g1[...]))
    h1_out[...] = h1
    q = narrow(dot_nn(h1, wq[...]))
    k = narrow(dot_nn(h1, wk[...]))
    v = narrow(dot_nn(h1, wv[...]))
    q_out[...] = q
    k_out[...] = k
    v_out[...] = v
    bias = head_bias(table[...].T, rows)
    allowed = causal_mask(rows)
    mixed = []
    for pair in range(pairs):
        at = slice(pair * 2 * HD, (pair + 1) * 2 * HD)
        scores = dot_nt(k[:, at], pair_mask(q[:, at]))
        both = jnp.concatenate(
            [toeplitz(bias[2 * pair : 2 * pair + 1], rows), toeplitz(bias[2 * pair + 1 : 2 * pair + 2], rows)],
            axis=1,
        )
        scores = jnp.where(allowed, scores + both, NEG)
        top = jnp.max(scores, axis=0, keepdims=True)
        raised = jnp.exp(scores - top)
        chances = raised / jnp.sum(raised, axis=0, keepdims=True)
        mixed.append(pair_diag(dot_tn(v[:, at], narrow(chances)), rows))
    mix = narrow(jnp.concatenate(mixed, axis=0).T)
    mix_out[...] = mix
    after = value + dot_nn(mix, wo[...])
    after_out[...] = after
    h2 = narrow(rms(after, g2[...]))
    h2_out[...] = h2
    cq_out[...] = narrow(dot_nn(h2, wcq[...]))


def cross_forward_kernel(slot, lengths, enc, wk, wv, cq, k_out, v_out, mix_out, lse_out, masked, top, total, acc):
    step = pl.program_id(0)
    rows, width = cq.shape
    block = enc.shape[0]
    pairs = width // (2 * HD)

    @pl.when(step == 0)
    def _():
        for pair in range(pairs):
            at = slice(pair * 2 * HD, (pair + 1) * 2 * HD)
            masked[pair] = pair_mask(cq[:, at])
        top[...] = jnp.full(top.shape, NEG, F32)
        total[...] = jnp.zeros(total.shape, F32)
        acc[...] = jnp.zeros(acc.shape, F32)

    source = enc[...]
    k_out[...] = narrow(dot_nn(source, wk[...]))
    v_out[...] = narrow(dot_nn(source, wv[...]))
    place = lax.broadcasted_iota(jnp.int32, (slot, 2 * rows), 0)
    passages = block // slot
    valid = jnp.concatenate([place < lengths[step * passages + i] for i in range(passages)], axis=0)
    for pair in range(pairs):
        at = slice(pair * 2 * HD, (pair + 1) * 2 * HD)
        scores = jnp.where(valid, dot_nt(k_out[:, at], masked[pair]), NEG)
        before = top[pair : pair + 1]
        now = jnp.maximum(before, jnp.max(scores, axis=0, keepdims=True))
        top[pair : pair + 1] = now
        fade = jnp.exp(before - now)
        raised = jnp.exp(scores - now)
        total[pair : pair + 1] = total[pair : pair + 1] * fade + jnp.sum(raised, axis=0, keepdims=True)
        part = pair_diag(dot_tn(v_out[:, at], narrow(raised)), rows)
        fades = jnp.concatenate(
            [jnp.broadcast_to(fade[:, :rows], (HD, rows)), jnp.broadcast_to(fade[:, rows:], (HD, rows))], axis=0
        )
        acc[at, :] = acc[at, :] * fades + part

    @pl.when(step == pl.num_programs(0) - 1)
    def _():
        for pair in range(pairs):
            at = slice(pair * 2 * HD, (pair + 1) * 2 * HD)
            sums = total[pair : pair + 1]
            lse_out[pair : pair + 1] = top[pair : pair + 1] + jnp.log(sums)
            inverse = 1.0 / sums
            spread = jnp.concatenate(
                [jnp.broadcast_to(inverse[:, :rows], (HD, rows)), jnp.broadcast_to(inverse[:, rows:], (HD, rows))],
                axis=0,
            )
            mix_out[at, :] = acc[at, :] * spread


def feed_kernel(
    mix_t, after_self, cot, wo, w_in, w_out, g3,
    result_out, grad_out, gmix_out, delta_out, dgain_out, d_in, d_out, d_o,
):
    rows, width = cot.shape
    hidden_units = w_in.shape[1]
    mix = narrow(mix_t[...].T)
    after = after_self[...] + dot_nn(mix, wo[...])
    h3 = narrow(rms(after, g3[...]))
    inner = dot_nn(h3, w_in[...])
    bent = jnp.tanh(ROOT * (inner + 0.044715 * (inner * inner * inner)))
    active = narrow(0.5 * inner * (1.0 + bent))
    result_out[...] = after + dot_nn(active, w_out[...])
    cb = cot[...]
    d_out[...] = narrow(dot_tn(active, cb))
    slope = 0.5 * (1.0 + bent) + (0.5 * ROOT) * inner * (1.0 - bent * bent) * (1.0 + (3 * 0.044715) * inner * inner)
    gi = narrow(dot_nt(cb, w_out[...]) * slope)
    pieces = hidden_units // width
    for piece in range(pieces):
        d_in[piece] = narrow(dot_tn(h3, gi[:, piece * width : (piece + 1) * width]))
    back, gain_grad = rms_back(after, g3[...], dot_nt(gi, w_in[...]))
    dgain_out[...] = gain_grad
    grad = cb.astype(F32) + back
    grad_out[...] = grad
    gb = narrow(grad)
    d_o[...] = narrow(dot_tn(mix, gb))
    gmix = narrow(dot_nt(gb, wo[...]))
    gmix_out[...] = gmix
    product = gmix.astype(F32).T * mix_t[...]
    for pair in range(width // (2 * HD)):
        first = jnp.sum(product[pair * 2 * HD : pair * 2 * HD + HD], axis=0, keepdims=True)
        second = jnp.sum(product[pair * 2 * HD + HD : (pair + 1) * 2 * HD], axis=0, keepdims=True)
        delta_out[pair : pair + 1] = jnp.concatenate([first, second], axis=1)


def cross_backward_kernel(
    slot, lengths, enc, k, v, wk, wv, cq, gmix, lse, delta,
    enc_out, dq_out, dk_out, dv_out, masked, gmasked, dq_t, dkv, acc,
):
    step = pl.program_id(0)
    rows, width = cq.shape
    block = enc.shape[0]
    pairs = width // (2 * HD)

    @pl.when(step == 0)
    def _():
        for pair in range(pairs):
            at = slice(pair * 2 * HD, (pair + 1) * 2 * HD)
            masked[pair] = pair_mask(cq[:, at])
            gmasked[pair] = pair_mask(gmix[:, at])
        dq_t[...] = jnp.zeros(dq_t.shape, F32)
        acc[...] = jnp.zeros(acc.shape, F32)

    place = lax.broadcasted_iota(jnp.int32, (slot, 2 * rows), 0)
    passages = block // slot
    valid = jnp.concatenate([place < lengths[step * passages + i] for i in range(passages)], axis=0)
    for pair in range(pairs):
        at = slice(pair * 2 * HD, (pair + 1) * 2 * HD)
        scores = jnp.where(valid, dot_nt(k[:, at], masked[pair]), NEG)
        chances = jnp.exp(scores - lse[pair : pair + 1])
        dkv[:, width + pair * 2 * HD : width + (pair + 1) * 2 * HD] = narrow(dot_nn(narrow(chances), gmasked[pair]))
        ds = narrow(chances * (dot_nt(v[:, at], gmasked[pair]) - delta[pair : pair + 1]))
        dkv[:, at] = narrow(dot_nn(ds, masked[pair]))
        dq_t[at, :] = dq_t[at, :] + pair_diag(dot_tn(k[:, at], ds), rows)
    enc_out[...] = narrow(dot_nt(dkv[:, :width], wk[...]) + dot_nt(dkv[:, width:], wv[...]))
    acc[...] = acc[...] + dot_tn(enc[...], dkv[...])

    @pl.when(step == pl.num_programs(0) - 1)
    def _():
        dq_out[...] = narrow(dq_t[...].T)
        dk_out[...] = narrow(acc[:, :width])
        dv_out[...] = narrow(acc[:, width:])


def self_backward_kernel(
    hidden, h1, q, k, v, mix, after_self, h2, dcq, grad_cross, wq, wk, wv, wo, wcq, g1, g2, table,
    hidden_out, d_cq, d_o, d_q, d_k, d_v, dg1_out, dg2_out, dtable_out,
):
    rows, width = hidden.shape
    pairs = width // (2 * HD)
    d_cq[...] = narrow(dot_tn(h2[...], dcq[...]))
    back, gain_grad = rms_back(after_self[...], g2[...], dot_nt(dcq[...], wcq[...]))
    dg2_out[...] = gain_grad
    grad = grad_cross[...] + back
    sb = narrow(grad)
    d_o[...] = narrow(dot_tn(mix[...], sb))
    gmix = narrow(dot_nt(sb, wo[...]))
    bias = head_bias(table[...].T, rows)
    allowed = causal_mask(rows)
    dq_parts, dk_parts, dv_parts, sums = [], [], [], []
    for pair in range(pairs):
        at = slice(pair * 2 * HD, (pair + 1) * 2 * HD)
        masked = pair_mask(q[:, at])
        gmasked = pair_mask(gmix[:, at])
        scores = dot_nt(k[:, at], masked)
        both = jnp.concatenate(
            [toeplitz(bias[2 * pair : 2 * pair + 1], rows), toeplitz(bias[2 * pair + 1 : 2 * pair + 2], rows)],
            axis=1,
        )
        scores = jnp.where(allowed, scores + both, NEG)
        top = jnp.max(scores, axis=0, keepdims=True)
        raised = jnp.exp(scores - top)
        chances = raised / jnp.sum(raised, axis=0, keepdims=True)
        dv_parts.append(narrow(dot_nn(narrow(chances), gmasked)))
        dp = dot_nt(v[:, at], gmasked)
        ds = chances * (dp - jnp.sum(chances * dp, axis=0, keepdims=True))
        sums.append(diagonal_sums(ds[:, :rows]))
        sums.append(diagonal_sums(ds[:, rows:]))
        dsb = narrow(ds)
        dk_parts.append(narrow(dot_nn(dsb, masked)))
        dq_parts.append(pair_diag(dot_tn(k[:, at], dsb), rows))
    dq = narrow(jnp.concatenate(dq_parts, axis=0).T)
    dk = jnp.concatenate(dk_parts, axis=1)
    dv = jnp.concatenate(dv_parts, axis=1)
    d_q[...] = narrow(dot_tn(h1[...], dq))
    d_k[...] = narrow(dot_tn(h1[...], dk))
    d_v[...] = narrow(dot_tn(h1[...], dv))
    into = dot_nt(dq, wq[...]) + dot_nt(dk, wk[...]) + dot_nt(dv, wv[...])
    back, gain_grad = rms_back(hidden[...].astype(F32), g1[...], into)
    dg1_out[...] = gain_grad
    hidden_out[...] = grad + back
    by_distance = jnp.concatenate(sums, axis=0)
    onehot = bucket_onehot_rows(table.shape[0], rows)
    dtable_out[...] = lax.dot_general(
        onehot, by_distance, (((1,), (1,)), ((), ())), precision=lax.Precision.HIGHEST, preferred_element_type=F32
    )


def halving_order(bits, piece):
    first = list(range(bits))
    if sum(other in PLANES_FIRST for other in range(piece + 1)) % 2 != piece % 2:
        first[0], first[1] = first[1], first[0]
    return first[2:] + first[:2] if piece in PLANES_FIRST else first


class Inputs(NamedTuple):
    lengths: Any
    encodings: Any
    wq: Any
    wk: Any
    wv: Any
    wo: Any
    wcq: Any
    wck: Any
    wcv: Any
    wco: Any
    w_in: Any
    w_out: Any
    hidden: Any
    cot: Any
    g1: Any
    g2: Any
    g3: Any
    table: Any


class Outputs(NamedTuple):
    result: Any
    hidden: Any
    enc: Any
    squares: Any
    fin: Any
    fout: Any
    gains: Any
    table: Any


class Scratch(NamedTuple):
    left_self: Any
    left_feed: Any
    right: Any
    give: Any
    late: Any
    late_give: Any
    enc: Any
    keys: Any
    values: Any
    queries: Any
    grads: Any
    stats: Any
    weights: Any
    masked: Any
    gmasked: Any
    acc: Any
    q: Any
    k: Any
    v: Any
    after_self: Any
    grad_cross: Any
    top: Any
    lse: Any
    delta: Any
    swap_give: Any
    swap_take: Any
    mine: Any
    last_own: Any
    last_other: Any
    out_result: Any
    out_hidden: Any
    out_squares: Any
    out_fin: Any
    out_fout: Any
    small_give: Any
    small_take: Any
    small_sum: Any
    load: Any
    pair_send: Any
    pair_recv: Any
    sum_send: Any
    sum_recv: Any
    in_send: Any
    in_recv: Any
    all_send: Any
    line_recv: Any
    first_recv: Any
    plane_recv: Any
    own: Any
    out: Any
    small_send: Any
    small_recv: Any
    last_send: Any
    last_recv: Any


CO, CQ, SO, SQ, SK, SV, CK, CV = range(8)


def layer_kernel(n, slot, count_in, count_out, *refs):
    bits = n.bit_length() - 1
    ins = Inputs(*refs[: len(Inputs._fields)])
    outs = Outputs(*refs[len(ins) : len(ins) + len(Outputs._fields)])
    scratch = refs[len(ins) + len(outs) :]
    r, stages = Scratch(*scratch[: len(Scratch._fields)]), scratch[len(Scratch._fields) :]
    mine, weights = r.mine, r.weights
    share, half = mine.shape[2], mine.shape[3] // 2
    pieces = 2 * mine.shape[0]
    rows, width = ins.hidden.shape
    units = count_out * width
    span = count_in * half
    pairs = width // (2 * HD)
    two = 2 * HD
    line = n // 4
    me, core = lax.axis_index(PASS), lax.axis_index(CORE)
    low = me % 4
    partner = (me, 1 - core)
    wq, wk, wv, wo, wcq, wck, wcv, wco = (weights.at[i] for i in range(8))
    g1, g2, g3 = (g[...].reshape(1, width) for g in (ins.g1, ins.g2, ins.g3))

    def remote(src, dst, send, recv, device):
        return pltpu.make_async_remote_copy(
            src_ref=src, dst_ref=dst, send_sem=send, recv_sem=recv, device_id=device, device_id_type=MESH
        )

    def all_sent(like, sem):
        remote(like, like, sem, sem, partner).wait_send()

    def all_come(like, sem):
        remote(like, like, sem, sem, partner).wait_recv()

    def by_core(body):
        for c in range(2):
            pl.when(core == c)(functools.partial(body, c))

    def columns(pair):
        return slice(pair * two, (pair + 1) * two)

    parts = units // width
    loads = [(w, weights.at[i]) for i, w in enumerate(ins[2:10])]
    tiles = mine.reshape(2 * parts, width, width)
    for j in range(parts):
        at = slice(j * width, (j + 1) * width)
        loads += [(ins.w_in.at[:, at], tiles.at[j]), (ins.w_out.at[at], tiles.at[parts + j])]

    def load(i):
        return pltpu.make_async_copy(loads[i][0], loads[i][1], r.load.at[i])

    for i in range(8):
        load(i).start()

    barrier = pltpu.get_barrier_semaphore()
    pl.semaphore_signal(barrier, inc=1, device_id=partner, device_id_type=MESH)

    def greet(d, carry):
        pl.semaphore_signal(barrier, inc=1, device_id=(me ^ d, core), device_id_type=MESH)
        return carry

    lax.fori_loop(1, n, greet, 0)
    pl.semaphore_wait(barrier, n)

    def passage_at(p):
        return pl.ds(pl.multiple_of(p * slot, slot), slot)

    def bring(q):
        return remote(ins.encodings.at[q], r.enc.at[passage_at(me)], r.in_send.at[0], r.in_recv.at[me], (q, core))

    def arrived(p):
        return remote(ins.encodings.at[p], r.enc.at[passage_at(p)], r.in_send.at[0], r.in_recv.at[p], (p, core))

    def bring_range(first, last):
        def one(d, carry):
            bring(me ^ d).start()
            return carry

        lax.fori_loop(first, last, one, 0)

    bring_range(1, 4)
    own_passage = pltpu.make_async_copy(ins.encodings.at[me], r.enc.at[passage_at(me)], r.own.at[0])
    own_passage.start()
    for i in range(8, len(loads)):
        load(i).start()

    x_peer, y_peer = (me ^ 1, core), (me ^ 2, core)

    steps_of_line = [[k for k in range(1, line) if k.bit_count() == hops] for hops in range(1, bits - 1)]
    line_bits = len(steps_of_line)

    def line_copy(kind, k):
        last = k & -k
        origin = me ^ (4 * (k ^ last))
        ref = r.stats.at[origin] if kind == 2 else (r.queries, r.grads)[kind].at[:, origin]
        return remote(ref, ref, r.all_send.at[kind], r.line_recv.at[kind, k - 1], (me ^ (4 * last), core))

    def spread_line(kind, number):
        if number:
            for k in steps_of_line[number - 1]:
                line_copy(kind, k).wait_recv()
        for k in reversed(steps_of_line[number]) if number < line_bits else ():
            line_copy(kind, k).start()

    def plane_copy(kind, number, k):
        part = number % 2
        first, second = (x_peer, y_peer) if part == 0 else (y_peer, x_peer)
        origin = me ^ (4 * k) if number < 4 else me ^ (4 * k) ^ (1 << part)
        at = (r.queries, r.grads)[kind].at[part, origin]
        recv = r.first_recv.at[kind, number, k] if number < 2 else r.plane_recv.at[kind]
        return remote(at, at, r.all_send.at[kind], recv, first if number < 2 else second)

    def stat_plane(d):
        view = r.stats.reshape(line, 4, *r.stats.shape[1:]).at[:, low]
        return remote(view, view, r.all_send.at[2], r.plane_recv.at[2], (me ^ d, core))

    def spread_plane(kind, blocks):
        for number in range(4):
            for k in blocks:
                plane_copy(kind, number, k).start()

    def spread_rest(kind, blocks):
        for k in blocks:
            for number in range(2):
                plane_copy(kind, number, k).wait_recv()
        for k in blocks:
            for number in range(4, 6):
                plane_copy(kind, number, k).start()

    def spread_taken(kind):
        like = r.stats.at[: 3 * line] if kind == 2 else r.grads.at[:, : 2 * line]
        all_come(like, r.plane_recv.at[kind])

    def spread_sent(kind):
        like = r.stats.at[: 4 * line - 1] if kind == 2 else r.grads.at[:, : 4 * line - 1]
        all_sent(like, r.all_send.at[kind])

    ready = (
        (r.out_result, outs.result), (r.out_hidden, outs.hidden), (r.out_squares, outs.squares), (r.out_fin, outs.fin),
        (r.out_fout, outs.fout),
    )

    def give_out(i):
        return pltpu.make_async_copy(*ready[i], r.out.at[2 + i])

    value = ins.hidden[...].astype(F32)
    h1 = narrow(rms(value, g1))
    r.left_self[0, :, :width] = h1
    for i, ref in enumerate((r.q, r.k, r.v)):
        load(i).wait()
        ref[...] = narrow(dot_nn(h1, weights[i]))
    bias = head_bias(ins.table[...], rows)
    allowed = causal_mask(rows)

    def self_chances(pair):
        at = columns(pair)
        masked = pair_mask(r.q[:, at])
        scores = dot_nt(r.k[:, at], masked)
        both = jnp.concatenate([toeplitz(bias[2 * pair + i : 2 * pair + i + 1], rows) for i in range(2)], axis=1)
        scores = jnp.where(allowed, scores + both, NEG)
        raised = jnp.exp(scores - jnp.max(scores, axis=0, keepdims=True))
        return at, masked, raised / jnp.sum(raised, axis=0, keepdims=True)

    for pair in range(pairs):
        at, _, chances = self_chances(pair)
        r.acc[at, :] = pair_diag(dot_tn(r.v[:, at], narrow(chances)), rows)
    mix1 = narrow(r.acc[...].T)
    r.left_self[0, :, 2 * width :] = mix1
    load(3).wait()
    after_self = value + dot_nn(mix1, wo[...])
    r.after_self[...] = after_self
    h2 = narrow(rms(after_self, g2))
    r.left_self[0, :, width : 2 * width] = h2
    load(4).wait()
    cq = narrow(dot_nn(h2, wcq[...]))
    for c in range(2):
        r.queries[c, me] = cq[:, c * half : (c + 1) * half]
    spread_line(0, 0)
    bring_range(n // 2, 3 * n // 4)
    for pair in range(pairs):
        r.masked[pair] = pair_mask(cq[:, columns(pair)])
    r.top[...] = jnp.full(r.top.shape, NEG, F32)
    r.lse[...] = jnp.zeros(r.lse.shape, F32)
    r.acc[...] = jnp.zeros(r.acc.shape, F32)

    def pair_copy(i):
        src = (r.left_self.at[0], r.left_feed.at[0], r.give)[i]
        dst = (r.left_self, r.left_feed, r.right)[i].at[1]
        return remote(src, dst, r.pair_send.at[i], r.pair_recv.at[i], partner)

    pair_copy(0).start()

    place = lax.broadcasted_iota(jnp.int32, (slot, 2 * rows), 0)

    def spread(row):
        return jnp.concatenate(
            [jnp.broadcast_to(row[:, :rows], (HD, rows)), jnp.broadcast_to(row[:, rows:], (HD, rows))], axis=0
        )

    load(5).wait()
    load(6).wait()
    own_passage.wait()
    few = 1
    turns = n // few

    def forward_block(turn, carry):
        @pl.when(turn == turns // 8)
        def _():
            for number in range(1, line_bits):
                spread_line(0, number)
            bring_range(3 * n // 4, n)
            bring_range(4, n // 2)

        @pl.when(turn == 3 * turns // 8)
        def _():
            spread_line(0, line_bits)
            spread_plane(0, range(line))

        pl.when(turn == 3 * turns // 4)(functools.partial(spread_rest, 0, range(line)))
        part = turn // (turns // 4)
        moved = turn % (turns // 4) + (part % 2 * 2 + part // 2) * (turns // 4)
        first = (moved ^ (me // few)) * few
        for i in range(few):

            @pl.when(first + i != me)
            def _(i=i):
                arrived(first + i).wait_recv()

        at = pl.ds(pl.multiple_of(first * slot, few * slot), few * slot)
        source = r.enc[at]
        r.keys[at] = narrow(dot_nn(source, wck[...]))
        r.values[at] = narrow(dot_nn(source, wcv[...]))
        valid = jnp.concatenate([place < ins.lengths[first + i] for i in range(few)], axis=0)
        for pair in range(pairs):
            cols = columns(pair)
            scores = jnp.where(valid, dot_nt(r.keys[at, cols], r.masked[pair]), NEG)
            before = r.top[pair : pair + 1]
            now = jnp.maximum(before, jnp.max(scores, axis=0, keepdims=True))
            r.top[pair : pair + 1] = now
            fade = jnp.exp(before - now)
            raised = jnp.exp(scores - now)
            r.lse[pair : pair + 1] = r.lse[pair : pair + 1] * fade + jnp.sum(raised, axis=0, keepdims=True)
            part = pair_diag(dot_tn(r.values[at, cols], narrow(raised)), rows)
            r.acc[cols, :] = r.acc[cols, :] * spread(fade) + part
        return carry

    lax.fori_loop(0, turns, forward_block, 0)
    for pair in range(pairs):
        cols = columns(pair)
        sums = r.lse[pair : pair + 1]
        r.lse[pair : pair + 1] = r.top[pair : pair + 1] + jnp.log(sums)
        r.acc[cols, :] = r.acc[cols, :] * spread(1.0 / sums)

    own_load = pltpu.make_async_copy(ins.encodings, r.enc.reshape(n, slot, width), r.own.at[0])
    own_load.start()
    mix2 = narrow(r.acc[...].T)
    r.left_feed[0, :, units + width :] = mix2
    load(7).wait()
    after_cross = r.after_self[...] + dot_nn(mix2, wco[...])
    h3 = narrow(rms(after_cross, g3))
    r.left_feed[0, :, units : units + width] = h3
    cb = ins.cot[...]
    result = after_cross
    into = jnp.zeros((rows, width), F32)
    products = {}

    def ahead_of(j):
        if j < parts:
            load(8 + 2 * j).wait()
            load(9 + 2 * j).wait()
            products[j] = dot_nn(h3, tiles[j]), dot_nt(cb, tiles[parts + j])

    ahead_of(0)
    for j in range(parts):
        ahead_of(j + 1)
        inner, back = products.pop(j)
        bent = jnp.tanh(ROOT * (inner + 0.044715 * (inner * inner * inner)))
        active = narrow(0.5 * inner * (1.0 + bent))
        r.left_feed[0, :, j * width : (j + 1) * width] = active
        slope = 0.5 * (1.0 + bent) + (0.5 * ROOT) * inner * (1.0 - bent * bent) * (1.0 + (3 * 0.044715) * inner * inner)
        gi = narrow(back * slope)
        into = into + dot_nt(gi, tiles[j])
        result = result + dot_nn(active, tiles[parts + j])
        to = slice((j % (parts // 2)) * width, (j % (parts // 2) + 1) * width)

        def keep(c, gi=gi, to=to, owner=j // (parts // 2)):
            if c == owner:
                r.right[0, :, to] = gi
            else:
                r.give[:, to] = gi

        by_core(keep)
    r.out_result[...] = result
    give_out(0).start()
    pair_copy(1).start()
    back, dg3 = rms_back(after_cross, g3, into)
    grad = cb.astype(F32) + back
    r.grad_cross[...] = grad
    gb = narrow(grad)

    def keep_columns(c):
        for j, value in enumerate((cb, gb)):
            to = slice(span + j * half, span + (j + 1) * half)
            r.right[0, :, to] = value[:, c * half : (c + 1) * half]
            r.give[:, to] = value[:, (1 - c) * half : (2 - c) * half]

    by_core(keep_columns)
    pair_copy(2).start()
    gmix = narrow(dot_nt(gb, wco[...]))
    for c in range(2):
        r.grads[c, me] = gmix[:, c * half : (c + 1) * half]
    spread_line(1, 0)
    spread_plane(1, [0])
    product = gmix.astype(F32).T * r.acc[...]
    for pair in range(pairs):
        at = columns(pair)
        r.gmasked[pair] = pair_mask(gmix[:, at])
        part = product[at]
        r.delta[pair : pair + 1] = jnp.concatenate(
            [jnp.sum(part[:HD], axis=0, keepdims=True), jnp.sum(part[HD:], axis=0, keepdims=True)], axis=1
        )
    lane = lax.broadcasted_iota(jnp.int32, (1, 2 * rows), 1)
    extent = jnp.zeros((1, 2 * rows), F32)
    for p in range(n):
        extent = jnp.where(lane == p, ins.lengths[p].astype(F32), extent)
    r.stats[me, :pairs] = r.lse[...]
    r.stats[me, pairs : 2 * pairs] = r.delta[...]
    r.stats[me, 2 * pairs : 2 * pairs + 1] = extent
    spread_line(2, 0)
    r.acc[...] = jnp.zeros(r.acc.shape, F32)

    def lanes(piece):
        return slice((piece % 2) * half, (piece % 2 + 1) * half)

    def split(piece, stage):
        done = halving_order(bits, piece)[:stage]
        bit = halving_order(bits, piece)[stage]
        inner = 1 << len([b for b in range(bit) if b not in done])
        outer = (n >> stage) // (2 * inner)

        def half_of(value):
            if stage:
                return stages[stage - 1].reshape(pieces, outer, 2, inner, share, half).at[piece, :, value]
            return mine.reshape(pieces // 2, outer, 2, inner, share, 2 * half).at[piece // 2, :, value, :, :, lanes(piece)]

        return half_of, (me >> bit) & 1, inner, outer, bit

    def stage_copy(piece, stage):
        half_of, value, inner, outer, bit = split(piece, stage)
        dst = stages[stage].at[piece].reshape(outer, inner, share, half)
        sems = r.sum_send.at[0], r.sum_recv.at[piece, stage]
        return remote(half_of(1 - value), dst, *sems, (me ^ (1 << bit), core))

    first_square = count_in + count_out
    square_places = (7, 4, 3, 0, 1, 2, 5, 6)

    def put(piece, c, total):
        if piece < count_in:
            r.out_fin[:, (c * count_in + piece) * half : (c * count_in + piece + 1) * half] = total
        elif piece < first_square:
            k = piece - count_in
            r.out_fout[k * share : (k + 1) * share, c * half : (c + 1) * half] = total
        else:
            r.out_squares[square_places[piece - first_square], :, c * half : (c + 1) * half] = total

    def last_copy(piece):
        return remote(r.last_own.at[piece], r.last_other.at[piece], r.last_send.at[0], r.last_recv.at[0], partner)

    def begin(piece):
        stage_copy(piece, 0).start()

    def arrive(piece, stage):
        stage_copy(piece, stage).wait_recv()
        half_of, value, inner, outer, _ = split(piece, stage)
        kept = half_of(value)
        dst = stages[stage].at[piece]
        if stage + 1 < bits:

            def one(i, carry):
                dst[i] = narrow(kept[i // inner, i % inner].astype(F32) + dst[i].astype(F32))
                return carry

            lax.fori_loop(0, outer * inner, one, 0)
            stage_copy(piece, stage + 1).start()
        else:
            total = kept[0, 0].astype(F32) + dst[0].astype(F32)
            r.last_own[piece] = narrow(total)
            last_copy(piece).start()
            by_core(lambda c: put(piece, c, total))

    def owners(value):
        return narrow(value).reshape(n, share, half)

    def keep_piece(piece, value):
        mine[piece // 2, :, :, lanes(piece)] = value

    for i in range(3):
        pair_copy(i).wait_recv()
    left_self, left_feed, right = (x.reshape(2 * rows, x.shape[2]) for x in (r.left_self, r.left_feed, r.right))
    early = [piece for piece in range(first_square) if piece not in PLANES_FIRST]
    for piece in range(count_in):
        keep_piece(piece, owners(dot_tn(left_feed[:, units : units + width], right[:, piece * half : (piece + 1) * half])))
        if piece in early[:2]:
            begin(piece)
    per = width // (count_out * share)
    for part in range(count_out):
        value = narrow(dot_tn(left_feed[:, part * width : (part + 1) * width], right[:, span : span + half]))
        value = value.reshape(per, count_out, share, half)
        for k in range(count_out):
            piece = count_in + k
            mine[piece // 2, part * per : (part + 1) * per, :, lanes(piece)] = value[:, k]
    keep_piece(first_square + CO, owners(dot_tn(left_feed[:, units + width :], right[:, span + half :])))
    for piece in early[2:]:
        begin(piece)

    many = 4

    def question_block(turn, carry):
        at = pl.ds(pl.multiple_of(turn * many * slot, many * slot), many * slot)
        valid = jnp.concatenate([place < ins.lengths[turn * many + i] for i in range(many)], axis=0)
        for pair in range(pairs):
            cols = columns(pair)
            key = r.keys[at, cols]
            scores = jnp.where(valid, dot_nt(key, r.masked[pair]), NEG)
            chances = jnp.exp(scores - r.lse[pair : pair + 1])
            ds = narrow(chances * (dot_nt(r.values[at, cols], r.gmasked[pair]) - r.delta[pair : pair + 1]))
            r.acc[cols, :] = r.acc[cols, :] + pair_diag(dot_tn(key, ds), rows)
        return carry

    lax.fori_loop(0, n // (2 * many), question_block, 0)

    for number in range(1, line_bits):
        spread_line(1, number)
        spread_line(2, number)
        spread_plane(1, steps_of_line[number - 1])
    for piece in PLANES_FIRST:
        if piece < first_square:
            begin(piece)
    lax.fori_loop(n // (2 * many), n // many, question_block, 0)

    late = (CQ, SO, SQ, SK, SV)
    lefts = (width, 2 * width, 0, 0, 0)

    def late_copy(i):
        return remote(r.late_give.at[i], r.late.at[i, 1], r.pair_send.at[3], r.pair_recv.at[3 + i], partner)

    def late_give(name, value):
        i = late.index(name)

        def part(c):
            r.late[i, 0] = value[:, c * half : (c + 1) * half]
            r.late_give[i] = value[:, (1 - c) * half : (2 - c) * half]

        by_core(part)
        late_copy(i).start()

    def late_take(name, now=True):
        i = late.index(name)
        late_copy(i).wait_recv()
        left = left_self[:, lefts[i] : lefts[i] + width]
        keep_piece(first_square + name, owners(dot_tn(left, r.late.at[i].reshape(2 * rows, half)[...])))
        if now:
            begin(first_square + name)

    dcq = narrow(r.acc[...].T)
    late_give(CQ, dcq)
    back, dg2 = rms_back(r.after_self[...], g2, dot_nt(dcq, wcq[...]))
    grad = r.grad_cross[...] + back
    sb = narrow(grad)
    late_give(SO, sb)

    own_load.wait()

    def project(turn, carry):
        at = pl.ds(pl.multiple_of(turn * many * slot, many * slot), many * slot)
        source = r.enc[at]
        r.keys[at] = narrow(dot_nn(source, wck[...]))
        r.values[at] = narrow(dot_nn(source, wcv[...]))
        return carry

    lax.fori_loop(0, n // (2 * many), project, 0)
    spread_rest(1, [0])
    spread_line(1, line_bits)
    spread_plane(1, steps_of_line[-1])
    spread_line(2, line_bits)
    for d in range(1, 4):
        stat_plane(d).start()
    for ks in steps_of_line[:-1]:
        spread_rest(1, ks)
    lax.fori_loop(n // (2 * many), n // many, project, 0)
    late_take(CQ, False)

    gself = narrow(dot_nt(sb, wo[...]))
    dq_parts, dk_parts, dv_parts, sums = [], [], [], []
    for pair in range(pairs):
        at, masked, chances = self_chances(pair)
        gmasked = pair_mask(gself[:, at])
        dv_parts.append(narrow(dot_nn(narrow(chances), gmasked)))
        dp = dot_nt(r.v[:, at], gmasked)
        ds = chances * (dp - jnp.sum(chances * dp, axis=0, keepdims=True))
        sums.append(diagonal_sums(ds[:, :rows]))
        sums.append(diagonal_sums(ds[:, rows:]))
        dsb = narrow(ds)
        dk_parts.append(narrow(dot_nn(dsb, masked)))
        dq_parts.append(pair_diag(dot_tn(r.k[:, at], dsb), rows))
    dq = narrow(jnp.concatenate(dq_parts, axis=0).T)
    dk = jnp.concatenate(dk_parts, axis=1)
    dv = jnp.concatenate(dv_parts, axis=1)
    late_give(SQ, dq)
    late_give(SK, dk)
    late_give(SV, dv)
    late_take(SO, False)
    into = dot_nt(dq, wq[...]) + dot_nt(dk, wk[...]) + dot_nt(dv, wv[...])
    late_take(SQ, False)
    late_take(SK, False)
    late_take(SV, False)
    back, dg1 = rms_back(ins.hidden[...].astype(F32), g1, into)
    r.out_hidden[...] = grad + back
    give_out(1).start()
    onehot = bucket_onehot_rows(ins.table.shape[1], rows)
    dtable = lax.dot_general(
        jnp.concatenate(sums, axis=0), onehot, (((1,), (1,)), ((), ())), precision=lax.Precision.HIGHEST,
        preferred_element_type=F32,
    )

    heads, buckets = dtable.shape
    per_row = 128 // buckets
    table_rows = [
        jnp.concatenate([dtable[i + j : i + j + 1] for j in range(per_row)], axis=1) for i in range(0, heads, per_row)
    ]
    terms = jnp.concatenate([dg1, dg2, dg3], axis=0)
    for o in range(n):
        r.small_give[o, :3, :share] = terms[:, o * share : (o + 1) * share]
        r.small_give[o, 3 : 3 + len(table_rows)] = jnp.concatenate(table_rows, axis=0)
    r.small_take[me] = r.small_give[me]

    def small_copy(device):
        return remote(r.small_give.at[device], r.small_take.at[me], r.small_send.at[0], r.small_recv.at[0], (device, core))

    def small_one(d, carry):
        small_copy(me ^ d).start()
        return carry

    lax.fori_loop(1, n, small_one, 0)

    def small_pair():
        return remote(r.small_sum.at[0], r.small_sum.at[1], r.small_send.at[1], r.small_recv.at[1], partner)

    def small_add():
        all_come(r.small_take.at[: n - 1], r.small_recv.at[0])
        total = r.small_take[0]
        for o in range(1, n):
            total = total + r.small_take[o]
        r.small_sum[0] = total
        small_pair().start()

    def small_end():
        small_pair().wait_recv()
        total = r.small_sum[0] + r.small_sum[1]
        for i in range(3):
            outs.gains[i] = total[i : i + 1, :share]
        for i in range(len(table_rows)):
            for j in range(per_row):
                outs.table[i * per_row + j : i * per_row + j + 1] = total[3 + i : 4 + i, j * buckets : (j + 1) * buckets]

    place_f = place.astype(F32)

    def owner_block(turn, carry):
        q = (turn % line) * 4 + (low ^ (turn // line))
        at = passage_at(q)
        stats = r.stats[q]
        extent = jnp.sum(jnp.where(lane == me, stats[2 * pairs : 2 * pairs + 1], 0.0), axis=1, keepdims=True)
        valid = place_f < extent
        for pair in range(pairs):
            cols = columns(pair)
            c, within = pair // (pairs // 2), columns(pair % (pairs // 2))
            masked, gmasked = pair_mask(r.queries[c, q, :, within]), pair_mask(r.grads[c, q, :, within])
            scores = jnp.where(valid, dot_nt(r.keys[at, cols], masked), NEG)
            chances = jnp.exp(scores - stats[pair : pair + 1])
            ds = narrow(chances * (dot_nt(r.values[at, cols], gmasked) - stats[pairs + pair : pairs + pair + 1]))
            r.values[at, cols] = narrow(dot_nn(narrow(chances), gmasked))
            r.keys[at, cols] = narrow(dot_nn(ds, masked))
        return carry

    spread_rest(1, steps_of_line[-1])

    middle, last = range(first_square, first_square + CK), range(first_square + CK, pieces)

    def taken_up(event):
        piece, stage = event
        if piece in early:
            keys = (0.0, 1.1, 3.0, 4.3)
        elif piece in last:
            keys = (3.5, 3.8, 4.2, 4.9)
        elif piece not in middle:
            keys = (0.5 if piece < count_in else 1.0, 3.3, 3.9, 4.4)
        elif piece in PLANES_FIRST:
            keys = (3.25, 3.75, 4.1, 4.7)
        elif piece == first_square + SV:
            keys = (3.05, 3.85, 4.25, 4.75)
        elif piece == first_square + SK:
            keys = (3.05, 3.58, 4.02, 4.65)
        else:
            keys = (2.0, 3.1, 3.6, 4.6)
        return keys[min(stage, 2)] if stage + 1 < bits else keys[3]

    events = sorted(((piece, stage) for piece in range(pieces) for stage in range(bits)), key=taken_up)
    visits = [[event for event in events if min(int(taken_up(event)), 3) == visit] for visit in range(4)]
    for piece, stage in visits[0]:
        arrive(piece, stage)
    for piece in middle:
        begin(piece)

    lax.fori_loop(0, line, owner_block, 0)

    spread_taken(0)
    spread_taken(1)
    spread_taken(2)
    lax.fori_loop(line, 2 * line, owner_block, 0)
    for piece, stage in visits[1]:
        arrive(piece, stage)
    lax.fori_loop(2 * line, n, owner_block, 0)
    for piece, stage in visits[2]:
        arrive(piece, stage)

    def encoding_block(turn):
        at = slice(turn * many * slot, (turn + 1) * many * slot)
        value = narrow(dot_nt(r.keys[at], wck[...]) + dot_nt(r.values[at], wcv[...]))
        for c in range(2):
            to = slice(turn * many, (turn + 1) * many)
            r.grads[c, to] = value[:, c * half : (c + 1) * half].reshape(many, slot, half)

    def out_copy(c):
        return pltpu.make_async_copy(r.grads.at[c], outs.enc.at[:, :, c * half : (c + 1) * half], r.out.at[c])

    for kind in range(3):
        spread_sent(kind)

    def swap_copy(i):
        return remote(r.swap_give.at[i], r.swap_take.at[i], r.pair_send.at[4], r.pair_recv.at[8 + i], partner)

    def columns_of(ref, c):
        return owners(dot_tn(r.enc[...], ref[:, pl.ds(pl.multiple_of(c * half, 128), half)]))

    for i, ref in enumerate((r.keys, r.values)):
        r.swap_give[i] = columns_of(ref, 1 - core)
        swap_copy(i).start()
    for i, (name, ref) in enumerate(((CK, r.keys), (CV, r.values))):
        piece = first_square + name
        keep_piece(piece, columns_of(ref, core))
        swap_copy(i).wait_recv()

        def one(o, carry, i=i, to=mine.at[piece // 2, :, :, lanes(piece)]):
            to[o] = narrow(to[o].astype(F32) + r.swap_take[i, o].astype(F32))
            return carry

        lax.fori_loop(0, n, one, 0)
        begin(piece)

    rest = visits[3]
    for number, (piece, stage) in enumerate(rest):
        if (piece, stage) == (last[0], 0):
            for turn in range(n // many):
                encoding_block(turn)
            for c in range(2):
                out_copy(c).start()
        arrive(piece, stage)
        if (piece, stage) == (last[1], 0):
            small_add()
    small_end()

    all_come(r.last_other, r.last_recv.at[0])
    for piece in range(pieces):
        total = r.last_other[piece].astype(F32)
        by_core(lambda c: put(piece, 1 - c, total))
        if piece in (count_in - 1, first_square - 1, pieces - 1):
            give_out(3 if piece < count_in else 4 if piece < first_square else 2).start()

    for i in range(len(ready)):
        give_out(i).wait()
    for c in range(2):
        out_copy(c).wait()

    all_sent(r.enc.at[: (n - 1) * slot], r.in_send.at[0])
    for i in range(3):
        pair_copy(i).wait_send()
    all_sent(r.late_give, r.pair_send.at[3])
    all_sent(r.swap_give, r.pair_send.at[4])
    all_sent(mine.at[:, : n - 1], r.sum_send.at[0])
    all_sent(r.last_own, r.last_send.at[0])
    all_sent(r.small_give.at[: n - 1], r.small_send.at[0])
    all_sent(r.small_sum.at[0], r.small_send.at[1])


def layer(n, slot, args):
    rows, width = args.hidden.shape
    units = args.w_in.shape[1]
    share, half = width // n, width // 2
    bits = n.bit_length() - 1
    pairs = width // (2 * HD)
    keys = n * slot
    count_in = count_out = units // width
    pieces = 8 + count_in + count_out
    table = args.table.shape
    vmem, hbm = pl.BlockSpec(memory_space=pltpu.VMEM), pl.BlockSpec(memory_space=pl.ANY)
    in_specs = [pl.BlockSpec(memory_space=pltpu.SMEM)] + [hbm] * 11 + [vmem] * 6
    wide = jax.ShapeDtypeStruct((rows, width), F32)
    results = Outputs(
        result=wide, hidden=wide, enc=jax.ShapeDtypeStruct((n, slot, width), BF),
        squares=jax.ShapeDtypeStruct((8, share, width), F32), fin=jax.ShapeDtypeStruct((share, units), F32),
        fout=jax.ShapeDtypeStruct((count_out * share, width), F32), gains=jax.ShapeDtypeStruct((3, 1, share), F32),
        table=jax.ShapeDtypeStruct(table, F32),
    )
    dma = pltpu.SemaphoreType.DMA
    sixteen, full = pltpu.VMEM((rows, width), BF), pltpu.VMEM((rows, width), F32)
    stat, masks = pltpu.VMEM((pairs, 2 * rows), F32), pltpu.VMEM((pairs, 2 * rows, 2 * HD), BF)
    blocks, shared = pltpu.VMEM((keys, width), BF), pltpu.VMEM((2, n, rows, half), BF)
    swap = pltpu.VMEM((2, n, share, half), BF)
    last = pltpu.VMEM((pieces, share, half), BF)
    up = lambda count: -(-count // 8) * 8
    small_rows = up(3 + table[0] * table[1] // 128)
    scratch = Scratch(
        left_self=pltpu.VMEM((2, rows, 3 * width), BF),
        left_feed=pltpu.VMEM((2, rows, units + 2 * width), BF),
        right=pltpu.VMEM((2, rows, units // 2 + width), BF),
        give=pltpu.VMEM((rows, units // 2 + width), BF),
        late=pltpu.VMEM((5, 2, rows, half), BF),
        late_give=pltpu.VMEM((5, rows, half), BF),
        enc=blocks, keys=blocks, values=blocks, queries=shared, grads=shared,
        stats=pltpu.VMEM((n, up(2 * pairs + 1), 2 * rows), F32),
        weights=pltpu.VMEM((8, width, width), BF),
        masked=masks, gmasked=masks,
        acc=pltpu.VMEM((width, rows), F32),
        q=sixteen, k=sixteen, v=sixteen, after_self=full, grad_cross=full,
        top=stat, lse=stat, delta=stat, swap_give=swap, swap_take=swap,
        mine=pltpu.VMEM((pieces // 2, n, share, width), BF),
        last_own=last, last_other=last,
        out_result=full, out_hidden=full,
        out_squares=pltpu.VMEM((8, share, width), F32),
        out_fin=pltpu.VMEM((share, units), F32),
        out_fout=pltpu.VMEM((count_out * share, width), F32),
        small_give=pltpu.VMEM((n, small_rows, 128), F32), small_take=pltpu.VMEM((n, small_rows, 128), F32),
        small_sum=pltpu.VMEM((2, small_rows, 128), F32),
        load=dma((8 + 2 * (units // width),)),
        pair_send=dma((5,)), pair_recv=dma((10,)),
        sum_send=dma((1,)), sum_recv=dma((pieces, bits)),
        in_send=dma((1,)), in_recv=dma((n,)),
        all_send=dma((3,)), line_recv=dma((3, n // 4 - 1)), first_recv=dma((2, 2, n // 4)), plane_recv=dma((3,)),
        own=dma((1,)), out=dma((7,)),
        small_send=dma((2,)), small_recv=dma((2,)),
        last_send=dma((1,)), last_recv=dma((1,)),
    )
    stages = [pltpu.VMEM((pieces, n >> (b + 1), share, half), BF) for b in range(bits)]
    return pl.pallas_call(
        functools.partial(layer_kernel, n, slot, count_in, count_out),
        out_shape=tuple(results),
        in_specs=in_specs,
        out_specs=tuple([hbm] * 6 + [vmem] * 2),
        scratch_shapes=list(scratch) + stages,
        compiler_params=pltpu.CompilerParams(collective_id=1, has_side_effects=True, vmem_limit_bytes=LAYER_LIMIT),
    )(*args)


def finish_kernel(parts, *refs):
    count, total = len(parts), sum(parts)
    ins, outs, held, sems = refs[:count], refs[count : count + total], refs[count + total : -1], refs[-1]
    into = [pltpu.make_async_copy(ins[i], held[i], sems.at[i]) for i in range(count)]
    for copy in into:
        copy.start()
    back = []
    for i in range(count):
        into[i].wait()
        for part in range(parts[i]):
            number = len(back)
            src = held[i] if parts[i] == 1 else held[i].at[part]
            back.append(pltpu.make_async_copy(src, outs[number], sems.at[count + number]))
            back[-1].start()
    for copy in back:
        copy.wait()


def finish(arrays, parts):
    count, total = len(arrays), sum(parts)
    spec = pl.BlockSpec(memory_space=pl.ANY)
    shapes = []
    for array, part in zip(arrays, parts):
        shapes += [jax.ShapeDtypeStruct(array.shape[part > 1 :], array.dtype)] * part
    return pl.pallas_call(
        functools.partial(finish_kernel, parts),
        out_shape=tuple(shapes),
        in_specs=[spec] * count,
        out_specs=(spec,) * total,
        scratch_shapes=[pltpu.VMEM(a.shape, a.dtype) for a in arrays] + [pltpu.SemaphoreType.DMA((count + total,))],
        compiler_params=pltpu.CompilerParams(vmem_limit_bytes=VMEM_LIMIT),
    )(*arrays)


def whole(shape=None):
    return pl.BlockSpec(memory_space=pltpu.VMEM)


def call(kernel, outs, *args):
    return pl.pallas_call(
        kernel,
        out_shape=tuple(jax.ShapeDtypeStruct(shape, kind) for shape, kind in outs),
        in_specs=[whole()] * len(args),
        out_specs=tuple(whole() for _ in outs),
        compiler_params=pltpu.CompilerParams(vmem_limit_bytes=VMEM_LIMIT),
    )(*args)


def per_device(
    n, hidden, encodings, lengths, cotangent, wq, wk, wv, wo, wcq, wck, wcv, wco, w_in, w_out,
    gain_self, gain_cross, gain_feed, table,
):
    rows, width = hidden.shape[2], hidden.shape[3]
    slot = encodings.shape[3]
    passages = lengths.shape[2]
    units = w_in.shape[1]
    pairs = width // (2 * HD)
    keys = passages * slot
    own = hidden.reshape(rows, width)
    cot = cotangent.reshape(rows, width)
    g1, g2, g3 = (gain.reshape(1, width) for gain in (gain_self, gain_cross, gain_feed))
    length_row = lengths.reshape(passages)
    share = width // n
    fits = passages == n and keys * width * 8 <= 16 << 20 and units == 4 * width
    tables = 128 % table.shape[0] == 0 and table.size % 128 == 0
    if n & (n - 1) == 0 and n >= 8 and share % 16 == 0 and share <= 128 and fits and tables:
        out = layer(n, slot, Inputs(
            length_row, encodings.reshape(n, slot, width), wq, wk, wv, wo, wcq, wck, wcv, wco, w_in, w_out, own, cot,
            gain_self, gain_cross, gain_feed, table.T,
        ))
        result, hidden_grad, enc_grad, *sums, table_sum = finish(out, (1, 1, 1, 8, 1, 1, 3, 1))
        return (
            (result.reshape(hidden.shape), hidden_grad.reshape(hidden.shape), enc_grad.reshape(encodings.shape))
            + tuple(sums[:10])
            + tuple(gain.reshape(share) for gain in sums[10:])
            + (table_sum.T,)
        )

    source = lax.all_to_all(encodings, PASS, split_axis=2, concat_axis=0, tiled=True).reshape(keys, width)

    sixteen, wide = ((rows, width), BF), ((rows, width), F32)
    h1, q, k, v, mix1, after_self, h2, cq = call(
        self_forward_kernel,
        [sixteen] * 5 + [wide, sixteen, sixteen],
        own, wq, wk, wv, wo, wcq, g1, g2, table,
    )

    block = 4 * slot
    steps = keys // block
    stats = jax.ShapeDtypeStruct((pairs, 2 * rows), F32)
    smem = pl.BlockSpec(memory_space=pltpu.SMEM)
    tile = pl.BlockSpec((block, width), lambda i: (i, 0))
    square = pl.BlockSpec((width, width), lambda i: (0, 0))
    query = pl.BlockSpec((rows, width), lambda i: (0, 0))
    stat = pl.BlockSpec((pairs, 2 * rows), lambda i: (0, 0))
    ck, cv, mix_t, lse = pl.pallas_call(
        functools.partial(cross_forward_kernel, slot),
        grid=(steps,),
        out_shape=(
            jax.ShapeDtypeStruct((keys, width), BF),
            jax.ShapeDtypeStruct((keys, width), BF),
            jax.ShapeDtypeStruct((width, rows), F32),
            stats,
        ),
        in_specs=[smem, tile, square, square, query],
        out_specs=(tile, tile, pl.BlockSpec((width, rows), lambda i: (0, 0)), stat),
        scratch_shapes=[
            pltpu.VMEM((pairs, 2 * rows, 2 * HD), BF),
            pltpu.VMEM((pairs, 2 * rows), F32),
            pltpu.VMEM((pairs, 2 * rows), F32),
            pltpu.VMEM((width, rows), F32),
        ],
        compiler_params=pltpu.CompilerParams(vmem_limit_bytes=VMEM_LIMIT),
    )(length_row, source, wck, wcv, cq)

    pieces = units // width
    result, grad_cross, gmix, delta, dg3, d_in, d_out, d_co = call(
        feed_kernel,
        [wide, wide, sixteen, ((pairs, 2 * rows), F32), ((1, width), F32), ((pieces, width, width), BF),
         ((units, width), BF), ((width, width), BF)],
        mix_t, after_self, cot, wco, w_in, w_out, g3,
    )

    enc_grad, dcq, d_ck, d_cv = pl.pallas_call(
        functools.partial(cross_backward_kernel, slot),
        grid=(steps,),
        out_shape=(
            jax.ShapeDtypeStruct((keys, width), BF),
            jax.ShapeDtypeStruct((rows, width), BF),
            jax.ShapeDtypeStruct((width, width), BF),
            jax.ShapeDtypeStruct((width, width), BF),
        ),
        in_specs=[smem, tile, tile, tile, square, square, query, query, stat, stat],
        out_specs=(tile, query, square, square),
        scratch_shapes=[
            pltpu.VMEM((pairs, 2 * rows, 2 * HD), BF),
            pltpu.VMEM((pairs, 2 * rows, 2 * HD), BF),
            pltpu.VMEM((width, rows), F32),
            pltpu.VMEM((block, 2 * width), BF),
            pltpu.VMEM((width, 2 * width), F32),
        ],
        compiler_params=pltpu.CompilerParams(vmem_limit_bytes=VMEM_LIMIT),
    )(length_row, source, ck, cv, wck, wcv, cq, gmix, lse, delta)
    returned = lax.all_to_all(
        enc_grad.reshape(passages, 1, 1, slot, width), PASS, split_axis=0, concat_axis=2, tiled=True
    )

    gain_kind = ((1, width), F32)
    squared = ((width, width), BF)
    hidden_grad, d_cq, d_so, d_q, d_k, d_v, dg1, dg2, dtable = call(
        self_backward_kernel,
        [wide] + [squared] * 5 + [gain_kind, gain_kind, (table.shape, F32)],
        own, h1, q, k, v, mix1, after_self, h2, dcq, grad_cross, wq, wk, wv, wo, wcq, g1, g2, table,
    )

    both = [d_q, d_k, d_v, d_so, d_cq, d_ck, d_cv, d_co, d_in.transpose(1, 0, 2).reshape(width, units), d_out]

    def total(part):
        shared = lax.psum_scatter(part, PASS, scatter_dimension=0, tiled=True)
        return lax.psum(shared.astype(BF), CORE).astype(F32)

    sums = [total(part.astype(F32)) for part in both]
    totals, in_total, out_total = sums[:8], sums[8], sums[9]
    gains = [total(part.reshape(width)) for part in (dg1, dg2, dg3)]
    table_sum = lax.psum(dtable, (PASS, CORE))
    return (
        (result.reshape(hidden.shape), hidden_grad.reshape(hidden.shape), returned)
        + tuple(totals)
        + (in_total, out_total)
        + tuple(gains)
        + (table_sum,)
    )


def solution(mesh):
    rows = P(CORE, PASS, None, None)
    passage = P(PASS, CORE, None, None, None)
    in_specs = (rows, passage, P(CORE, PASS, None), rows) + (P(),) * 14
    out_specs = (rows, rows, passage) + (P(PASS, None),) * 10 + (P(PASS),) * 3 + (P(),)
    return jax.shard_map(
        functools.partial(per_device, mesh.shape[PASS]),
        mesh=mesh,
        in_specs=in_specs,
        out_specs=out_specs,
        check_vma=False,
    )
```

```python
import functools
from typing import Any, NamedTuple

import jax
import jax.numpy as jnp
from jax import lax
from jax.experimental import pallas as pl
from jax.experimental.pallas import tpu as pltpu
from jax.sharding import PartitionSpec as P

HD = 64
EPS = 1e-06
LIMITS = (19, 21, 24, 27, 31, 35, 40, 46, 52, 59, 67, 77, 87, 99, 113)
NEG = -1e30
BF = jnp.bfloat16
F32 = jnp.float32
MESH = pl.DeviceIdType.MESH
PASS, CORE = "pass", "pb"
PLANES_FIRST = (2, 3, 6, 7, 13)
ROOT = 0.7978845608028654
VMEM_LIMIT = 56 << 20
LAYER_LIMIT = 64 << 20


def narrow(value):
    return value.astype(BF)


def dot_nn(left, right):
    return lax.dot_general(left, right, (((1,), (0,)), ((), ())), preferred_element_type=F32)


def dot_nt(left, right):
    return lax.dot_general(left, right, (((1,), (1,)), ((), ())), preferred_element_type=F32)


def dot_tn(left, right):
    return lax.dot_general(left, right, (((0,), (0,)), ((), ())), preferred_element_type=F32)


def rms(value, gain):
    scale = lax.rsqrt(jnp.mean(value * value, axis=-1, keepdims=True) + EPS)
    return value * scale * gain


def rms_back(value, gain, grad):
    scale = lax.rsqrt(jnp.mean(value * value, axis=-1, keepdims=True) + EPS)
    scaled = grad * gain
    inner = jnp.mean(scaled * value, axis=-1, keepdims=True)
    rows = scaled * scale - value * (scale * scale * scale * inner)
    gain_grad = jnp.sum(grad * (value * scale), axis=0, keepdims=True)
    return rows, gain_grad


def pair_mask(pair):
    lane = lax.broadcasted_iota(jnp.int32, pair.shape, 1)
    zero = jnp.zeros_like(pair)
    return jnp.concatenate(
        [jnp.where(lane < HD, pair, zero), jnp.where(lane >= HD, pair, zero)], axis=0
    )


def pair_diag(both, rows):
    return jnp.concatenate([both[:HD, :rows], both[HD:, rows:]], axis=0)


def bucket_onehot_rows(buckets, length):
    distance = lax.broadcasted_iota(jnp.int32, (buckets, length), 1)
    row = lax.broadcasted_iota(jnp.int32, (buckets, length), 0)
    beyond = jnp.zeros_like(distance)
    for edge in LIMITS:
        beyond = beyond + (distance >= edge).astype(jnp.int32)
    bucket = jnp.where(distance < 16, distance, 16 + beyond)
    return (bucket == row).astype(F32)


def head_bias(table, rows):
    onehot = bucket_onehot_rows(table.shape[1], rows)
    return lax.dot_general(
        table, onehot, (((1,), (0,)), ((), ())), precision=lax.Precision.HIGHEST,
        preferred_element_type=F32,
    )


def toeplitz(row, rows):
    return pltpu.roll(jnp.broadcast_to(row, (rows, rows)), 0, 1, stride=1, stride_axis=0)


def diagonal_sums(square):
    rows = square.shape[0]
    place = lax.broadcasted_iota(jnp.int32, square.shape, 0)
    for bit in range(3):
        moved = pltpu.roll(square, rows - (1 << bit), 1)
        square = jnp.where((place >> bit) & 1 == 1, moved, square)
    total = square[:8]
    for group in range(1, rows // 8):
        total = total + pltpu.roll(square[8 * group : 8 * group + 8], rows - 8 * group, 1)
    return jnp.sum(total, axis=0, keepdims=True)


def causal_mask(rows):
    key = lax.broadcasted_iota(jnp.int32, (rows, 2 * rows), 0)
    query = lax.broadcasted_iota(jnp.int32, (rows, 2 * rows), 1)
    query = jnp.where(query >= rows, query - rows, query)
    return key <= query


def self_forward_kernel(
    hidden, wq, wk, wv, wo, wcq, g1, g2, table,
    h1_out, q_out, k_out, v_out, mix_out, after_out, h2_out, cq_out,
):
    rows, width = hidden.shape
    pairs = width // (2 * HD)
    value = hidden[...].astype(F32)
    h1 = narrow(rms(value, g1[...]))
    h1_out[...] = h1
    q = narrow(dot_nn(h1, wq[...]))
    k = narrow(dot_nn(h1, wk[...]))
    v = narrow(dot_nn(h1, wv[...]))
    q_out[...] = q
    k_out[...] = k
    v_out[...] = v
    bias = head_bias(table[...].T, rows)
    allowed = causal_mask(rows)
    mixed = []
    for pair in range(pairs):
        at = slice(pair * 2 * HD, (pair + 1) * 2 * HD)
        scores = dot_nt(k[:, at], pair_mask(q[:, at]))
        both = jnp.concatenate(
            [toeplitz(bias[2 * pair : 2 * pair + 1], rows), toeplitz(bias[2 * pair + 1 : 2 * pair + 2], rows)],
            axis=1,
        )
        scores = jnp.where(allowed, scores + both, NEG)
        top = jnp.max(scores, axis=0, keepdims=True)
        raised = jnp.exp(scores - top)
        chances = raised / jnp.sum(raised, axis=0, keepdims=True)
        mixed.append(pair_diag(dot_tn(v[:, at], narrow(chances)), rows))
    mix = narrow(jnp.concatenate(mixed, axis=0).T)
    mix_out[...] = mix
    after = value + dot_nn(mix, wo[...])
    after_out[...] = after
    h2 = narrow(rms(after, g2[...]))
    h2_out[...] = h2
    cq_out[...] = narrow(dot_nn(h2, wcq[...]))


def cross_forward_kernel(slot, lengths, enc, wk, wv, cq, k_out, v_out, mix_out, lse_out, masked, top, total, acc):
    step = pl.program_id(0)
    rows, width = cq.shape
    block = enc.shape[0]
    pairs = width // (2 * HD)

    @pl.when(step == 0)
    def _():
        for pair in range(pairs):
            at = slice(pair * 2 * HD, (pair + 1) * 2 * HD)
            masked[pair] = pair_mask(cq[:, at])
        top[...] = jnp.full(top.shape, NEG, F32)
        total[...] = jnp.zeros(total.shape, F32)
        acc[...] = jnp.zeros(acc.shape, F32)

    source = enc[...]
    k_out[...] = narrow(dot_nn(source, wk[...]))
    v_out[...] = narrow(dot_nn(source, wv[...]))
    place = lax.broadcasted_iota(jnp.int32, (slot, 2 * rows), 0)
    passages = block // slot
    valid = jnp.concatenate([place < lengths[step * passages + i] for i in range(passages)], axis=0)
    for pair in range(pairs):
        at = slice(pair * 2 * HD, (pair + 1) * 2 * HD)
        scores = jnp.where(valid, dot_nt(k_out[:, at], masked[pair]), NEG)
        before = top[pair : pair + 1]
        now = jnp.maximum(before, jnp.max(scores, axis=0, keepdims=True))
        top[pair : pair + 1] = now
        fade = jnp.exp(before - now)
        raised = jnp.exp(scores - now)
        total[pair : pair + 1] = total[pair : pair + 1] * fade + jnp.sum(raised, axis=0, keepdims=True)
        part = pair_diag(dot_tn(v_out[:, at], narrow(raised)), rows)
        fades = jnp.concatenate(
            [jnp.broadcast_to(fade[:, :rows], (HD, rows)), jnp.broadcast_to(fade[:, rows:], (HD, rows))], axis=0
        )
        acc[at, :] = acc[at, :] * fades + part

    @pl.when(step == pl.num_programs(0) - 1)
    def _():
        for pair in range(pairs):
            at = slice(pair * 2 * HD, (pair + 1) * 2 * HD)
            sums = total[pair : pair + 1]
            lse_out[pair : pair + 1] = top[pair : pair + 1] + jnp.log(sums)
            inverse = 1.0 / sums
            spread = jnp.concatenate(
                [jnp.broadcast_to(inverse[:, :rows], (HD, rows)), jnp.broadcast_to(inverse[:, rows:], (HD, rows))],
                axis=0,
            )
            mix_out[at, :] = acc[at, :] * spread


def feed_kernel(
    mix_t, after_self, cot, wo, w_in, w_out, g3,
    result_out, grad_out, gmix_out, delta_out, dgain_out, d_in, d_out, d_o,
):
    rows, width = cot.shape
    hidden_units = w_in.shape[1]
    mix = narrow(mix_t[...].T)
    after = after_self[...] + dot_nn(mix, wo[...])
    h3 = narrow(rms(after, g3[...]))
    inner = dot_nn(h3, w_in[...])
    bent = jnp.tanh(ROOT * (inner + 0.044715 * (inner * inner * inner)))
    active = narrow(0.5 * inner * (1.0 + bent))
    result_out[...] = after + dot_nn(active, w_out[...])
    cb = cot[...]
    d_out[...] = narrow(dot_tn(active, cb))
    slope = 0.5 * (1.0 + bent) + (0.5 * ROOT) * inner * (1.0 - bent * bent) * (1.0 + (3 * 0.044715) * inner * inner)
    gi = narrow(dot_nt(cb, w_out[...]) * slope)
    pieces = hidden_units // width
    for piece in range(pieces):
        d_in[piece] = narrow(dot_tn(h3, gi[:, piece * width : (piece + 1) * width]))
    back, gain_grad = rms_back(after, g3[...], dot_nt(gi, w_in[...]))
    dgain_out[...] = gain_grad
    grad = cb.astype(F32) + back
    grad_out[...] = grad
    gb = narrow(grad)
    d_o[...] = narrow(dot_tn(mix, gb))
    gmix = narrow(dot_nt(gb, wo[...]))
    gmix_out[...] = gmix
    product = gmix.astype(F32).T * mix_t[...]
    for pair in range(width // (2 * HD)):
        first = jnp.sum(product[pair * 2 * HD : pair * 2 * HD + HD], axis=0, keepdims=True)
        second = jnp.sum(product[pair * 2 * HD + HD : (pair + 1) * 2 * HD], axis=0, keepdims=True)
        delta_out[pair : pair + 1] = jnp.concatenate([first, second], axis=1)


def cross_backward_kernel(
    slot, lengths, enc, k, v, wk, wv, cq, gmix, lse, delta,
    enc_out, dq_out, dk_out, dv_out, masked, gmasked, dq_t, dkv, acc,
):
    step = pl.program_id(0)
    rows, width = cq.shape
    block = enc.shape[0]
    pairs = width // (2 * HD)

    @pl.when(step == 0)
    def _():
        for pair in range(pairs):
            at = slice(pair * 2 * HD, (pair + 1) * 2 * HD)
            masked[pair] = pair_mask(cq[:, at])
            gmasked[pair] = pair_mask(gmix[:, at])
        dq_t[...] = jnp.zeros(dq_t.shape, F32)
        acc[...] = jnp.zeros(acc.shape, F32)

    place = lax.broadcasted_iota(jnp.int32, (slot, 2 * rows), 0)
    passages = block // slot
    valid = jnp.concatenate([place < lengths[step * passages + i] for i in range(passages)], axis=0)
    for pair in range(pairs):
        at = slice(pair * 2 * HD, (pair + 1) * 2 * HD)
        scores = jnp.where(valid, dot_nt(k[:, at], masked[pair]), NEG)
        chances = jnp.exp(scores - lse[pair : pair + 1])
        dkv[:, width + pair * 2 * HD : width + (pair + 1) * 2 * HD] = narrow(dot_nn(narrow(chances), gmasked[pair]))
        ds = narrow(chances * (dot_nt(v[:, at], gmasked[pair]) - delta[pair : pair + 1]))
        dkv[:, at] = narrow(dot_nn(ds, masked[pair]))
        dq_t[at, :] = dq_t[at, :] + pair_diag(dot_tn(k[:, at], ds), rows)
    enc_out[...] = narrow(dot_nt(dkv[:, :width], wk[...]) + dot_nt(dkv[:, width:], wv[...]))
    acc[...] = acc[...] + dot_tn(enc[...], dkv[...])

    @pl.when(step == pl.num_programs(0) - 1)
    def _():
        dq_out[...] = narrow(dq_t[...].T)
        dk_out[...] = narrow(acc[:, :width])
        dv_out[...] = narrow(acc[:, width:])


def self_backward_kernel(
    hidden, h1, q, k, v, mix, after_self, h2, dcq, grad_cross, wq, wk, wv, wo, wcq, g1, g2, table,
    hidden_out, d_cq, d_o, d_q, d_k, d_v, dg1_out, dg2_out, dtable_out,
):
    rows, width = hidden.shape
    pairs = width // (2 * HD)
    d_cq[...] = narrow(dot_tn(h2[...], dcq[...]))
    back, gain_grad = rms_back(after_self[...], g2[...], dot_nt(dcq[...], wcq[...]))
    dg2_out[...] = gain_grad
    grad = grad_cross[...] + back
    sb = narrow(grad)
    d_o[...] = narrow(dot_tn(mix[...], sb))
    gmix = narrow(dot_nt(sb, wo[...]))
    bias = head_bias(table[...].T, rows)
    allowed = causal_mask(rows)
    dq_parts, dk_parts, dv_parts, sums = [], [], [], []
    for pair in range(pairs):
        at = slice(pair * 2 * HD, (pair + 1) * 2 * HD)
        masked = pair_mask(q[:, at])
        gmasked = pair_mask(gmix[:, at])
        scores = dot_nt(k[:, at], masked)
        both = jnp.concatenate(
            [toeplitz(bias[2 * pair : 2 * pair + 1], rows), toeplitz(bias[2 * pair + 1 : 2 * pair + 2], rows)],
            axis=1,
        )
        scores = jnp.where(allowed, scores + both, NEG)
        top = jnp.max(scores, axis=0, keepdims=True)
        raised = jnp.exp(scores - top)
        chances = raised / jnp.sum(raised, axis=0, keepdims=True)
        dv_parts.append(narrow(dot_nn(narrow(chances), gmasked)))
        dp = dot_nt(v[:, at], gmasked)
        ds = chances * (dp - jnp.sum(chances * dp, axis=0, keepdims=True))
        sums.append(diagonal_sums(ds[:, :rows]))
        sums.append(diagonal_sums(ds[:, rows:]))
        dsb = narrow(ds)
        dk_parts.append(narrow(dot_nn(dsb, masked)))
        dq_parts.append(pair_diag(dot_tn(k[:, at], dsb), rows))
    dq = narrow(jnp.concatenate(dq_parts, axis=0).T)
    dk = jnp.concatenate(dk_parts, axis=1)
    dv = jnp.concatenate(dv_parts, axis=1)
    d_q[...] = narrow(dot_tn(h1[...], dq))
    d_k[...] = narrow(dot_tn(h1[...], dk))
    d_v[...] = narrow(dot_tn(h1[...], dv))
    into = dot_nt(dq, wq[...]) + dot_nt(dk, wk[...]) + dot_nt(dv, wv[...])
    back, gain_grad = rms_back(hidden[...].astype(F32), g1[...], into)
    dg1_out[...] = gain_grad
    hidden_out[...] = grad + back
    by_distance = jnp.concatenate(sums, axis=0)
    onehot = bucket_onehot_rows(table.shape[0], rows)
    dtable_out[...] = lax.dot_general(
        onehot, by_distance, (((1,), (1,)), ((), ())), precision=lax.Precision.HIGHEST, preferred_element_type=F32
    )


def halving_order(bits, piece):
    first = list(range(bits))
    if sum(other in PLANES_FIRST for other in range(piece + 1)) % 2 != piece % 2:
        first[0], first[1] = first[1], first[0]
    return first[2:] + first[:2] if piece in PLANES_FIRST else first


class Inputs(NamedTuple):
    lengths: Any
    encodings: Any
    wq: Any
    wk: Any
    wv: Any
    wo: Any
    wcq: Any
    wck: Any
    wcv: Any
    wco: Any
    w_in: Any
    w_out: Any
    hidden: Any
    cot: Any
    g1: Any
    g2: Any
    g3: Any
    table: Any


class Outputs(NamedTuple):
    result: Any
    hidden: Any
    enc: Any
    squares: Any
    fin: Any
    fout: Any
    gains: Any
    table: Any


class Scratch(NamedTuple):
    left_self: Any
    left_feed: Any
    right: Any
    give: Any
    late: Any
    late_give: Any
    enc: Any
    keys: Any
    values: Any
    queries: Any
    grads: Any
    stats: Any
    weights: Any
    masked: Any
    gmasked: Any
    acc: Any
    q: Any
    k: Any
    v: Any
    after_self: Any
    grad_cross: Any
    top: Any
    lse: Any
    delta: Any
    swap_give: Any
    swap_take: Any
    mine: Any
    last_own: Any
    last_other: Any
    out_result: Any
    out_hidden: Any
    out_squares: Any
    out_fin: Any
    out_fout: Any
    small_give: Any
    small_take: Any
    small_sum: Any
    load: Any
    pair_send: Any
    pair_recv: Any
    sum_send: Any
    sum_recv: Any
    in_send: Any
    in_recv: Any
    all_send: Any
    line_recv: Any
    first_recv: Any
    plane_recv: Any
    own: Any
    out: Any
    small_send: Any
    small_recv: Any
    last_send: Any
    last_recv: Any


CO, CQ, SO, SQ, SK, SV, CK, CV = range(8)


def layer_kernel(n, slot, count_in, count_out, *refs):
    bits = n.bit_length() - 1
    ins = Inputs(*refs[: len(Inputs._fields)])
    outs = Outputs(*refs[len(ins) : len(ins) + len(Outputs._fields)])
    scratch = refs[len(ins) + len(outs) :]
    r, stages = Scratch(*scratch[: len(Scratch._fields)]), scratch[len(Scratch._fields) :]
    mine, weights = r.mine, r.weights
    share, half = mine.shape[2], mine.shape[3] // 2
    pieces = 2 * mine.shape[0]
    rows, width = ins.hidden.shape
    units = count_out * width
    span = count_in * half
    pairs = width // (2 * HD)
    two = 2 * HD
    line = n // 4
    me, core = lax.axis_index(PASS), lax.axis_index(CORE)
    low = me % 4
    partner = (me, 1 - core)
    wq, wk, wv, wo, wcq, wck, wcv, wco = (weights.at[i] for i in range(8))
    g1, g2, g3 = (g[...].reshape(1, width) for g in (ins.g1, ins.g2, ins.g3))

    def remote(src, dst, send, recv, device):
        return pltpu.make_async_remote_copy(
            src_ref=src, dst_ref=dst, send_sem=send, recv_sem=recv, device_id=device, device_id_type=MESH
        )

    def all_sent(like, sem):
        remote(like, like, sem, sem, partner).wait_send()

    def all_come(like, sem):
        remote(like, like, sem, sem, partner).wait_recv()

    def by_core(body):
        for c in range(2):
            pl.when(core == c)(functools.partial(body, c))

    def columns(pair):
        return slice(pair * two, (pair + 1) * two)

    parts = units // width
    loads = [(w, weights.at[i]) for i, w in enumerate(ins[2:10])]
    tiles = mine.reshape(2 * parts, width, width)
    for j in range(parts):
        at = slice(j * width, (j + 1) * width)
        loads += [(ins.w_in.at[:, at], tiles.at[j]), (ins.w_out.at[at], tiles.at[parts + j])]

    def load(i):
        return pltpu.make_async_copy(loads[i][0], loads[i][1], r.load.at[i])

    for i in range(8):
        load(i).start()

    barrier = pltpu.get_barrier_semaphore()
    pl.semaphore_signal(barrier, inc=1, device_id=partner, device_id_type=MESH)

    def greet(d, carry):
        pl.semaphore_signal(barrier, inc=1, device_id=(me ^ d, core), device_id_type=MESH)
        return carry

    lax.fori_loop(1, n, greet, 0)
    pl.semaphore_wait(barrier, n)

    def passage_at(p):
        return pl.ds(pl.multiple_of(p * slot, slot), slot)

    def bring(q):
        return remote(ins.encodings.at[q], r.enc.at[passage_at(me)], r.in_send.at[0], r.in_recv.at[me], (q, core))

    def arrived(p):
        return remote(ins.encodings.at[p], r.enc.at[passage_at(p)], r.in_send.at[0], r.in_recv.at[p], (p, core))

    def bring_range(first, last):
        def one(d, carry):
            bring(me ^ d).start()
            return carry

        lax.fori_loop(first, last, one, 0)

    bring_range(1, 4)
    own_passage = pltpu.make_async_copy(ins.encodings.at[me], r.enc.at[passage_at(me)], r.own.at[0])
    own_passage.start()
    for i in range(8, len(loads)):
        load(i).start()

    x_peer, y_peer = (me ^ 1, core), (me ^ 2, core)

    steps_of_line = [[k for k in range(1, line) if k.bit_count() == hops] for hops in range(1, bits - 1)]
    line_bits = len(steps_of_line)

    def line_copy(kind, k):
        last = k & -k
        origin = me ^ (4 * (k ^ last))
        ref = r.stats.at[origin] if kind == 2 else (r.queries, r.grads)[kind].at[:, origin]
        return remote(ref, ref, r.all_send.at[kind], r.line_recv.at[kind, k - 1], (me ^ (4 * last), core))

    def spread_line(kind, number):
        if number:
            for k in steps_of_line[number - 1]:
                line_copy(kind, k).wait_recv()
        for k in reversed(steps_of_line[number]) if number < line_bits else ():
            line_copy(kind, k).start()

    def plane_copy(kind, number, k):
        part = number % 2
        first, second = (x_peer, y_peer) if part == 0 else (y_peer, x_peer)
        origin = me ^ (4 * k) if number < 4 else me ^ (4 * k) ^ (1 << part)
        at = (r.queries, r.grads)[kind].at[part, origin]
        recv = r.first_recv.at[kind, number, k] if number < 2 else r.plane_recv.at[kind]
        return remote(at, at, r.all_send.at[kind], recv, first if number < 2 else second)

    def stat_plane(d):
        view = r.stats.reshape(line, 4, *r.stats.shape[1:]).at[:, low]
        return remote(view, view, r.all_send.at[2], r.plane_recv.at[2], (me ^ d, core))

    def spread_plane(kind, blocks):
        for number in range(4):
            for k in blocks:
                plane_copy(kind, number, k).start()

    def spread_rest(kind, blocks):
        for k in blocks:
            for number in range(2):
                plane_copy(kind, number, k).wait_recv()
        for k in blocks:
            for number in range(4, 6):
                plane_copy(kind, number, k).start()

    def spread_taken(kind):
        like = r.stats.at[: 3 * line] if kind == 2 else r.grads.at[:, : 2 * line]
        all_come(like, r.plane_recv.at[kind])

    def spread_sent(kind):
        like = r.stats.at[: 4 * line - 1] if kind == 2 else r.grads.at[:, : 4 * line - 1]
        all_sent(like, r.all_send.at[kind])

    ready = (
        (r.out_result, outs.result), (r.out_hidden, outs.hidden), (r.out_squares, outs.squares), (r.out_fin, outs.fin),
        (r.out_fout, outs.fout),
    )

    def give_out(i):
        return pltpu.make_async_copy(*ready[i], r.out.at[2 + i])

    value = ins.hidden[...].astype(F32)
    h1 = narrow(rms(value, g1))
    r.left_self[0, :, :width] = h1
    for i, ref in enumerate((r.q, r.k, r.v)):
        load(i).wait()
        ref[...] = narrow(dot_nn(h1, weights[i]))
    bias = head_bias(ins.table[...], rows)
    allowed = causal_mask(rows)

    def self_chances(pair):
        at = columns(pair)
        masked = pair_mask(r.q[:, at])
        scores = dot_nt(r.k[:, at], masked)
        both = jnp.concatenate([toeplitz(bias[2 * pair + i : 2 * pair + i + 1], rows) for i in range(2)], axis=1)
        scores = jnp.where(allowed, scores + both, NEG)
        raised = jnp.exp(scores - jnp.max(scores, axis=0, keepdims=True))
        return at, masked, raised / jnp.sum(raised, axis=0, keepdims=True)

    for pair in range(pairs):
        at, _, chances = self_chances(pair)
        r.acc[at, :] = pair_diag(dot_tn(r.v[:, at], narrow(chances)), rows)
    mix1 = narrow(r.acc[...].T)
    r.left_self[0, :, 2 * width :] = mix1
    load(3).wait()
    after_self = value + dot_nn(mix1, wo[...])
    r.after_self[...] = after_self
    h2 = narrow(rms(after_self, g2))
    r.left_self[0, :, width : 2 * width] = h2
    load(4).wait()
    cq = narrow(dot_nn(h2, wcq[...]))
    for c in range(2):
        r.queries[c, me] = cq[:, c * half : (c + 1) * half]
    spread_line(0, 0)
    bring_range(n // 2, 3 * n // 4)
    for pair in range(pairs):
        r.masked[pair] = pair_mask(cq[:, columns(pair)])
    r.top[...] = jnp.full(r.top.shape, NEG, F32)
    r.lse[...] = jnp.zeros(r.lse.shape, F32)
    r.acc[...] = jnp.zeros(r.acc.shape, F32)

    def pair_copy(i):
        src = (r.left_self.at[0], r.left_feed.at[0], r.give)[i]
        dst = (r.left_self, r.left_feed, r.right)[i].at[1]
        return remote(src, dst, r.pair_send.at[i], r.pair_recv.at[i], partner)

    pair_copy(0).start()

    place = lax.broadcasted_iota(jnp.int32, (slot, 2 * rows), 0)

    def spread(row):
        return jnp.concatenate(
            [jnp.broadcast_to(row[:, :rows], (HD, rows)), jnp.broadcast_to(row[:, rows:], (HD, rows))], axis=0
        )

    load(5).wait()
    load(6).wait()
    own_passage.wait()
    few = 1
    turns = n // few

    def forward_block(turn, carry):
        @pl.when(turn == turns // 8)
        def _():
            for number in range(1, line_bits):
                spread_line(0, number)
            bring_range(3 * n // 4, n)
            bring_range(4, n // 2)

        @pl.when(turn == 3 * turns // 8)
        def _():
            spread_line(0, line_bits)
            spread_plane(0, range(line))

        pl.when(turn == 3 * turns // 4)(functools.partial(spread_rest, 0, range(line)))
        part = turn // (turns // 4)
        moved = turn % (turns // 4) + (part % 2 * 2 + part // 2) * (turns // 4)
        first = (moved ^ (me // few)) * few
        for i in range(few):

            @pl.when(first + i != me)
            def _(i=i):
                arrived(first + i).wait_recv()

        at = pl.ds(pl.multiple_of(first * slot, few * slot), few * slot)
        source = r.enc[at]
        r.keys[at] = narrow(dot_nn(source, wck[...]))
        r.values[at] = narrow(dot_nn(source, wcv[...]))
        valid = jnp.concatenate([place < ins.lengths[first + i] for i in range(few)], axis=0)
        for pair in range(pairs):
            cols = columns(pair)
            scores = jnp.where(valid, dot_nt(r.keys[at, cols], r.masked[pair]), NEG)
            before = r.top[pair : pair + 1]
            now = jnp.maximum(before, jnp.max(scores, axis=0, keepdims=True))
            r.top[pair : pair + 1] = now
            fade = jnp.exp(before - now)
            raised = jnp.exp(scores - now)
            r.lse[pair : pair + 1] = r.lse[pair : pair + 1] * fade + jnp.sum(raised, axis=0, keepdims=True)
            part = pair_diag(dot_tn(r.values[at, cols], narrow(raised)), rows)
            r.acc[cols, :] = r.acc[cols, :] * spread(fade) + part
        return carry

    lax.fori_loop(0, turns, forward_block, 0)
    for pair in range(pairs):
        cols = columns(pair)
        sums = r.lse[pair : pair + 1]
        r.lse[pair : pair + 1] = r.top[pair : pair + 1] + jnp.log(sums)
        r.acc[cols, :] = r.acc[cols, :] * spread(1.0 / sums)

    own_load = pltpu.make_async_copy(ins.encodings, r.enc.reshape(n, slot, width), r.own.at[0])
    own_load.start()
    mix2 = narrow(r.acc[...].T)
    r.left_feed[0, :, units + width :] = mix2
    load(7).wait()
    after_cross = r.after_self[...] + dot_nn(mix2, wco[...])
    h3 = narrow(rms(after_cross, g3))
    r.left_feed[0, :, units : units + width] = h3
    cb = ins.cot[...]
    result = after_cross
    into = jnp.zeros((rows, width), F32)
    products = {}

    def ahead_of(j):
        if j < parts:
            load(8 + 2 * j).wait()
            load(9 + 2 * j).wait()
            products[j] = dot_nn(h3, tiles[j]), dot_nt(cb, tiles[parts + j])

    ahead_of(0)
    for j in range(parts):
        ahead_of(j + 1)
        inner, back = products.pop(j)
        bent = jnp.tanh(ROOT * (inner + 0.044715 * (inner * inner * inner)))
        active = narrow(0.5 * inner * (1.0 + bent))
        r.left_feed[0, :, j * width : (j + 1) * width] = active
        slope = 0.5 * (1.0 + bent) + (0.5 * ROOT) * inner * (1.0 - bent * bent) * (1.0 + (3 * 0.044715) * inner * inner)
        gi = narrow(back * slope)
        into = into + dot_nt(gi, tiles[j])
        result = result + dot_nn(active, tiles[parts + j])
        to = slice((j % (parts // 2)) * width, (j % (parts // 2) + 1) * width)

        def keep(c, gi=gi, to=to, owner=j // (parts // 2)):
            if c == owner:
                r.right[0, :, to] = gi
            else:
                r.give[:, to] = gi

        by_core(keep)
    r.out_result[...] = result
    give_out(0).start()
    pair_copy(1).start()
    back, dg3 = rms_back(after_cross, g3, into)
    grad = cb.astype(F32) + back
    r.grad_cross[...] = grad
    gb = narrow(grad)

    def keep_columns(c):
        for j, value in enumerate((cb, gb)):
            to = slice(span + j * half, span + (j + 1) * half)
            r.right[0, :, to] = value[:, c * half : (c + 1) * half]
            r.give[:, to] = value[:, (1 - c) * half : (2 - c) * half]

    by_core(keep_columns)
    pair_copy(2).start()
    gmix = narrow(dot_nt(gb, wco[...]))
    for c in range(2):
        r.grads[c, me] = gmix[:, c * half : (c + 1) * half]
    spread_line(1, 0)
    spread_plane(1, [0])
    product = gmix.astype(F32).T * r.acc[...]
    for pair in range(pairs):
        at = columns(pair)
        r.gmasked[pair] = pair_mask(gmix[:, at])
        part = product[at]
        r.delta[pair : pair + 1] = jnp.concatenate(
            [jnp.sum(part[:HD], axis=0, keepdims=True), jnp.sum(part[HD:], axis=0, keepdims=True)], axis=1
        )
    lane = lax.broadcasted_iota(jnp.int32, (1, 2 * rows), 1)
    extent = jnp.zeros((1, 2 * rows), F32)
    for p in range(n):
        extent = jnp.where(lane == p, ins.lengths[p].astype(F32), extent)
    r.stats[me, :pairs] = r.lse[...]
    r.stats[me, pairs : 2 * pairs] = r.delta[...]
    r.stats[me, 2 * pairs : 2 * pairs + 1] = extent
    spread_line(2, 0)
    r.acc[...] = jnp.zeros(r.acc.shape, F32)

    def lanes(piece):
        return slice((piece % 2) * half, (piece % 2 + 1) * half)

    def split(piece, stage):
        done = halving_order(bits, piece)[:stage]
        bit = halving_order(bits, piece)[stage]
        inner = 1 << len([b for b in range(bit) if b not in done])
        outer = (n >> stage) // (2 * inner)

        def half_of(value):
            if stage:
                return stages[stage - 1].reshape(pieces, outer, 2, inner, share, half).at[piece, :, value]
            return mine.reshape(pieces // 2, outer, 2, inner, share, 2 * half).at[piece // 2, :, value, :, :, lanes(piece)]

        return half_of, (me >> bit) & 1, inner, outer, bit

    def stage_copy(piece, stage):
        half_of, value, inner, outer, bit = split(piece, stage)
        dst = stages[stage].at[piece].reshape(outer, inner, share, half)
        sems = r.sum_send.at[0], r.sum_recv.at[piece, stage]
        return remote(half_of(1 - value), dst, *sems, (me ^ (1 << bit), core))

    first_square = count_in + count_out
    square_places = (7, 4, 3, 0, 1, 2, 5, 6)

    def put(piece, c, total):
        if piece < count_in:
            r.out_fin[:, (c * count_in + piece) * half : (c * count_in + piece + 1) * half] = total
        elif piece < first_square:
            k = piece - count_in
            r.out_fout[k * share : (k + 1) * share, c * half : (c + 1) * half] = total
        else:
            r.out_squares[square_places[piece - first_square], :, c * half : (c + 1) * half] = total

    def last_copy(piece):
        recv = r.last_recv.at[int(piece >= first_square)]
        return remote(r.last_own.at[piece], r.last_other.at[piece], r.last_send.at[0], recv, partner)

    def begin(piece):
        stage_copy(piece, 0).start()

    def arrive(piece, stage):
        stage_copy(piece, stage).wait_recv()
        half_of, value, inner, outer, _ = split(piece, stage)
        kept = half_of(value)
        dst = stages[stage].at[piece]
        if stage + 1 < bits:

            def one(i, carry):
                dst[i] = narrow(kept[i // inner, i % inner].astype(F32) + dst[i].astype(F32))
                return carry

            lax.fori_loop(0, outer * inner, one, 0)
            stage_copy(piece, stage + 1).start()
        else:
            total = kept[0, 0].astype(F32) + dst[0].astype(F32)
            r.last_own[piece] = narrow(total)
            last_copy(piece).start()
            by_core(lambda c: put(piece, c, total))

    def owners(value):
        return narrow(value).reshape(n, share, half)

    def keep_piece(piece, value):
        mine[piece // 2, :, :, lanes(piece)] = value

    for i in range(3):
        pair_copy(i).wait_recv()
    left_self, left_feed, right = (x.reshape(2 * rows, x.shape[2]) for x in (r.left_self, r.left_feed, r.right))
    early = [piece for piece in range(first_square) if piece not in PLANES_FIRST]
    for piece in range(count_in):
        keep_piece(piece, owners(dot_tn(left_feed[:, units : units + width], right[:, piece * half : (piece + 1) * half])))
        if piece in early[:2]:
            begin(piece)
    per = width // (count_out * share)
    for part in range(count_out):
        value = narrow(dot_tn(left_feed[:, part * width : (part + 1) * width], right[:, span : span + half]))
        value = value.reshape(per, count_out, share, half)
        for k in range(count_out):
            piece = count_in + k
            mine[piece // 2, part * per : (part + 1) * per, :, lanes(piece)] = value[:, k]
    keep_piece(first_square + CO, owners(dot_tn(left_feed[:, units + width :], right[:, span + half :])))
    for piece in early[2:]:
        begin(piece)

    many = 4

    def question_block(turn, carry):
        at = pl.ds(pl.multiple_of(turn * many * slot, many * slot), many * slot)
        valid = jnp.concatenate([place < ins.lengths[turn * many + i] for i in range(many)], axis=0)
        for pair in range(pairs):
            cols = columns(pair)
            key = r.keys[at, cols]
            scores = jnp.where(valid, dot_nt(key, r.masked[pair]), NEG)
            chances = jnp.exp(scores - r.lse[pair : pair + 1])
            ds = narrow(chances * (dot_nt(r.values[at, cols], r.gmasked[pair]) - r.delta[pair : pair + 1]))
            r.acc[cols, :] = r.acc[cols, :] + pair_diag(dot_tn(key, ds), rows)
        return carry

    lax.fori_loop(0, n // (2 * many), question_block, 0)

    for number in range(1, line_bits):
        spread_line(1, number)
        spread_line(2, number)
        spread_plane(1, steps_of_line[number - 1])
    for piece in PLANES_FIRST:
        if piece < first_square:
            begin(piece)
    lax.fori_loop(n // (2 * many), n // many, question_block, 0)

    late = (CQ, SO, SQ, SK, SV)
    lefts = (width, 2 * width, 0, 0, 0)

    def late_copy(i):
        return remote(r.late_give.at[i], r.late.at[i, 1], r.pair_send.at[3], r.pair_recv.at[3 + i], partner)

    def late_give(name, value):
        i = late.index(name)

        def part(c):
            r.late[i, 0] = value[:, c * half : (c + 1) * half]
            r.late_give[i] = value[:, (1 - c) * half : (2 - c) * half]

        by_core(part)
        late_copy(i).start()

    def late_take(name, now=True):
        i = late.index(name)
        late_copy(i).wait_recv()
        left = left_self[:, lefts[i] : lefts[i] + width]
        keep_piece(first_square + name, owners(dot_tn(left, r.late.at[i].reshape(2 * rows, half)[...])))
        if now:
            begin(first_square + name)

    dcq = narrow(r.acc[...].T)
    late_give(CQ, dcq)
    back, dg2 = rms_back(r.after_self[...], g2, dot_nt(dcq, wcq[...]))
    grad = r.grad_cross[...] + back
    sb = narrow(grad)
    late_give(SO, sb)

    own_load.wait()

    def project(turn, carry):
        at = pl.ds(pl.multiple_of(turn * many * slot, many * slot), many * slot)
        source = r.enc[at]
        r.keys[at] = narrow(dot_nn(source, wck[...]))
        r.values[at] = narrow(dot_nn(source, wcv[...]))
        return carry

    lax.fori_loop(0, n // (2 * many), project, 0)
    spread_rest(1, [0])
    spread_line(1, line_bits)
    spread_plane(1, steps_of_line[-1])
    spread_line(2, line_bits)
    for d in range(1, 4):
        stat_plane(d).start()
    for ks in steps_of_line[:-1]:
        spread_rest(1, ks)
    lax.fori_loop(n // (2 * many), n // many, project, 0)
    late_take(CQ, False)

    gself = narrow(dot_nt(sb, wo[...]))
    dq_parts, dk_parts, dv_parts, sums = [], [], [], []
    for pair in range(pairs):
        at, masked, chances = self_chances(pair)
        gmasked = pair_mask(gself[:, at])
        dv_parts.append(narrow(dot_nn(narrow(chances), gmasked)))
        dp = dot_nt(r.v[:, at], gmasked)
        ds = chances * (dp - jnp.sum(chances * dp, axis=0, keepdims=True))
        sums.append(diagonal_sums(ds[:, :rows]))
        sums.append(diagonal_sums(ds[:, rows:]))
        dsb = narrow(ds)
        dk_parts.append(narrow(dot_nn(dsb, masked)))
        dq_parts.append(pair_diag(dot_tn(r.k[:, at], dsb), rows))
    dq = narrow(jnp.concatenate(dq_parts, axis=0).T)
    dk = jnp.concatenate(dk_parts, axis=1)
    dv = jnp.concatenate(dv_parts, axis=1)
    late_give(SQ, dq)
    late_give(SK, dk)
    late_give(SV, dv)
    late_take(SO, False)
    into = dot_nt(dq, wq[...]) + dot_nt(dk, wk[...]) + dot_nt(dv, wv[...])
    late_take(SQ, False)
    late_take(SK, False)
    late_take(SV, False)
    back, dg1 = rms_back(ins.hidden[...].astype(F32), g1, into)
    r.out_hidden[...] = grad + back
    give_out(1).start()
    onehot = bucket_onehot_rows(ins.table.shape[1], rows)
    dtable = lax.dot_general(
        jnp.concatenate(sums, axis=0), onehot, (((1,), (1,)), ((), ())), precision=lax.Precision.HIGHEST,
        preferred_element_type=F32,
    )

    heads, buckets = dtable.shape
    per_row = 128 // buckets
    table_rows = [
        jnp.concatenate([dtable[i + j : i + j + 1] for j in range(per_row)], axis=1) for i in range(0, heads, per_row)
    ]
    terms = jnp.concatenate([dg1, dg2, dg3], axis=0)
    for o in range(n):
        r.small_give[o, :3, :share] = terms[:, o * share : (o + 1) * share]
        r.small_give[o, 3 : 3 + len(table_rows)] = jnp.concatenate(table_rows, axis=0)
    r.small_take[me] = r.small_give[me]

    def small_copy(device):
        return remote(r.small_give.at[device], r.small_take.at[me], r.small_send.at[0], r.small_recv.at[0], (device, core))

    def small_one(d, carry):
        small_copy(me ^ d).start()
        return carry

    lax.fori_loop(1, n, small_one, 0)

    def small_pair():
        return remote(r.small_sum.at[0], r.small_sum.at[1], r.small_send.at[1], r.small_recv.at[1], partner)

    def small_add():
        all_come(r.small_take.at[: n - 1], r.small_recv.at[0])
        total = r.small_take[0]
        for o in range(1, n):
            total = total + r.small_take[o]
        r.small_sum[0] = total
        small_pair().start()

    def small_end():
        small_pair().wait_recv()
        total = r.small_sum[0] + r.small_sum[1]
        for i in range(3):
            outs.gains[i] = total[i : i + 1, :share]
        for i in range(len(table_rows)):
            for j in range(per_row):
                outs.table[i * per_row + j : i * per_row + j + 1] = total[3 + i : 4 + i, j * buckets : (j + 1) * buckets]

    place_f = place.astype(F32)

    def owner_block(turn, carry):
        q = (turn % line) * 4 + (low ^ (turn // line))
        at = passage_at(q)
        stats = r.stats[q]
        extent = jnp.sum(jnp.where(lane == me, stats[2 * pairs : 2 * pairs + 1], 0.0), axis=1, keepdims=True)
        valid = place_f < extent
        for pair in range(pairs):
            cols = columns(pair)
            c, within = pair // (pairs // 2), columns(pair % (pairs // 2))
            masked, gmasked = pair_mask(r.queries[c, q, :, within]), pair_mask(r.grads[c, q, :, within])
            scores = jnp.where(valid, dot_nt(r.keys[at, cols], masked), NEG)
            chances = jnp.exp(scores - stats[pair : pair + 1])
            ds = narrow(chances * (dot_nt(r.values[at, cols], gmasked) - stats[pairs + pair : pairs + pair + 1]))
            r.values[at, cols] = narrow(dot_nn(narrow(chances), gmasked))
            r.keys[at, cols] = narrow(dot_nn(ds, masked))
        return carry

    spread_rest(1, steps_of_line[-1])

    middle, last = range(first_square, first_square + CK), range(first_square + CK, pieces)

    def taken_up(event):
        piece, stage = event
        if piece in early:
            keys = (0.0, 1.1, 3.0, 4.3)
        elif piece in last:
            keys = (3.5, 3.8, 4.2, 4.9)
        elif piece not in middle:
            keys = (0.5 if piece < count_in else 1.0, 3.3, 3.9, 4.4)
        elif piece in PLANES_FIRST:
            keys = (3.25, 3.75, 4.1, 4.7)
        elif piece == first_square + SV:
            keys = (3.05, 3.85, 4.25, 4.75)
        elif piece == first_square + SK:
            keys = (3.05, 3.58, 4.02, 4.65)
        else:
            keys = (2.0, 3.1, 3.6, 4.6)
        return keys[min(stage, 2)] if stage + 1 < bits else keys[3]

    events = sorted(((piece, stage) for piece in range(pieces) for stage in range(bits)), key=taken_up)
    visits = [[event for event in events if min(int(taken_up(event)), 3) == visit] for visit in range(4)]
    for piece, stage in visits[0]:
        arrive(piece, stage)
    for piece in middle:
        begin(piece)

    lax.fori_loop(0, line, owner_block, 0)

    spread_taken(0)
    spread_taken(1)
    spread_taken(2)
    lax.fori_loop(line, 2 * line, owner_block, 0)
    for piece, stage in visits[1]:
        arrive(piece, stage)
    lax.fori_loop(2 * line, n, owner_block, 0)
    for piece, stage in visits[2]:
        arrive(piece, stage)

    def encoding_block(turn):
        at = slice(turn * many * slot, (turn + 1) * many * slot)
        value = narrow(dot_nt(r.keys[at], wck[...]) + dot_nt(r.values[at], wcv[...]))
        for c in range(2):
            to = slice(turn * many, (turn + 1) * many)
            r.grads[c, to] = value[:, c * half : (c + 1) * half].reshape(many, slot, half)

    def out_copy(c):
        return pltpu.make_async_copy(r.grads.at[c], outs.enc.at[:, :, c * half : (c + 1) * half], r.out.at[c])

    for kind in range(3):
        spread_sent(kind)

    def swap_copy(i):
        return remote(r.swap_give.at[i], r.swap_take.at[i], r.pair_send.at[4], r.pair_recv.at[8 + i], partner)

    def columns_of(ref, c):
        return owners(dot_tn(r.enc[...], ref[:, pl.ds(pl.multiple_of(c * half, 128), half)]))

    for i, ref in enumerate((r.keys, r.values)):
        r.swap_give[i] = columns_of(ref, 1 - core)
        swap_copy(i).start()
    for i, (name, ref) in enumerate(((CK, r.keys), (CV, r.values))):
        piece = first_square + name
        keep_piece(piece, columns_of(ref, core))
        swap_copy(i).wait_recv()

        def one(o, carry, i=i, to=mine.at[piece // 2, :, :, lanes(piece)]):
            to[o] = narrow(to[o].astype(F32) + r.swap_take[i, o].astype(F32))
            return carry

        lax.fori_loop(0, n, one, 0)
        begin(piece)

    def take_other(group, members):
        all_come(r.last_other.at[members.start : members.stop], r.last_recv.at[group])
        for piece in members:
            total = r.last_other[piece].astype(F32)
            by_core(lambda c: put(piece, 1 - c, total))

    rest = visits[3]
    for number, (piece, stage) in enumerate(rest):
        if (piece, stage) == (last[0], 0):
            for turn in range(n // many):
                encoding_block(turn)
            for c in range(2):
                out_copy(c).start()
        arrive(piece, stage)
        if (piece, stage) == (last[1], 0):
            small_add()
        if (piece, stage) == (last[0], bits - 1):
            take_other(0, range(first_square))
            give_out(3).start()
            give_out(4).start()
    small_end()

    take_other(1, range(first_square, pieces))
    give_out(2).start()

    for i in range(len(ready)):
        give_out(i).wait()
    for c in range(2):
        out_copy(c).wait()

    all_sent(r.enc.at[: (n - 1) * slot], r.in_send.at[0])
    for i in range(3):
        pair_copy(i).wait_send()
    all_sent(r.late_give, r.pair_send.at[3])
    all_sent(r.swap_give, r.pair_send.at[4])
    all_sent(mine.at[:, : n - 1], r.sum_send.at[0])
    all_sent(r.last_own, r.last_send.at[0])
    all_sent(r.small_give.at[: n - 1], r.small_send.at[0])
    all_sent(r.small_sum.at[0], r.small_send.at[1])


def layer(n, slot, args):
    rows, width = args.hidden.shape
    units = args.w_in.shape[1]
    share, half = width // n, width // 2
    bits = n.bit_length() - 1
    pairs = width // (2 * HD)
    keys = n * slot
    count_in = count_out = units // width
    pieces = 8 + count_in + count_out
    table = args.table.shape
    vmem, hbm = pl.BlockSpec(memory_space=pltpu.VMEM), pl.BlockSpec(memory_space=pl.ANY)
    in_specs = [pl.BlockSpec(memory_space=pltpu.SMEM)] + [hbm] * 11 + [vmem] * 6
    wide = jax.ShapeDtypeStruct((rows, width), F32)
    results = Outputs(
        result=wide, hidden=wide, enc=jax.ShapeDtypeStruct((n, slot, width), BF),
        squares=jax.ShapeDtypeStruct((8, share, width), F32), fin=jax.ShapeDtypeStruct((share, units), F32),
        fout=jax.ShapeDtypeStruct((count_out * share, width), F32), gains=jax.ShapeDtypeStruct((3, 1, share), F32),
        table=jax.ShapeDtypeStruct(table, F32),
    )
    dma = pltpu.SemaphoreType.DMA
    sixteen, full = pltpu.VMEM((rows, width), BF), pltpu.VMEM((rows, width), F32)
    stat, masks = pltpu.VMEM((pairs, 2 * rows), F32), pltpu.VMEM((pairs, 2 * rows, 2 * HD), BF)
    blocks, shared = pltpu.VMEM((keys, width), BF), pltpu.VMEM((2, n, rows, half), BF)
    swap = pltpu.VMEM((2, n, share, half), BF)
    last = pltpu.VMEM((pieces, share, half), BF)
    up = lambda count: -(-count // 8) * 8
    small_rows = up(3 + table[0] * table[1] // 128)
    scratch = Scratch(
        left_self=pltpu.VMEM((2, rows, 3 * width), BF),
        left_feed=pltpu.VMEM((2, rows, units + 2 * width), BF),
        right=pltpu.VMEM((2, rows, units // 2 + width), BF),
        give=pltpu.VMEM((rows, units // 2 + width), BF),
        late=pltpu.VMEM((5, 2, rows, half), BF),
        late_give=pltpu.VMEM((5, rows, half), BF),
        enc=blocks, keys=blocks, values=blocks, queries=shared, grads=shared,
        stats=pltpu.VMEM((n, up(2 * pairs + 1), 2 * rows), F32),
        weights=pltpu.VMEM((8, width, width), BF),
        masked=masks, gmasked=masks,
        acc=pltpu.VMEM((width, rows), F32),
        q=sixteen, k=sixteen, v=sixteen, after_self=full, grad_cross=full,
        top=stat, lse=stat, delta=stat, swap_give=swap, swap_take=swap,
        mine=pltpu.VMEM((pieces // 2, n, share, width), BF),
        last_own=last, last_other=last,
        out_result=full, out_hidden=full,
        out_squares=pltpu.VMEM((8, share, width), F32),
        out_fin=pltpu.VMEM((share, units), F32),
        out_fout=pltpu.VMEM((count_out * share, width), F32),
        small_give=pltpu.VMEM((n, small_rows, 128), F32), small_take=pltpu.VMEM((n, small_rows, 128), F32),
        small_sum=pltpu.VMEM((2, small_rows, 128), F32),
        load=dma((8 + 2 * (units // width),)),
        pair_send=dma((5,)), pair_recv=dma((10,)),
        sum_send=dma((1,)), sum_recv=dma((pieces, bits)),
        in_send=dma((1,)), in_recv=dma((n,)),
        all_send=dma((3,)), line_recv=dma((3, n // 4 - 1)), first_recv=dma((2, 2, n // 4)), plane_recv=dma((3,)),
        own=dma((1,)), out=dma((7,)),
        small_send=dma((2,)), small_recv=dma((2,)),
        last_send=dma((1,)), last_recv=dma((2,)),
    )
    stages = [pltpu.VMEM((pieces, n >> (b + 1), share, half), BF) for b in range(bits)]
    return pl.pallas_call(
        functools.partial(layer_kernel, n, slot, count_in, count_out),
        out_shape=tuple(results),
        in_specs=in_specs,
        out_specs=tuple([hbm] * 6 + [vmem] * 2),
        scratch_shapes=list(scratch) + stages,
        compiler_params=pltpu.CompilerParams(collective_id=1, has_side_effects=True, vmem_limit_bytes=LAYER_LIMIT),
    )(*args)


def finish_kernel(parts, *refs):
    count, total = len(parts), sum(parts)
    ins, outs, held, sems = refs[:count], refs[count : count + total], refs[count + total : -1], refs[-1]
    into = [pltpu.make_async_copy(ins[i], held[i], sems.at[i]) for i in range(count)]
    for copy in into:
        copy.start()
    back = []
    for i in range(count):
        into[i].wait()
        for part in range(parts[i]):
            number = len(back)
            src = held[i] if parts[i] == 1 else held[i].at[part]
            back.append(pltpu.make_async_copy(src, outs[number], sems.at[count + number]))
            back[-1].start()
    for copy in back:
        copy.wait()


def finish(arrays, parts):
    count, total = len(arrays), sum(parts)
    spec = pl.BlockSpec(memory_space=pl.ANY)
    shapes = []
    for array, part in zip(arrays, parts):
        shapes += [jax.ShapeDtypeStruct(array.shape[part > 1 :], array.dtype)] * part
    return pl.pallas_call(
        functools.partial(finish_kernel, parts),
        out_shape=tuple(shapes),
        in_specs=[spec] * count,
        out_specs=(spec,) * total,
        scratch_shapes=[pltpu.VMEM(a.shape, a.dtype) for a in arrays] + [pltpu.SemaphoreType.DMA((count + total,))],
        compiler_params=pltpu.CompilerParams(vmem_limit_bytes=VMEM_LIMIT),
    )(*arrays)


def whole(shape=None):
    return pl.BlockSpec(memory_space=pltpu.VMEM)


def call(kernel, outs, *args):
    return pl.pallas_call(
        kernel,
        out_shape=tuple(jax.ShapeDtypeStruct(shape, kind) for shape, kind in outs),
        in_specs=[whole()] * len(args),
        out_specs=tuple(whole() for _ in outs),
        compiler_params=pltpu.CompilerParams(vmem_limit_bytes=VMEM_LIMIT),
    )(*args)


def per_device(
    n, hidden, encodings, lengths, cotangent, wq, wk, wv, wo, wcq, wck, wcv, wco, w_in, w_out,
    gain_self, gain_cross, gain_feed, table,
):
    rows, width = hidden.shape[2], hidden.shape[3]
    slot = encodings.shape[3]
    passages = lengths.shape[2]
    units = w_in.shape[1]
    pairs = width // (2 * HD)
    keys = passages * slot
    own = hidden.reshape(rows, width)
    cot = cotangent.reshape(rows, width)
    g1, g2, g3 = (gain.reshape(1, width) for gain in (gain_self, gain_cross, gain_feed))
    length_row = lengths.reshape(passages)
    share = width // n
    fits = passages == n and keys * width * 8 <= 16 << 20 and units == 4 * width
    tables = 128 % table.shape[0] == 0 and table.size % 128 == 0
    if n & (n - 1) == 0 and n >= 8 and share % 16 == 0 and share <= 128 and fits and tables:
        out = layer(n, slot, Inputs(
            length_row, encodings.reshape(n, slot, width), wq, wk, wv, wo, wcq, wck, wcv, wco, w_in, w_out, own, cot,
            gain_self, gain_cross, gain_feed, table.T,
        ))
        result, hidden_grad, enc_grad, *sums, table_sum = finish(out, (1, 1, 1, 8, 1, 1, 3, 1))
        return (
            (result.reshape(hidden.shape), hidden_grad.reshape(hidden.shape), enc_grad.reshape(encodings.shape))
            + tuple(sums[:10])
            + tuple(gain.reshape(share) for gain in sums[10:])
            + (table_sum.T,)
        )

    source = lax.all_to_all(encodings, PASS, split_axis=2, concat_axis=0, tiled=True).reshape(keys, width)

    sixteen, wide = ((rows, width), BF), ((rows, width), F32)
    h1, q, k, v, mix1, after_self, h2, cq = call(
        self_forward_kernel,
        [sixteen] * 5 + [wide, sixteen, sixteen],
        own, wq, wk, wv, wo, wcq, g1, g2, table,
    )

    block = 4 * slot
    steps = keys // block
    stats = jax.ShapeDtypeStruct((pairs, 2 * rows), F32)
    smem = pl.BlockSpec(memory_space=pltpu.SMEM)
    tile = pl.BlockSpec((block, width), lambda i: (i, 0))
    square = pl.BlockSpec((width, width), lambda i: (0, 0))
    query = pl.BlockSpec((rows, width), lambda i: (0, 0))
    stat = pl.BlockSpec((pairs, 2 * rows), lambda i: (0, 0))
    ck, cv, mix_t, lse = pl.pallas_call(
        functools.partial(cross_forward_kernel, slot),
        grid=(steps,),
        out_shape=(
            jax.ShapeDtypeStruct((keys, width), BF),
            jax.ShapeDtypeStruct((keys, width), BF),
            jax.ShapeDtypeStruct((width, rows), F32),
            stats,
        ),
        in_specs=[smem, tile, square, square, query],
        out_specs=(tile, tile, pl.BlockSpec((width, rows), lambda i: (0, 0)), stat),
        scratch_shapes=[
            pltpu.VMEM((pairs, 2 * rows, 2 * HD), BF),
            pltpu.VMEM((pairs, 2 * rows), F32),
            pltpu.VMEM((pairs, 2 * rows), F32),
            pltpu.VMEM((width, rows), F32),
        ],
        compiler_params=pltpu.CompilerParams(vmem_limit_bytes=VMEM_LIMIT),
    )(length_row, source, wck, wcv, cq)

    pieces = units // width
    result, grad_cross, gmix, delta, dg3, d_in, d_out, d_co = call(
        feed_kernel,
        [wide, wide, sixteen, ((pairs, 2 * rows), F32), ((1, width), F32), ((pieces, width, width), BF),
         ((units, width), BF), ((width, width), BF)],
        mix_t, after_self, cot, wco, w_in, w_out, g3,
    )

    enc_grad, dcq, d_ck, d_cv = pl.pallas_call(
        functools.partial(cross_backward_kernel, slot),
        grid=(steps,),
        out_shape=(
            jax.ShapeDtypeStruct((keys, width), BF),
            jax.ShapeDtypeStruct((rows, width), BF),
            jax.ShapeDtypeStruct((width, width), BF),
            jax.ShapeDtypeStruct((width, width), BF),
        ),
        in_specs=[smem, tile, tile, tile, square, square, query, query, stat, stat],
        out_specs=(tile, query, square, square),
        scratch_shapes=[
            pltpu.VMEM((pairs, 2 * rows, 2 * HD), BF),
            pltpu.VMEM((pairs, 2 * rows, 2 * HD), BF),
            pltpu.VMEM((width, rows), F32),
            pltpu.VMEM((block, 2 * width), BF),
            pltpu.VMEM((width, 2 * width), F32),
        ],
        compiler_params=pltpu.CompilerParams(vmem_limit_bytes=VMEM_LIMIT),
    )(length_row, source, ck, cv, wck, wcv, cq, gmix, lse, delta)
    returned = lax.all_to_all(
        enc_grad.reshape(passages, 1, 1, slot, width), PASS, split_axis=0, concat_axis=2, tiled=True
    )

    gain_kind = ((1, width), F32)
    squared = ((width, width), BF)
    hidden_grad, d_cq, d_so, d_q, d_k, d_v, dg1, dg2, dtable = call(
        self_backward_kernel,
        [wide] + [squared] * 5 + [gain_kind, gain_kind, (table.shape, F32)],
        own, h1, q, k, v, mix1, after_self, h2, dcq, grad_cross, wq, wk, wv, wo, wcq, g1, g2, table,
    )

    both = [d_q, d_k, d_v, d_so, d_cq, d_ck, d_cv, d_co, d_in.transpose(1, 0, 2).reshape(width, units), d_out]

    def total(part):
        shared = lax.psum_scatter(part, PASS, scatter_dimension=0, tiled=True)
        return lax.psum(shared.astype(BF), CORE).astype(F32)

    sums = [total(part.astype(F32)) for part in both]
    totals, in_total, out_total = sums[:8], sums[8], sums[9]
    gains = [total(part.reshape(width)) for part in (dg1, dg2, dg3)]
    table_sum = lax.psum(dtable, (PASS, CORE))
    return (
        (result.reshape(hidden.shape), hidden_grad.reshape(hidden.shape), returned)
        + tuple(totals)
        + (in_total, out_total)
        + tuple(gains)
        + (table_sum,)
    )


def solution(mesh):
    rows = P(CORE, PASS, None, None)
    passage = P(PASS, CORE, None, None, None)
    in_specs = (rows, passage, P(CORE, PASS, None), rows) + (P(),) * 14
    out_specs = (rows, rows, passage) + (P(PASS, None),) * 10 + (P(PASS),) * 3 + (P(),)
    return jax.shard_map(
        functools.partial(per_device, mesh.shape[PASS]),
        mesh=mesh,
        in_specs=in_specs,
        out_specs=out_specs,
        check_vma=False,
    )
```
